32 devices in a mesh: patch: 8 (over z, x), sect: 4 (over y, core).
Axes of the slice: x: 2, y: 2, z: 4, core: 2. Of those that a mesh axis runs over, the one named last changes fastest.
Arguments:
- displacement: float32 [16, 3, 128, 4096], P('patch', None, 'sect'), may hold values from -6 to 6
- lame_params: float32 [16, 2], replicated, may hold values from 0.5 to 2
- patch_sizes: int32 [16, 2], P('patch'), may hold values from 34 to 61, as said below
- partners: int32 [16, 4], P('patch'), may hold values from 0 to 63, as said below
- transfer: float32 [16, 4, 64, 64], P('patch'), may hold values from -0.75 to 0.75
Outputs:
- first_apply: float32 [16, 3, 128, 4096], P('patch', None, 'sect')
- second_apply: float32 [16, 3, 128, 4096], P('patch', None, 'sect')
The draws below stay inside these ranges and needn't reach their ends.
Inputs may be any that keep to these rules, and one draw needn't show every extreme that they name: patch_sizes[p, 0] and patch_sizes[p, 1] count the active control points of patch p along x and y. The relation of faces is symmetric: if partners[p, f] = 4 q + g then partners[q, g] = 4 p + f. The patches 2 i to 2 i + 1 form group i; the faces of group i meet faces of groups i - 1 and i + 1 (modulo the number of groups) only, 4 faces with each.
All inputs are finite; a program needn't handle non-finite values.
Results may differ from the reference program's by a relative error of at most 0.000054.
Values sent between devices are 32-bit elements; how exact they have to be, the bound alone decides.
No kernel may reach another device: no remote copies, remote signals or barrier semaphores. Data moves between devices by JAX's collectives and lax.ppermute only.
A program may use at most 64 MiB of HBM per device.

```python
import math
import jax
import jax.numpy as jnp
from jax import lax

PAD = 64
PATCH_DEV = 2
PATCHES = 16
NZ = 128
MAXN = 61
MINN = 34


def draw_patch_sizes(key, part):
    key_size, key_place = jax.random.split(key)
    drawn_sizes = jax.random.randint(key_size, (PATCHES * 2,), MINN, MAXN + 1).astype(jnp.int32)
    place_max = jax.random.randint(key_place, (), 0, PATCHES * 2).astype(jnp.int32)
    drawn_sizes = drawn_sizes.at[place_max].set(MAXN)
    drawn_sizes = drawn_sizes.at[(place_max + PATCHES) % (PATCHES * 2)].set(MINN)
    return drawn_sizes.reshape(PATCHES, 2).astype(jnp.int32)


def draw_partners(key, part):
    groups = PATCHES // PATCH_DEV
    face_total = 4 * PATCH_DEV
    key_score = jax.random.fold_in(key, 1)
    group_ids = jnp.arange(groups, dtype=jnp.int32)
    after_group = (group_ids + 1) % groups
    before_group = (group_ids + groups - 1) % groups
    scores = jax.random.randint(key_score, (groups, face_total), 0, 1 << 20).astype(jnp.int32) * face_total + jnp.arange(face_total, dtype=jnp.int32)[None, :]
    ranked = jnp.argsort(scores, axis=1).astype(jnp.int32)
    half_faces = face_total // 2
    leading = ranked[:, :half_faces]
    trailing = ranked[:, half_faces:]
    code_leading = after_group[:, None] * face_total + trailing[after_group]
    code_trailing = before_group[:, None] * face_total + leading[before_group]
    row_index = group_ids[:, None]
    table = jnp.zeros((groups, face_total), jnp.int32)
    table = table.at[row_index, leading].set(code_leading)
    table = table.at[row_index, trailing].set(code_trailing)
    return table.reshape(PATCHES, 4)


def block_levels(rng, extent, cuts, smallest, largest):
    factor_of = 1.0
    for dim, blocks in cuts:
        steps = jax.random.uniform(jax.random.fold_in(jax.random.fold_in(rng, 6), dim), (blocks,), jnp.float32, smallest / len(cuts), largest / len(cuts))
        factor_of = factor_of * jnp.repeat(jnp.exp(steps), extent[dim] // blocks).reshape((-1,) + (1,) * (len(extent) - 1 - dim))
    return factor_of


def bell_draw(own_key, dims, deviation, most, pieces=(), kind=jnp.bfloat16):
    drawn = deviation * jax.random.normal(own_key, dims, jnp.float32)
    if pieces:
        drawn = drawn * block_levels(own_key, dims, pieces, -0.22, 0.18)
    return jnp.clip(drawn, -most, most).astype(kind)


def setup_inputs(seed: int = 0) -> dict:
    keys = jax.random.split(jax.random.key(seed), 6)
    displacement = bell_draw(keys[0], (PATCHES, 3, NZ, PAD * PAD), 1.0, 6.0, ((0, 8), (2, 4)), jnp.float32)
    lame_params = jnp.clip(jnp.exp(jax.random.uniform(keys[1], (PATCHES, 2), jnp.float32, math.log(0.5), math.log(2.0))), 0.5, 2.0)
    patch_sizes = draw_patch_sizes(jax.random.fold_in(keys[5], 71), 0)
    partners = draw_partners(jax.random.fold_in(keys[5], 71), 0)
    transfer = bell_draw(keys[4], (PATCHES, 4, PAD, PAD), PAD ** -0.5, 0.75, ((0, 8),), jnp.float32)
    return dict(displacement=displacement, lame_params=lame_params, patch_sizes=patch_sizes, partners=partners, transfer=transfer)


MASS_BAND = (2416.0 / 5040.0, 1191.0 / 5040.0, 120.0 / 5040.0, 1.0 / 5040.0)
STIFF_BAND = (80.0 / 120.0, -15.0 / 120.0, -24.0 / 120.0, -1.0 / 120.0)
SLOPE_BAND = (245.0 / 720.0, 56.0 / 720.0, 1.0 / 720.0)
PENALTY = 3.0
HIGHEST_PREC = lax.Precision.HIGHEST


def shifted(values, offset, which_axis):
    length = values.shape[which_axis]
    pad_width = [(0, 0)] * values.ndim
    pad_width[which_axis] = (3, 3)
    padded = jnp.pad(values, pad_width)
    return lax.slice_in_dim(padded, 3 + offset, 3 + offset + length, axis=which_axis)


def apply_band(values, band_kind, which_axis):
    if band_kind == "slope":
        summed = SLOPE_BAND[0] * (shifted(values, 1, which_axis) - shifted(values, -1, which_axis))
        for d in (2, 3):
            summed = summed + SLOPE_BAND[d - 1] * (shifted(values, d, which_axis) - shifted(values, -d, which_axis))
        return summed
    factors = MASS_BAND if band_kind == "mass" else STIFF_BAND
    summed = factors[0] * values
    for d in (1, 2, 3):
        summed = summed + factors[d] * (shifted(values, d, which_axis) + shifted(values, -d, which_axis))
    return summed


def inplane(block_grid, kind_x, kind_y):
    return apply_band(apply_band(block_grid, kind_y, 2), kind_x, 1)


def volume(block_grid, shear_mod, grad_div):
    mass_z = [apply_band(block_grid[j], "mass", 0) for j in range(3)]
    stiff_z = [apply_band(block_grid[j], "stiff", 0) for j in range(3)]
    slope_z = [apply_band(block_grid[j], "slope", 0) for j in range(3)]
    comp_x = (shear_mod + grad_div) * inplane(mass_z[0], "stiff", "mass") + shear_mod * inplane(mass_z[0], "mass", "stiff") + shear_mod * inplane(stiff_z[0], "mass", "mass") - grad_div * (inplane(mass_z[1], "slope", "slope") + inplane(slope_z[2], "slope", "mass"))
    comp_y = shear_mod * inplane(mass_z[1], "stiff", "mass") + (shear_mod + grad_div) * inplane(mass_z[1], "mass", "stiff") + shear_mod * inplane(stiff_z[1], "mass", "mass") - grad_div * (inplane(mass_z[0], "slope", "slope") + inplane(slope_z[2], "mass", "slope"))
    comp_z = shear_mod * (inplane(mass_z[2], "stiff", "mass") + inplane(mass_z[2], "mass", "stiff")) + (shear_mod + grad_div) * inplane(stiff_z[2], "mass", "mass") - grad_div * (inplane(slope_z[0], "slope", "mass") + inplane(slope_z[1], "mass", "slope"))
    return jnp.stack([comp_x, comp_y, comp_z])


def trace_pair(outer_layer, inner_layer):
    return jnp.stack([outer_layer, 3.0 * (inner_layer - outer_layer)])


def face_traces(block_grid, size_x, size_y):
    x_low = trace_pair(block_grid[:, :, 0, :], block_grid[:, :, 1, :])
    x_high = trace_pair(lax.dynamic_index_in_dim(block_grid, size_x - 1, 2, keepdims=False), lax.dynamic_index_in_dim(block_grid, size_x - 2, 2, keepdims=False))
    y_low = trace_pair(block_grid[:, :, :, 0], block_grid[:, :, :, 1])
    y_high = trace_pair(lax.dynamic_index_in_dim(block_grid, size_y - 1, 3, keepdims=False), lax.dynamic_index_in_dim(block_grid, size_y - 2, 3, keepdims=False))
    stacked = jnp.stack([x_low, x_high, y_low, y_high])
    return stacked.reshape(4, 2, 3, -1)


def face_terms(own_tr, partner_tr, transfer_p, mu_own, mu_far):
    depth_cells = own_tr.shape[-1] // PAD
    own_grid = own_tr.reshape(4, 2, 3, depth_cells, PAD)
    far_grid = partner_tr.reshape(4, 2, 3, depth_cells, PAD)
    projected = jnp.einsum("fij,fbczj->fbczi", transfer_p, far_grid, precision=HIGHEST_PREC)
    mu_face = (0.5 * (mu_own + mu_far))[:, None, None, None]
    jump_term = own_grid[:, 0] - projected[:, 0]
    flux_term = 0.5 * mu_face * (projected[:, 1] - own_grid[:, 1])
    outer_term = (PENALTY - 1.5) * mu_face * jump_term - flux_term
    inner_term = 1.5 * mu_face * jump_term
    return outer_term, inner_term


def add_at(target_grid, addend, layer_idx, which_axis):
    current = lax.dynamic_index_in_dim(target_grid, layer_idx, which_axis, keepdims=False)
    return lax.dynamic_update_index_in_dim(target_grid, current + addend, layer_idx, which_axis)


def add_faces(target_grid, outer_term, inner_term, size_x, size_y):
    target_grid = add_at(target_grid, outer_term[0], 0, 2)
    target_grid = add_at(target_grid, inner_term[0], 1, 2)
    target_grid = add_at(target_grid, outer_term[1], size_x - 1, 2)
    target_grid = add_at(target_grid, inner_term[1], size_x - 2, 2)
    target_grid = add_at(target_grid, outer_term[2], 0, 3)
    target_grid = add_at(target_grid, inner_term[2], 1, 3)
    target_grid = add_at(target_grid, outer_term[3], size_y - 1, 3)
    target_grid = add_at(target_grid, inner_term[3], size_y - 2, 3)
    return target_grid


def apply_all(values, lame_params, patch_sizes, partners, transfer):
    patch_count = values.shape[0]
    places = jnp.arange(PAD, dtype=jnp.int32)
    active = ((places[None, :, None] < patch_sizes[:, 0, None, None]) & (places[None, None, :] < patch_sizes[:, 1, None, None])).astype(jnp.float32).reshape(patch_count, 1, 1, PAD * PAD)
    masked = values * active
    blocks = masked.reshape(patch_count, 3, NZ, PAD, PAD)
    traces = jax.vmap(face_traces)(blocks, patch_sizes[:, 0], patch_sizes[:, 1])
    flat_traces = traces.reshape(patch_count * 4, 2, 3, -1)
    partner_all = flat_traces[partners.reshape(-1)].reshape(patch_count, 4, 2, 3, -1)
    mu_other = lame_params[partners // 4, 0]

    def one_patch(patch_items):
        block_grid, own_tr, partner_tr, transfer_p, lame_row, mu_far, sizes_row, active_row = patch_items
        result = volume(block_grid, lame_row[0], lame_row[0] + lame_row[1])
        outer_term, inner_term = face_terms(own_tr, partner_tr, transfer_p, lame_row[0], mu_far)
        result = add_faces(result, outer_term, inner_term, sizes_row[0], sizes_row[1])
        return result.reshape(3, NZ, PAD * PAD) * active_row

    return lax.map(one_patch, (blocks, traces, partner_all, transfer, lame_params, mu_other, patch_sizes, active))


def reference(displacement, lame_params, patch_sizes, partners, transfer):
    first_apply = apply_all(displacement, lame_params, patch_sizes, partners, transfer)
    second_apply = apply_all(first_apply, lame_params, patch_sizes, partners, transfer)
    return first_apply, second_apply
```

```python
import functools

import jax
import jax.numpy as jnp
import ml_dtypes
import numpy as np
from jax import lax
from jax.experimental import pallas as pl
from jax.experimental.pallas import tpu as pltpu
from jax.sharding import PartitionSpec as P

PAD = 64
LANES = 128
HALO = 3
COMPS = 3
FACES = 4
MASS_INT = (2416.0, 1191.0, 120.0, 1.0)
STIFF_INT = (80.0, -15.0, -24.0, -1.0)
SLOPE_INT = (245.0, 56.0, 1.0)
MASS_DEN = 5040.0
STIFF_DEN = 120.0
SLOPE_DEN = 720.0
PENALTY = 3.0
XBLOCK = 16
XROWS = 8
VMEM_BYTES = 56 * 1024 * 1024
F32 = jnp.float32
BF16 = jnp.bfloat16


def split_np(table):
    high = table.astype(ml_dtypes.bfloat16)
    low = (table - high.astype(np.float64)).astype(ml_dtypes.bfloat16)
    return high, low


def band_np(size, kind):
    table = np.zeros((size, size))
    for i in range(size):
        for d in range(0, 4):
            for sign in (1, -1):
                j = i + sign * d
                if 0 <= j < size:
                    if kind == "slope":
                        if d:
                            table[i, j] = sign * SLOPE_INT[d - 1] / SLOPE_DEN
                    elif kind == "mass":
                        table[i, j] = MASS_INT[d] / MASS_DEN
                    else:
                        table[i, j] = STIFF_INT[d] / STIFF_DEN
    return table


def depth_table(depth):
    table = np.concatenate([band_np(depth, k) for k in ("mass", "stiff", "slope")], axis=0)
    high, low = split_np(table)
    return np.concatenate([high, high, low], axis=1)


def plane_tables():
    out = []
    for kind in ("mass", "stiff", "slope"):
        one = band_np(PAD, kind).T
        both = np.zeros((LANES, LANES))
        both[:PAD, :PAD] = one
        both[PAD:, PAD:] = one
        out.append(both)
    return np.stack(out).astype(np.float32)


def order_table():
    table = np.zeros((512, 512))
    for g in range(4):
        for x16 in range(16):
            for p in range(2):
                for layer in range(4):
                    row = g * 128 + x16 * 8 + p * 4 + layer
                    col = ((p * 2 + layer // 2) * 2 + layer % 2) * 64 + 16 * g + x16
                    table[row, col] = 1.0
    return table


def split(values):
    high = values.astype(BF16)
    low = (values - high.astype(F32)).astype(BF16)
    return high, low


def lane_iota(shape=(1, LANES)):
    return lax.broadcasted_iota(jnp.int32, shape, len(shape) - 1)


def swap_halves(values):
    return pltpu.roll(values, PAD, axis=values.ndim - 1)


def merge(low_half, high_half):
    return jnp.where(lane_iota() < PAD, low_half, high_half)


def dot(a, b):
    return jnp.dot(a, b, preferred_element_type=F32)


def face_sides(partners_ref, me, groups):
    before = lax.rem(me + groups - 1, groups)
    codes = [partners_ref[k // FACES, k % FACES] for k in range(2 * FACES)]
    sides = [jnp.where(code // (2 * FACES) == before, 0, 1) for code in codes]
    return codes, sides


def send_sources(partners_ref, me, groups):
    codes, sides = face_sides(partners_ref, me, groups)
    sources = [[jnp.int32(0)] * FACES for _ in range(2)]
    for k in range(2 * FACES):
        rank = jnp.int32(0)
        for other in range(2 * FACES):
            if other != k:
                below = (sides[other] == sides[k]) & (codes[other] < codes[k])
                rank = rank + jnp.where(below, 1, 0)
        for side in range(2):
            for slot in range(FACES):
                hit = (sides[k] == side) & (rank == slot)
                sources[side][slot] = jnp.where(hit, k, sources[side][slot])
    return sources


def receive_slots(partners_ref, me, groups):
    _, sides = face_sides(partners_ref, me, groups)
    slots = []
    for k in range(2 * FACES):
        rank = jnp.int32(0)
        for other in range(k):
            rank = rank + jnp.where(sides[other] == sides[k], 1, 0)
        slots.append(rank)
    return sides, slots


def layer_select(sizes_ref):
    rows = lax.broadcasted_iota(jnp.int32, (LANES, LANES), 0)
    cols = lax.broadcasted_iota(jnp.int32, (LANES, LANES), 1)
    patch = (cols // 4) % 2
    layer = cols % 4
    size_y = jnp.where(patch == 0, sizes_ref[0, 1], sizes_ref[1, 1])
    at = jnp.where(layer < 2, layer, size_y + 1 - layer)
    base = jnp.where(rows == patch * PAD + at, 1.0, 0.0)
    return [jnp.where(cols // 8 == j, base, 0.0).astype(BF16) for j in range(16)]


def row_at(ref, x, depth):
    parts = []
    for c in range(COMPS):
        start = c * PAD * depth + x * depth
        if not isinstance(x, int):
            start = pl.multiple_of(start, depth)
        parts.append(ref[pl.ds(start, depth), :])
    return jnp.concatenate(parts, axis=0)


def send_layers(field, sizes_ref, partners_ref, order, own, to_before, to_after, low, high, me, groups, depth):
    for c in range(COMPS):
        for d in range(HALO):
            low[c, d] = field[pl.ds(c * PAD * depth + d, PAD, stride=depth), :]
            high[c, d] = field[pl.ds(c * PAD * depth + depth - HALO + d, PAD, stride=depth), :]
    outer, inner = row_at(field, 0, depth), row_at(field, 1, depth)
    own[0] = merge(outer, swap_halves(inner))
    own[FACES] = merge(swap_halves(outer), inner)
    outer, inner = [row_at(field, sizes_ref[0, 0] - 1 - i, depth) for i in range(2)]
    own[1] = merge(outer, swap_halves(inner))
    outer, inner = [row_at(field, sizes_ref[1, 0] - 1 - i, depth) for i in range(2)]
    own[FACES + 1] = merge(swap_halves(outer), inner)
    select = jnp.concatenate(layer_select(sizes_ref), axis=0)
    groups_rows = []
    for g in range(4):
        for c in range(COMPS):
            base = c * PAD * depth + 16 * g * depth
            wide = [field[base + j * depth : base + (j + 1) * depth, :] for j in range(16)]
            groups_rows.append(jnp.concatenate(wide, axis=1))
    rows = jnp.concatenate(groups_rows, axis=0)
    count = rows.shape[0]
    row_high, row_low = split(rows)
    picked = dot(jnp.concatenate([row_high, row_low], axis=0), select)
    picked = picked[:count] + picked[count:]
    per = COMPS * depth
    picked = jnp.concatenate([picked[g * per : (g + 1) * per] for g in range(4)], axis=1)
    pick_high, pick_low = split(picked)
    sorted_layers = dot(jnp.concatenate([pick_high, pick_low], axis=0), order[...])
    sorted_layers = sorted_layers[:per] + sorted_layers[per:]
    for p in range(2):
        for f in range(2):
            at = (p * 2 + f) * LANES
            own[p * FACES + 2 + f] = sorted_layers[:, at : at + LANES]
    sources = send_sources(partners_ref, me, groups)
    for slot in range(FACES):
        to_before[slot] = own[sources[0][slot]]
        to_after[slot] = own[sources[1][slot]]


def active_lanes(sizes_ref):
    lane = lane_iota()
    size_x = jnp.where(lane < PAD, sizes_ref[0, 0], sizes_ref[1, 0])
    size_y = jnp.where(lane < PAD, sizes_ref[0, 1], sizes_ref[1, 1])
    return size_x, (lane % PAD) < size_y


def start_kernel(groups, depth, me_ref, sizes_ref, partners_ref, disp, order, field, own, to_before, to_after, low, high):
    me = me_ref[0]
    size_x, in_y = active_lanes(sizes_ref)
    for k in range(PAD // 2):
        keep_even = in_y & (2 * k < size_x)
        keep_odd = in_y & (2 * k + 1 < size_x)
        for c in range(COMPS):
            one = disp[0, c, :, k * LANES : (k + 1) * LANES]
            two = disp[1, c, :, k * LANES : (k + 1) * LANES]
            even = merge(one, swap_halves(two))
            odd = merge(swap_halves(one), two)
            base = (c * PAD + 2 * k) * depth
            field[base : base + depth, :] = jnp.where(keep_even, even, 0.0)
            field[base + depth : base + 2 * depth, :] = jnp.where(keep_odd, odd, 0.0)
    send_layers(field, sizes_ref, partners_ref, order, own, to_before, to_after, low, high, me, groups, depth)


MASS, STIFF, SLOPE = 0, 1, 2
TILES = (
    (((0, MASS), (0, STIFF)), ((0, STIFF), (0, MASS))),
    (((1, MASS), (1, STIFF)), ((1, STIFF), (1, MASS))),
    (((2, MASS), (2, STIFF)), ((2, STIFF), (2, MASS))),
    (((1, MASS), (2, SLOPE)), ((0, SLOPE), (1, MASS))),
    (((0, SLOPE), (1, SLOPE)), ((2, SLOPE), (2, MASS))),
    (((0, MASS), None), ((1, SLOPE), None)),
)
TERMS = {
    ((0, MASS), (0, STIFF)): (MASS, "both"),
    ((0, MASS), (0, MASS)): (STIFF, "mu"),
    ((0, STIFF), (0, MASS)): (MASS, "mu"),
    ((1, MASS), (0, SLOPE)): (SLOPE, "grad"),
    ((2, SLOPE), (0, SLOPE)): (MASS, "grad"),
    ((1, MASS), (1, STIFF)): (MASS, "mu"),
    ((1, MASS), (1, MASS)): (STIFF, "both"),
    ((1, STIFF), (1, MASS)): (MASS, "mu"),
    ((2, SLOPE), (1, MASS)): (SLOPE, "grad"),
    ((0, MASS), (1, SLOPE)): (SLOPE, "grad"),
    ((2, MASS), (2, STIFF)): (MASS, "mu"),
    ((2, MASS), (2, MASS)): (STIFF, "mu"),
    ((2, STIFF), (2, MASS)): (MASS, "both"),
    ((1, SLOPE), (2, MASS)): (SLOPE, "grad"),
    ((0, SLOPE), (2, SLOPE)): (MASS, "grad"),
}
OUT_SCALE = {STIFF: 1.0 / STIFF_DEN, MASS: 1.0 / MASS_DEN, SLOPE: 1.0 / SLOPE_DEN}


def weights_kernel(lame_ref, me_ref, tables, weights):
    first = me_ref[0] * 2
    lane = lane_iota()

    def per_lane(one, two):
        return jnp.where(lane < PAD, one, two)

    mu = per_lane(lame_ref[first, 0], lame_ref[first + 1, 0])
    grad = mu + per_lane(lame_ref[first, 1], lame_ref[first + 1, 1])
    factors = {"mu": mu, "both": mu + grad, "grad": -grad}
    placed = set()
    for t, (sources, targets) in enumerate(TILES):
        for i, source in enumerate(sources):
            for o, target in enumerate(targets):
                term = TERMS.get((source, target))
                if term is None or (source, target) in placed:
                    block = jnp.zeros((LANES, LANES), F32)
                else:
                    placed.add((source, target))
                    block = tables[term[0]] * (factors[term[1]] * OUT_SCALE[target[1]])
                block_high, block_low = split(block)
                cols = slice(o * LANES, (o + 1) * LANES)
                for part, piece in enumerate((block_high, block_high, block_low)):
                    at = part * 2 * LANES + i * LANES
                    weights[t, at : at + LANES, cols] = piece


def plane_sums(fields, weights):
    sums = {}
    for t, (sources, targets) in enumerate(TILES):
        if sources[1] is None:
            high, low = fields[sources[0]]
            weight = jnp.concatenate(
                [weights[t, part * 2 * LANES : part * 2 * LANES + LANES, :LANES] for part in range(3)], axis=0
            )
        else:
            high, low = [jnp.concatenate([fields[s][part] for s in sources], axis=1) for part in range(2)]
            weight = weights[t]
        out = dot(jnp.concatenate([high, low, high], axis=1), weight)
        for o, target in enumerate(targets):
            if target is not None:
                piece = out[:, o * LANES : (o + 1) * LANES]
                sums[target] = piece if target not in sums else sums[target] + piece
    return sums


def band_x(stiff, mass, slope):
    total = STIFF_INT[0] * stiff(0) + MASS_INT[0] * mass(0)
    for d in (1, 2):
        total = total + STIFF_INT[d] * (stiff(d) + stiff(-d))
        total = total + MASS_INT[d] * (mass(d) + mass(-d))
        total = total + SLOPE_INT[d - 1] * (slope(d) - slope(-d))
    return total + ((mass(3) + mass(-3)) - (stiff(3) + stiff(-3))) + (slope(3) - slope(-3))


def volume_kernel(depth, field, z_table, weights, out, sums_ref):
    for i in range(9):
        for x in (0, 1, 2, PAD + 3, PAD + 4, PAD + 5):
            sums_ref[i, x] = jnp.zeros((depth, LANES), F32)

    def in_plane(block, carry):
        x0 = block * XBLOCK
        fields = {}
        for c in range(COMPS):
            start = pl.multiple_of((c * PAD + x0) * depth, XBLOCK * depth)
            rows = field[pl.ds(start, XBLOCK * depth), :]
            wide = jnp.concatenate([rows[j * depth : (j + 1) * depth] for j in range(XBLOCK)], axis=1)
            high, low = split(wide)
            banded = dot(z_table[...], jnp.concatenate([high, low, high], axis=0))
            parts = split(banded)
            for kind in range(3):
                fields[(c, kind)] = tuple(
                    jnp.concatenate(
                        [
                            part[kind * depth : (kind + 1) * depth, j * LANES : (j + 1) * LANES]
                            for j in range(XBLOCK)
                        ],
                        axis=0,
                    )
                    for part in parts
                )
        sums = plane_sums(fields, weights)
        for (c, kind), value in sums.items():
            sums_ref[c * 3 + kind, pl.ds(x0 + 3, XBLOCK)] = value.reshape(XBLOCK, depth, LANES)
        return carry

    lax.fori_loop(0, PAD // XBLOCK, in_plane, 0)

    def along_x(step, carry):
        x0 = (step // (depth // 8)) * XROWS
        z0 = pl.multiple_of((step % (depth // 8)) * 8, 8)
        for c in range(COMPS):
            held = [sums_ref[c * 3 + kind, pl.ds(x0, XROWS + 6), pl.ds(z0, 8), :] for kind in range(3)]

            def at(kind):
                return lambda d: held[kind][3 + d : 3 + d + XROWS]

            result = band_x(at(STIFF), at(MASS), at(SLOPE))
            for j in range(XROWS):
                start = pl.multiple_of((c * PAD + x0 + j) * depth + z0, 8)
                out[pl.ds(start, 8), :] = result[j]
        return carry

    lax.fori_loop(0, (PAD // XROWS) * (depth // 8), along_x, 0)


def depth_edges(before, after):
    mass, stiff, slope = [], [], []
    for table, den, out, sign in (
        (MASS_INT[1:], MASS_DEN, mass, 1.0),
        (STIFF_INT[1:], STIFF_DEN, stiff, 1.0),
        (SLOPE_INT, SLOPE_DEN, slope, -1.0),
    ):
        coef = [value / den for value in table]
        for z in range(3):
            total = None
            for d in range(z + 1, 4):
                piece = (sign * coef[d - 1]) * before[3 + z - d]
                total = piece if total is None else total + piece
            out.append(total)
        for z in range(3):
            total = None
            for d in range(3 - z, 4):
                piece = coef[d - 1] * after[z + d - 3]
                total = piece if total is None else total + piece
            out.append(total)
    return [jnp.concatenate(parts, axis=0) for parts in (mass, stiff, slope)]


EDGE_ROWS = 80


def finish_kernel(
    groups,
    depth,
    last,
    me_ref,
    sizes_ref,
    partners_ref,
    lame_ref,
    volume,
    own,
    from_before,
    from_after,
    z_before,
    z_after,
    transfer,
    weights,
    order,
    order_back,
    result,
    *rest,
):
    if last:
        field, edge = rest
    else:
        field, own_next, to_before, to_after, low, high, edge = rest
    me = me_ref[0]
    sides, slots = receive_slots(partners_ref, me, groups)
    terms = []
    for p in range(2):
        for f in range(FACES):
            k = p * FACES + f
            far = jnp.where(sides[k] == 0, from_before[slots[k]], from_after[slots[k]])
            mu_face = 0.5 * (lame_ref[me * 2 + p, 0] + lame_ref[partners_ref[p, f] // FACES, 0])
            mat = transfer[p, f]
            zero = jnp.zeros((PAD, PAD), F32)
            both = jnp.concatenate(
                [jnp.concatenate([mat, zero], axis=1), jnp.concatenate([zero, mat], axis=1)], axis=0
            )
            far_high, far_low = split(far)
            mat_high, mat_low = split(both)
            moved = lax.dot_general(
                jnp.concatenate([far_high, far_low, far_high], axis=1),
                jnp.concatenate([mat_high, mat_high, mat_low], axis=1),
                (((1,), (1,)), ((), ())),
                preferred_element_type=F32,
            )
            terms.append(((PENALTY - 1.5) * mu_face) * (own[k] - moved))
    per = COMPS * depth
    stacked = jnp.concatenate([swap_halves(terms[p * FACES + 2 + f]) for p in range(2) for f in range(2)], axis=1)
    term_high, term_low = split(stacked)
    placed = dot(jnp.concatenate([term_high, term_low], axis=0), order_back[...])
    placed = placed[:per] + placed[per:]
    placed = jnp.concatenate([placed[:, g * LANES : (g + 1) * LANES] for g in range(4)], axis=0)
    placed_parts = jnp.concatenate(split(placed), axis=1)
    select = layer_select(sizes_ref)
    for j in range(0, 16, 2):
        pair = jnp.concatenate([select[j], select[j + 1]], axis=0)
        spread = lax.dot_general(
            placed_parts,
            jnp.concatenate([pair, pair], axis=1),
            (((1,), (1,)), ((), ())),
            preferred_element_type=F32,
        )
        for g in range(4):
            for c in range(COMPS):
                for i in range(2):
                    base = (c * PAD + 16 * g + j + i) * depth
                    at = (g * COMPS + c) * depth
                    piece = spread[at : at + depth, i * LANES : (i + 1) * LANES]
                    field[base : base + depth, :] = volume[base : base + depth, :] + piece
    def add_row(x, addend):
        for c in range(COMPS):
            start = c * PAD * depth + x * depth
            if not isinstance(x, int):
                start = pl.multiple_of(start, depth)
            field[pl.ds(start, depth), :] += addend[c * depth : (c + 1) * depth]

    zero = jnp.zeros((per, LANES), F32)
    one, two = terms[0], terms[FACES]
    add_row(0, merge(swap_halves(one), two))
    add_row(1, merge(one, swap_halves(two)))
    one, two = terms[1], terms[FACES + 1]
    add_row(sizes_ref[0, 0] - 1, merge(swap_halves(one), zero))
    add_row(sizes_ref[0, 0] - 2, merge(one, zero))
    add_row(sizes_ref[1, 0] - 1, merge(zero, two))
    add_row(sizes_ref[1, 0] - 2, merge(zero, swap_halves(two)))
    fields = {}
    for c in range(COMPS):
        banded = depth_edges([z_before[c, d] for d in range(HALO)], [z_after[c, d] for d in range(HALO)])
        for kind in range(3):
            fields[(c, kind)] = split(banded[kind])
    sums = plane_sums(fields, weights)
    for (c, kind), value in sums.items():
        for z in range(2 * HALO):
            base = ((c * 3 + kind) * 2 * HALO + z) * EDGE_ROWS
            edge[base : base + 8, :] = jnp.zeros((8, LANES), F32)
            edge[base + 8 + PAD : base + EDGE_ROWS, :] = jnp.zeros((8, LANES), F32)
            edge[base + 8 : base + 8 + PAD, :] = value[z * PAD : (z + 1) * PAD]
    for c in range(COMPS):
        for z in range(2 * HALO):

            def at(kind):
                base = ((c * 3 + kind) * 2 * HALO + z) * EDGE_ROWS + 8
                return lambda d: edge[base + d : base + d + PAD, :]

            plane = z if z < HALO else depth - 2 * HALO + z
            rows = pl.ds(c * PAD * depth + plane, PAD, stride=depth)
            field[rows, :] += band_x(at(STIFF), at(MASS), at(SLOPE))
    size_x, in_y = active_lanes(sizes_ref)
    for k in range(PAD // 2):
        keep_even = in_y & (2 * k < size_x)
        keep_odd = in_y & (2 * k + 1 < size_x)
        for c in range(COMPS):
            base = (c * PAD + 2 * k) * depth
            even = jnp.where(keep_even, field[base : base + depth, :], 0.0)
            odd = jnp.where(keep_odd, field[base + depth : base + 2 * depth, :], 0.0)
            if not last:
                field[base : base + depth, :] = even
                field[base + depth : base + 2 * depth, :] = odd
            result[0, c, :, k * LANES : (k + 1) * LANES] = merge(even, swap_halves(odd))
            result[1, c, :, k * LANES : (k + 1) * LANES] = merge(swap_halves(even), odd)
    if not last:
        send_layers(
            field, sizes_ref, partners_ref, order, own_next, to_before, to_after, low, high, me, groups, depth
        )


def shards(displacement, lame_params, patch_sizes, partners, transfer):
    depth = displacement.shape[2]
    groups = lax.axis_size("patch")
    sections = lax.axis_size("sect")
    me = lax.axis_index("patch").astype(jnp.int32).reshape(1)
    rows = COMPS * PAD * depth
    per = COMPS * depth
    smem = pl.BlockSpec(memory_space=pltpu.SMEM)
    vmem = pl.BlockSpec(memory_space=pltpu.VMEM)
    params = pltpu.CompilerParams(vmem_limit_bytes=VMEM_BYTES)
    z_table = jnp.asarray(depth_table(depth))
    order = jnp.asarray(order_table().astype(ml_dtypes.bfloat16))
    order_back = jnp.asarray(order_table().T.astype(ml_dtypes.bfloat16))

    def shape(*dims, dtype=F32):
        return jax.ShapeDtypeStruct(dims, dtype)

    field_shape = shape(rows, LANES)
    layer_shapes = (
        shape(2 * FACES, per, LANES),
        shape(FACES, per, LANES),
        shape(FACES, per, LANES),
        shape(COMPS, HALO, PAD, LANES),
        shape(COMPS, HALO, PAD, LANES),
    )

    def exchange(layers):
        own, to_before, to_after, low, high = layers
        forward = [(i, (i + 1) % groups) for i in range(groups)]
        backward = [((i + 1) % groups, i) for i in range(groups)]
        from_before = lax.ppermute(to_after, "patch", forward)
        from_after = lax.ppermute(to_before, "patch", backward)
        z_before = lax.ppermute(high, "sect", [(i, i + 1) for i in range(sections - 1)])
        z_after = lax.ppermute(low, "sect", [(i + 1, i) for i in range(sections - 1)])
        return own, from_before, from_after, z_before, z_after

    weights = pl.pallas_call(
        weights_kernel,
        out_shape=shape(len(TILES), 6 * LANES, 2 * LANES, dtype=BF16),
        in_specs=[smem, smem, vmem],
        out_specs=vmem,
        compiler_params=params,
        name="plane_weights",
    )(lame_params, me, jnp.asarray(plane_tables()))

    field, *layers = pl.pallas_call(
        functools.partial(start_kernel, groups, depth),
        out_shape=(field_shape,) + layer_shapes,
        in_specs=[smem, smem, smem, vmem, vmem],
        out_specs=(vmem,) * 6,
        compiler_params=params,
        name="start_layers",
    )(me, patch_sizes, partners, displacement, order)

    def volume(values):
        return pl.pallas_call(
            functools.partial(volume_kernel, depth),
            out_shape=field_shape,
            in_specs=[vmem] * 3,
            out_specs=vmem,
            scratch_shapes=[pltpu.VMEM((9, PAD + 6, depth, LANES), F32)],
            compiler_params=params,
            cost_estimate=pl.CostEstimate(flops=10**10, bytes_accessed=8 * 10**6, transcendentals=0),
            name="volume_terms",
        )(values, z_table, weights)

    def finish(volume_part, exchanged, last):
        scratch = [pltpu.VMEM((9 * 2 * HALO * EDGE_ROWS, LANES), F32)]
        out_shape = (shape(*displacement.shape),)
        if last:
            scratch = [pltpu.VMEM((rows, LANES), F32)] + scratch
        else:
            out_shape = out_shape + (field_shape,) + layer_shapes
        return pl.pallas_call(
            functools.partial(finish_kernel, groups, depth, last),
            out_shape=out_shape,
            in_specs=[smem] * 4 + [vmem] * 10,
            out_specs=(vmem,) * len(out_shape),
            scratch_shapes=scratch,
            compiler_params=params,
            name="finish_last" if last else "finish_first",
        )(me, patch_sizes, partners, lame_params, volume_part, *exchanged, transfer, weights, order, order_back)

    first_apply, field, *next_layers = finish(volume(field), exchange(layers), False)
    (second_apply,) = finish(volume(field), exchange(next_layers), True)
    return first_apply, second_apply


def solution(mesh):
    return jax.shard_map(
        shards,
        mesh=mesh,
        in_specs=(
            P("patch", None, "sect", None),
            P(),
            P("patch", None),
            P("patch", None),
            P("patch", None, None, None),
        ),
        out_specs=(P("patch", None, "sect", None), P("patch", None, "sect", None)),
        check_vma=False,
    )
```

```python
import functools

import jax
import jax.numpy as jnp
import ml_dtypes
import numpy as np
from jax import lax
from jax.experimental import pallas as pl
from jax.experimental.pallas import tpu as pltpu
from jax.sharding import PartitionSpec as P

PAD = 64
LANES = 128
HALO = 3
COMPS = 3
FACES = 4
MASS_INT = (2416.0, 1191.0, 120.0, 1.0)
STIFF_INT = (80.0, -15.0, -24.0, -1.0)
SLOPE_INT = (245.0, 56.0, 1.0)
MASS_DEN = 5040.0
STIFF_DEN = 120.0
SLOPE_DEN = 720.0
PENALTY = 3.0
XBLOCK = 16
XROWS = 8
MIB = 1024 * 1024
F32 = jnp.float32
BF16 = jnp.bfloat16


def split_np(table):
    high = table.astype(ml_dtypes.bfloat16)
    low = (table - high.astype(np.float64)).astype(ml_dtypes.bfloat16)
    return high, low


def band_np(size, kind):
    table = np.zeros((size, size))
    for i in range(size):
        for d in range(0, 4):
            for sign in (1, -1):
                j = i + sign * d
                if 0 <= j < size:
                    if kind == "slope":
                        if d:
                            table[i, j] = sign * SLOPE_INT[d - 1] / SLOPE_DEN
                    elif kind == "mass":
                        table[i, j] = MASS_INT[d] / MASS_DEN
                    else:
                        table[i, j] = STIFF_INT[d] / STIFF_DEN
    return table


def depth_table(depth):
    table = np.concatenate([band_np(depth, k) for k in ("mass", "stiff", "slope")], axis=0)
    high, low = split_np(table)
    return np.concatenate([high, high, low], axis=1)


def in_kernel_bands():
    rows = lax.broadcasted_iota(jnp.int32, (LANES, LANES), 0)
    cols = lax.broadcasted_iota(jnp.int32, (LANES, LANES), 1)
    ahead = jnp.where(rows // PAD == cols // PAD, rows - cols, PAD)
    apart = jnp.abs(ahead)
    mass = jnp.zeros((LANES, LANES), F32)
    stiff, slope = mass, mass
    for d in range(4):
        mass = jnp.where(apart == d, MASS_INT[d] / MASS_DEN, mass)
        stiff = jnp.where(apart == d, STIFF_INT[d] / STIFF_DEN, stiff)
        if d:
            slope = jnp.where(ahead == d, SLOPE_INT[d - 1] / SLOPE_DEN, slope)
            slope = jnp.where(ahead == -d, -SLOPE_INT[d - 1] / SLOPE_DEN, slope)
    return mass, stiff, slope


def layer_order():
    rows = lax.broadcasted_iota(jnp.int32, (512, 512), 0)
    cols = lax.broadcasted_iota(jnp.int32, (512, 512), 1)
    x = (rows // 128) * 16 + (rows // 8) % 16
    return jnp.where(cols == (rows % 8) * 64 + x, 1.0, 0.0).astype(BF16)


def split(values):
    high = values.astype(BF16)
    low = (values - high.astype(F32)).astype(BF16)
    return high, low


def lane_iota(shape=(1, LANES)):
    return lax.broadcasted_iota(jnp.int32, shape, len(shape) - 1)


def swap_halves(values):
    return pltpu.roll(values, PAD, axis=values.ndim - 1)


def merge(low_half, high_half):
    return jnp.where(lane_iota() < PAD, low_half, high_half)


def dot(a, b):
    return jnp.dot(a, b, preferred_element_type=F32)


def face_sides(partners_ref, me, groups):
    before = lax.rem(me + groups - 1, groups)
    codes = [partners_ref[k // FACES, k % FACES] for k in range(2 * FACES)]
    sides = [jnp.where(code // (2 * FACES) == before, 0, 1) for code in codes]
    return codes, sides


def send_sources(partners_ref, me, groups):
    codes, sides = face_sides(partners_ref, me, groups)
    sources = [[jnp.int32(0)] * FACES for _ in range(2)]
    for k in range(2 * FACES):
        rank = jnp.int32(0)
        for other in range(2 * FACES):
            if other != k:
                below = (sides[other] == sides[k]) & (codes[other] < codes[k])
                rank = rank + jnp.where(below, 1, 0)
        for side in range(2):
            for slot in range(FACES):
                hit = (sides[k] == side) & (rank == slot)
                sources[side][slot] = jnp.where(hit, k, sources[side][slot])
    return sources


def receive_slots(partners_ref, me, groups):
    _, sides = face_sides(partners_ref, me, groups)
    slots = []
    for k in range(2 * FACES):
        rank = jnp.int32(0)
        for other in range(k):
            rank = rank + jnp.where(sides[other] == sides[k], 1, 0)
        slots.append(rank)
    return sides, slots


def layer_select(sizes_ref):
    rows = lax.broadcasted_iota(jnp.int32, (LANES, LANES), 0)
    cols = lax.broadcasted_iota(jnp.int32, (LANES, LANES), 1)
    patch = (cols // 4) % 2
    layer = cols % 4
    size_y = jnp.where(patch == 0, sizes_ref[0, 1], sizes_ref[1, 1])
    at = jnp.where(layer < 2, layer, size_y + 1 - layer)
    base = jnp.where(rows == patch * PAD + at, 1.0, 0.0)
    return [jnp.where(cols // 8 == j, base, 0.0).astype(BF16) for j in range(16)]


def row_at(ref, x, depth):
    parts = []
    for c in range(COMPS):
        start = c * PAD * depth + x * depth
        if not isinstance(x, int):
            start = pl.multiple_of(start, depth)
        parts.append(ref[pl.ds(start, depth), :])
    return jnp.concatenate(parts, axis=0)


def send_layers(field, sizes_ref, partners_ref, order, own, to_pair, to_ring, z_pair, z_ring, me_ref, groups, depth):
    me = me_ref[0]
    even_section = me_ref[1] % 2 == 0
    for c in range(COMPS):
        for d in range(HALO):
            low = field[pl.ds(c * PAD * depth + d, PAD, stride=depth), :]
            high = field[pl.ds(c * PAD * depth + depth - HALO + d, PAD, stride=depth), :]
            z_pair[c, d] = jnp.where(even_section, high, low)
            z_ring[c, d] = jnp.where(even_section, low, high)
    outer, inner = row_at(field, 0, depth), row_at(field, 1, depth)
    own[0] = merge(outer, swap_halves(inner))
    own[FACES] = merge(swap_halves(outer), inner)
    outer, inner = [row_at(field, sizes_ref[0, 0] - 1 - i, depth) for i in range(2)]
    own[1] = merge(outer, swap_halves(inner))
    outer, inner = [row_at(field, sizes_ref[1, 0] - 1 - i, depth) for i in range(2)]
    own[FACES + 1] = merge(swap_halves(outer), inner)
    select = jnp.concatenate(layer_select(sizes_ref), axis=0)
    groups_rows = []
    for g in range(4):
        for c in range(COMPS):
            base = c * PAD * depth + 16 * g * depth
            wide = [field[base + j * depth : base + (j + 1) * depth, :] for j in range(16)]
            groups_rows.append(jnp.concatenate(wide, axis=1))
    rows = jnp.concatenate(groups_rows, axis=0)
    count = rows.shape[0]
    row_high, row_low = split(rows)
    picked = dot(jnp.concatenate([row_high, row_low], axis=0), select)
    picked = picked[:count] + picked[count:]
    per = COMPS * depth
    picked = jnp.concatenate([picked[g * per : (g + 1) * per] for g in range(4)], axis=1)
    pick_high, pick_low = split(picked)
    sorted_layers = dot(jnp.concatenate([pick_high, pick_low], axis=0), order[...])
    sorted_layers = sorted_layers[:per] + sorted_layers[per:]
    for p in range(2):
        for f in range(2):
            at = (p * 2 + f) * LANES
            own[p * FACES + 2 + f] = sorted_layers[:, at : at + LANES]
    sources = send_sources(partners_ref, me, groups)
    even = me % 2 == 0
    for slot in range(FACES):
        to_pair[slot] = own[jnp.where(even, sources[1][slot], sources[0][slot])]
        to_ring[slot] = own[jnp.where(even, sources[0][slot], sources[1][slot])]


def active_lanes(sizes_ref):
    lane = lane_iota()
    size_x = jnp.where(lane < PAD, sizes_ref[0, 0], sizes_ref[1, 0])
    size_y = jnp.where(lane < PAD, sizes_ref[0, 1], sizes_ref[1, 1])
    return size_x, (lane % PAD) < size_y


MASS, STIFF, SLOPE = 0, 1, 2
TILES = (
    (((0, MASS), (0, STIFF)), ((0, STIFF), (0, MASS))),
    (((1, MASS), (1, STIFF)), ((1, STIFF), (1, MASS))),
    (((2, MASS), (2, STIFF)), ((2, STIFF), (2, MASS))),
    (((1, MASS), (2, SLOPE)), ((0, SLOPE), (1, MASS))),
    (((0, SLOPE), (1, SLOPE)), ((2, SLOPE), (2, MASS))),
    (((0, MASS), None), ((1, SLOPE), None)),
)
TERMS = {
    ((0, MASS), (0, STIFF)): (MASS, "both"),
    ((0, MASS), (0, MASS)): (STIFF, "mu"),
    ((0, STIFF), (0, MASS)): (MASS, "mu"),
    ((1, MASS), (0, SLOPE)): (SLOPE, "grad"),
    ((2, SLOPE), (0, SLOPE)): (MASS, "grad"),
    ((1, MASS), (1, STIFF)): (MASS, "mu"),
    ((1, MASS), (1, MASS)): (STIFF, "both"),
    ((1, STIFF), (1, MASS)): (MASS, "mu"),
    ((2, SLOPE), (1, MASS)): (SLOPE, "grad"),
    ((0, MASS), (1, SLOPE)): (SLOPE, "grad"),
    ((2, MASS), (2, STIFF)): (MASS, "mu"),
    ((2, MASS), (2, MASS)): (STIFF, "mu"),
    ((2, STIFF), (2, MASS)): (MASS, "both"),
    ((1, SLOPE), (2, MASS)): (SLOPE, "grad"),
    ((0, SLOPE), (2, SLOPE)): (MASS, "grad"),
}
OUT_SCALE = {STIFF: 1.0 / STIFF_DEN, MASS: 1.0 / MASS_DEN, SLOPE: 1.0 / SLOPE_DEN}


def fill_weights(lame_ref, me, weights):
    first = me * 2
    lane = lane_iota()
    tables = in_kernel_bands()

    def per_lane(one, two):
        return jnp.where(lane < PAD, one, two)

    mu = per_lane(lame_ref[0, first], lame_ref[0, first + 1])
    grad = mu + per_lane(lame_ref[1, first], lame_ref[1, first + 1])
    factors = {"mu": mu, "both": mu + grad, "grad": -grad}
    placed = set()
    for t, (sources, targets) in enumerate(TILES):
        for i, source in enumerate(sources):
            for o, target in enumerate(targets):
                term = TERMS.get((source, target))
                if term is None or (source, target) in placed:
                    block = jnp.zeros((LANES, LANES), F32)
                else:
                    placed.add((source, target))
                    block = tables[term[0]] * (factors[term[1]] * OUT_SCALE[target[1]])
                block_high, block_low = split(block)
                cols = slice(o * LANES, (o + 1) * LANES)
                for part, piece in enumerate((block_high, block_high, block_low)):
                    at = part * 2 * LANES + i * LANES
                    weights[t, at : at + LANES, cols] = piece


def start_kernel(
    groups, depth, me_ref, sizes_any, partners_any, lame_any, disp_any,
    field, own, to_pair, to_ring, z_pair, z_ring, weights, order,
    sizes_ref, partners_ref, lame_ref, disp, sems,
):
    copies = []
    for c in range(COMPS):
        copies.append(pltpu.make_async_copy(disp_any.at[:, c], disp.at[:, c], sems.at[c]))
    small = [
        pltpu.make_async_copy(sizes_any, sizes_ref, sems.at[COMPS]),
        pltpu.make_async_copy(partners_any, partners_ref, sems.at[COMPS + 1]),
        pltpu.make_async_copy(lame_any, lame_ref, sems.at[COMPS + 2]),
    ]
    for copy in small + copies:
        copy.start()
    order[...] = layer_order()
    for copy in small:
        copy.wait()
    me = me_ref[0]
    fill_weights(lame_ref, me, weights)
    size_x, in_y = active_lanes(sizes_ref)
    for c in range(COMPS):
        copies[c].wait()
        for k in range(PAD // 2):
            keep_even = in_y & (2 * k < size_x)
            keep_odd = in_y & (2 * k + 1 < size_x)
            one = disp[0, c, :, k * LANES : (k + 1) * LANES]
            two = disp[1, c, :, k * LANES : (k + 1) * LANES]
            even = merge(one, swap_halves(two))
            odd = merge(swap_halves(one), two)
            base = (c * PAD + 2 * k) * depth
            field[base : base + depth, :] = jnp.where(keep_even, even, 0.0)
            field[base + depth : base + 2 * depth, :] = jnp.where(keep_odd, odd, 0.0)
    send_layers(field, sizes_ref, partners_ref, order, own, to_pair, to_ring, z_pair, z_ring, me_ref, groups, depth)


def plane_sums(fields, weights):
    sums = {}
    for t, (sources, targets) in enumerate(TILES):
        if sources[1] is None:
            high, low = fields[sources[0]]
            weight = jnp.concatenate(
                [weights[t, part * 2 * LANES : part * 2 * LANES + LANES, :LANES] for part in range(3)], axis=0
            )
        else:
            high, low = [jnp.concatenate([fields[s][part] for s in sources], axis=1) for part in range(2)]
            weight = weights[t]
        out = dot(jnp.concatenate([high, low, high], axis=1), weight)
        for o, target in enumerate(targets):
            if target is not None:
                piece = out[:, o * LANES : (o + 1) * LANES]
                sums[target] = piece if target not in sums else sums[target] + piece
    return sums


def band_x(stiff, mass, slope):
    total = STIFF_INT[0] * stiff(0) + MASS_INT[0] * mass(0)
    for d in (1, 2):
        total = total + STIFF_INT[d] * (stiff(d) + stiff(-d))
        total = total + MASS_INT[d] * (mass(d) + mass(-d))
        total = total + SLOPE_INT[d - 1] * (slope(d) - slope(-d))
    return total + ((mass(3) + mass(-3)) - (stiff(3) + stiff(-3))) + (slope(3) - slope(-3))


def volume_kernel(depth, field, z_table, weights, out, sums_ref):
    for i in range(9):
        for x in (0, 1, 2, PAD + 3, PAD + 4, PAD + 5):
            sums_ref[i, x] = jnp.zeros((depth, LANES), F32)

    def in_plane(block, carry):
        x0 = block * XBLOCK
        fields = {}
        for c in range(COMPS):
            start = pl.multiple_of((c * PAD + x0) * depth, XBLOCK * depth)
            rows = field[pl.ds(start, XBLOCK * depth), :]
            wide = jnp.concatenate([rows[j * depth : (j + 1) * depth] for j in range(XBLOCK)], axis=1)
            high, low = split(wide)
            banded = dot(z_table[...], jnp.concatenate([high, low, high], axis=0))
            parts = split(banded)
            for kind in range(3):
                fields[(c, kind)] = tuple(
                    jnp.concatenate(
                        [
                            part[kind * depth : (kind + 1) * depth, j * LANES : (j + 1) * LANES]
                            for j in range(XBLOCK)
                        ],
                        axis=0,
                    )
                    for part in parts
                )
        sums = plane_sums(fields, weights)
        for (c, kind), value in sums.items():
            sums_ref[c * 3 + kind, pl.ds(x0 + 3, XBLOCK)] = value.reshape(XBLOCK, depth, LANES)
        return carry

    lax.fori_loop(0, PAD // XBLOCK, in_plane, 0)

    def along_x(step, carry):
        x0 = (step // (depth // 8)) * XROWS
        z0 = pl.multiple_of((step % (depth // 8)) * 8, 8)
        for c in range(COMPS):
            held = [sums_ref[c * 3 + kind, pl.ds(x0, XROWS + 6), pl.ds(z0, 8), :] for kind in range(3)]

            def at(kind):
                return lambda d: held[kind][3 + d : 3 + d + XROWS]

            result = band_x(at(STIFF), at(MASS), at(SLOPE))
            for j in range(XROWS):
                start = pl.multiple_of((c * PAD + x0 + j) * depth + z0, 8)
                out[pl.ds(start, 8), :] = result[j]
        return carry

    lax.fori_loop(0, (PAD // XROWS) * (depth // 8), along_x, 0)


def depth_edges(before, after):
    mass, stiff, slope = [], [], []
    for table, den, out, sign in (
        (MASS_INT[1:], MASS_DEN, mass, 1.0),
        (STIFF_INT[1:], STIFF_DEN, stiff, 1.0),
        (SLOPE_INT, SLOPE_DEN, slope, -1.0),
    ):
        coef = [value / den for value in table]
        for z in range(3):
            total = None
            for d in range(z + 1, 4):
                piece = (sign * coef[d - 1]) * before[3 + z - d]
                total = piece if total is None else total + piece
            out.append(total)
        for z in range(3):
            total = None
            for d in range(3 - z, 4):
                piece = coef[d - 1] * after[z + d - 3]
                total = piece if total is None else total + piece
            out.append(total)
    return [jnp.concatenate(parts, axis=0) for parts in (mass, stiff, slope)]


EDGE_ROWS = 80


def finish_kernel(
    groups,
    depth,
    last,
    me_ref,
    sizes_ref,
    partners_ref,
    lame_ref,
    volume,
    own,
    from_pair,
    from_ring,
    z_pair,
    z_ring,
    transfer,
    weights,
    order,
    result_any,
    *rest,
):
    if last:
        field, edge, result, sems = rest
    else:
        field, *sends, edge, result, sems = rest
    me = me_ref[0]
    pair_side = 1 - me % 2
    even_section = me_ref[1] % 2 == 0
    sides, slots = receive_slots(partners_ref, me, groups)
    terms = []
    for p in range(2):
        for f in range(FACES):
            k = p * FACES + f
            far = jnp.where(sides[k] == pair_side, from_pair[slots[k]], from_ring[slots[k]])
            mu_face = 0.5 * (lame_ref[0, me * 2 + p] + lame_ref[0, partners_ref[p, f] // FACES])
            mat = transfer[p, f]
            zero = jnp.zeros((PAD, PAD), F32)
            both = jnp.concatenate(
                [jnp.concatenate([mat, zero], axis=1), jnp.concatenate([zero, mat], axis=1)], axis=0
            )
            far_high, far_low = split(far)
            mat_high, mat_low = split(both)
            moved = lax.dot_general(
                jnp.concatenate([far_high, far_low, far_high], axis=1),
                jnp.concatenate([mat_high, mat_high, mat_low], axis=1),
                (((1,), (1,)), ((), ())),
                preferred_element_type=F32,
            )
            terms.append(((PENALTY - 1.5) * mu_face) * (own[k] - moved))
    per = COMPS * depth
    stacked = jnp.concatenate([swap_halves(terms[p * FACES + 2 + f]) for p in range(2) for f in range(2)], axis=1)
    term_high, term_low = split(stacked)
    placed = lax.dot_general(
        jnp.concatenate([term_high, term_low], axis=0),
        order[...],
        (((1,), (1,)), ((), ())),
        preferred_element_type=F32,
    )
    placed = placed[:per] + placed[per:]
    placed = jnp.concatenate([placed[:, g * LANES : (g + 1) * LANES] for g in range(4)], axis=0)
    placed_parts = jnp.concatenate(split(placed), axis=1)
    select = layer_select(sizes_ref)
    for j in range(0, 16, 2):
        pair = jnp.concatenate([select[j], select[j + 1]], axis=0)
        spread = lax.dot_general(
            placed_parts,
            jnp.concatenate([pair, pair], axis=1),
            (((1,), (1,)), ((), ())),
            preferred_element_type=F32,
        )
        for g in range(4):
            for c in range(COMPS):
                for i in range(2):
                    base = (c * PAD + 16 * g + j + i) * depth
                    at = (g * COMPS + c) * depth
                    piece = spread[at : at + depth, i * LANES : (i + 1) * LANES]
                    field[base : base + depth, :] = volume[base : base + depth, :] + piece
    def add_row(x, addend):
        for c in range(COMPS):
            start = c * PAD * depth + x * depth
            if not isinstance(x, int):
                start = pl.multiple_of(start, depth)
            field[pl.ds(start, depth), :] += addend[c * depth : (c + 1) * depth]

    zero = jnp.zeros((per, LANES), F32)
    one, two = terms[0], terms[FACES]
    add_row(0, merge(swap_halves(one), two))
    add_row(1, merge(one, swap_halves(two)))
    one, two = terms[1], terms[FACES + 1]
    add_row(sizes_ref[0, 0] - 1, merge(swap_halves(one), zero))
    add_row(sizes_ref[0, 0] - 2, merge(one, zero))
    add_row(sizes_ref[1, 0] - 1, merge(zero, two))
    add_row(sizes_ref[1, 0] - 2, merge(zero, swap_halves(two)))
    fields = {}
    for c in range(COMPS):
        before = [jnp.where(even_section, z_ring[c, d], z_pair[c, d]) for d in range(HALO)]
        after = [jnp.where(even_section, z_pair[c, d], z_ring[c, d]) for d in range(HALO)]
        banded = depth_edges(before, after)
        for kind in range(3):
            fields[(c, kind)] = split(banded[kind])
    sums = plane_sums(fields, weights)
    for (c, kind), value in sums.items():
        for z in range(2 * HALO):
            base = ((c * 3 + kind) * 2 * HALO + z) * EDGE_ROWS
            edge[base : base + 8, :] = jnp.zeros((8, LANES), F32)
            edge[base + 8 + PAD : base + EDGE_ROWS, :] = jnp.zeros((8, LANES), F32)
            edge[base + 8 : base + 8 + PAD, :] = value[z * PAD : (z + 1) * PAD]
    size_x, in_y = active_lanes(sizes_ref)
    copies = []
    for c in range(COMPS):
        for z in range(2 * HALO):

            def at(kind):
                base = ((c * 3 + kind) * 2 * HALO + z) * EDGE_ROWS + 8
                return lambda d: edge[base + d : base + d + PAD, :]

            plane = z if z < HALO else depth - 2 * HALO + z
            rows = pl.ds(c * PAD * depth + plane, PAD, stride=depth)
            field[rows, :] += band_x(at(STIFF), at(MASS), at(SLOPE))
        for k in range(PAD // 2):
            keep_even = in_y & (2 * k < size_x)
            keep_odd = in_y & (2 * k + 1 < size_x)
            base = (c * PAD + 2 * k) * depth
            even = jnp.where(keep_even, field[base : base + depth, :], 0.0)
            odd = jnp.where(keep_odd, field[base + depth : base + 2 * depth, :], 0.0)
            if not last:
                field[base : base + depth, :] = even
                field[base + depth : base + 2 * depth, :] = odd
            result[0, c, :, k * LANES : (k + 1) * LANES] = merge(even, swap_halves(odd))
            result[1, c, :, k * LANES : (k + 1) * LANES] = merge(swap_halves(even), odd)
        copies.append(pltpu.make_async_copy(result.at[:, c], result_any.at[:, c], sems.at[c]))
        copies[-1].start()
    if not last:
        send_layers(field, sizes_ref, partners_ref, order, *sends, me_ref, groups, depth)
    for copy in copies:
        copy.wait()


def shards(displacement, lame_params, patch_sizes, partners, transfer):
    depth = displacement.shape[2]
    groups = lax.axis_size("patch")
    sections = lax.axis_size("sect")
    me = jnp.stack([lax.axis_index("patch"), lax.axis_index("sect")]).astype(jnp.int32)
    rows = COMPS * PAD * depth
    per = COMPS * depth
    smem = pl.BlockSpec(memory_space=pltpu.SMEM)
    vmem = pl.BlockSpec(memory_space=pltpu.VMEM)
    away = pl.BlockSpec(memory_space=pl.ANY)
    z_table = jnp.asarray(depth_table(depth))
    lame = lame_params.T

    def shape(*dims, dtype=F32):
        return pltpu.VMEM(dims, dtype)

    def near(values):
        return pltpu.with_memory_space_constraint(values, pltpu.VMEM)

    def far(values):
        return pltpu.with_memory_space_constraint(values, pltpu.HBM)

    def params(mib):
        return pltpu.CompilerParams(vmem_limit_bytes=mib * MIB)

    field_shape = shape(rows, LANES)
    layer_shapes = (
        shape(2 * FACES, per, LANES),
        shape(FACES, per, LANES),
        shape(FACES, per, LANES),
        shape(COMPS, HALO, PAD, LANES),
        shape(COMPS, HALO, PAD, LANES),
    )

    def both_ways(pairs):
        return pairs + [(j, i) for i, j in pairs]

    def exchange(layers):
        own, to_pair, to_ring, z_pair, z_ring = layers
        z_pair = lax.ppermute(z_pair, "sect", both_ways([(i, i + 1) for i in range(0, sections - 1, 2)]))
        z_ring = lax.ppermute(z_ring, "sect", both_ways([(i, i + 1) for i in range(1, sections - 1, 2)]))
        from_pair = lax.ppermute(to_pair, "patch", both_ways([(i, i + 1) for i in range(0, groups, 2)]))
        from_ring = lax.ppermute(to_ring, "patch", both_ways([(i, (i + 1) % groups) for i in range(1, groups, 2)]))
        return own, from_pair, from_ring, z_pair, z_ring

    field, *layers, weights, order = pl.pallas_call(
        functools.partial(start_kernel, groups, depth),
        out_shape=(field_shape,)
        + layer_shapes
        + (shape(len(TILES), 6 * LANES, 2 * LANES, dtype=BF16), shape(512, 512, dtype=BF16)),
        in_specs=[smem] + [away] * 4,
        out_specs=(vmem,) * 8,
        scratch_shapes=[
            pltpu.SMEM(patch_sizes.shape, jnp.int32),
            pltpu.SMEM(partners.shape, jnp.int32),
            pltpu.SMEM(lame.shape, F32),
            pltpu.VMEM(displacement.shape, F32),
            pltpu.SemaphoreType.DMA((COMPS + 3,)),
        ],
        compiler_params=params(24),
        name="start_layers",
    )(me, far(patch_sizes), far(partners), far(lame), far(displacement))

    def volume(values):
        return pl.pallas_call(
            functools.partial(volume_kernel, depth),
            out_shape=field_shape,
            in_specs=[vmem] * 3,
            out_specs=vmem,
            scratch_shapes=[pltpu.VMEM((9, PAD + 6, depth, LANES), F32)],
            compiler_params=params(28),
            cost_estimate=pl.CostEstimate(flops=10**10, bytes_accessed=8 * 10**6, transcendentals=0),
            name="volume_terms",
        )(near(values), z_table, near(weights))

    def finish(volume_part, exchanged, last):
        scratch = [
            pltpu.VMEM((9 * 2 * HALO * EDGE_ROWS, LANES), F32),
            pltpu.VMEM(displacement.shape, F32),
            pltpu.SemaphoreType.DMA((COMPS,)),
        ]
        out_shape = (jax.ShapeDtypeStruct(displacement.shape, F32),)
        if last:
            scratch = [pltpu.VMEM((rows, LANES), F32)] + scratch
        else:
            out_shape = out_shape + (field_shape,) + layer_shapes
        return pl.pallas_call(
            functools.partial(finish_kernel, groups, depth, last),
            out_shape=out_shape,
            in_specs=[smem] * 4 + [vmem] * 9,
            out_specs=(away,) + (vmem,) * (len(out_shape) - 1),
            scratch_shapes=scratch,
            compiler_params=params(28),
            name="finish_last" if last else "finish_first",
        )(
            me,
            far(patch_sizes),
            far(partners),
            far(lame),
            near(volume_part),
            *[near(part) for part in exchanged],
            transfer,
            near(weights),
            near(order),
        )

    first_apply, field, *next_layers = finish(volume(field), exchange(layers), False)
    (second_apply,) = finish(volume(field), exchange(next_layers), True)
    return first_apply, second_apply


def solution(mesh):
    return jax.shard_map(
        shards,
        mesh=mesh,
        in_specs=(
            P("patch", None, "sect", None),
            P(),
            P("patch", None),
            P("patch", None),
            P("patch", None, None, None),
        ),
        out_specs=(P("patch", None, "sect", None), P("patch", None, "sect", None)),
        check_vma=False,
    )
```

```python
import functools

import jax
import jax.numpy as jnp
import ml_dtypes
import numpy as np
from jax import lax
from jax.experimental import pallas as pl
from jax.experimental.pallas import tpu as pltpu
from jax.sharding import PartitionSpec as P

PAD = 64
LANES = 128
HALO = 3
COMPS = 3
FACES = 4
MASS_INT = (2416.0, 1191.0, 120.0, 1.0)
STIFF_INT = (80.0, -15.0, -24.0, -1.0)
SLOPE_INT = (245.0, 56.0, 1.0)
MASS_DEN = 5040.0
STIFF_DEN = 120.0
SLOPE_DEN = 720.0
PENALTY = 3.0
XBLOCK = 16
XROWS = 8
MIB = 1024 * 1024
F32 = jnp.float32
BF16 = jnp.bfloat16


def split_np(table):
    high = table.astype(ml_dtypes.bfloat16)
    low = (table - high.astype(np.float64)).astype(ml_dtypes.bfloat16)
    return high, low


def band_np(size, kind):
    table = np.zeros((size, size))
    for i in range(size):
        for d in range(0, 4):
            for sign in (1, -1):
                j = i + sign * d
                if 0 <= j < size:
                    if kind == "slope":
                        if d:
                            table[i, j] = sign * SLOPE_INT[d - 1] / SLOPE_DEN
                    elif kind == "mass":
                        table[i, j] = MASS_INT[d] / MASS_DEN
                    else:
                        table[i, j] = STIFF_INT[d] / STIFF_DEN
    return table


def depth_table(depth):
    table = np.concatenate([band_np(depth, k) for k in ("mass", "stiff", "slope")], axis=0)
    high, low = split_np(table)
    return np.concatenate([high, high, low], axis=1)


def in_kernel_bands():
    rows = lax.broadcasted_iota(jnp.int32, (LANES, LANES), 0)
    cols = lax.broadcasted_iota(jnp.int32, (LANES, LANES), 1)
    ahead = jnp.where(rows // PAD == cols // PAD, rows - cols, PAD)
    apart = jnp.abs(ahead)
    mass = jnp.zeros((LANES, LANES), F32)
    stiff, slope = mass, mass
    for d in range(4):
        mass = jnp.where(apart == d, MASS_INT[d] / MASS_DEN, mass)
        stiff = jnp.where(apart == d, STIFF_INT[d] / STIFF_DEN, stiff)
        if d:
            slope = jnp.where(ahead == d, SLOPE_INT[d - 1] / SLOPE_DEN, slope)
            slope = jnp.where(ahead == -d, -SLOPE_INT[d - 1] / SLOPE_DEN, slope)
    return mass, stiff, slope


def layer_order():
    rows = lax.broadcasted_iota(jnp.int32, (512, 512), 0)
    cols = lax.broadcasted_iota(jnp.int32, (512, 512), 1)
    x = (rows // 128) * 16 + (rows // 8) % 16
    return jnp.where(cols == (rows % 8) * 64 + x, 1.0, 0.0).astype(BF16)


def split(values):
    high = values.astype(BF16)
    low = (values - high.astype(F32)).astype(BF16)
    return high, low


def lane_iota(shape=(1, LANES)):
    return lax.broadcasted_iota(jnp.int32, shape, len(shape) - 1)


def swap_halves(values):
    return pltpu.roll(values, PAD, axis=values.ndim - 1)


def merge(low_half, high_half):
    return jnp.where(lane_iota() < PAD, low_half, high_half)


def dot(a, b):
    return jnp.dot(a, b, preferred_element_type=F32)


def face_sides(partners_ref, me, groups):
    before = lax.rem(me + groups - 1, groups)
    codes = [partners_ref[k // FACES, k % FACES] for k in range(2 * FACES)]
    sides = [jnp.where(code // (2 * FACES) == before, 0, 1) for code in codes]
    return codes, sides


def send_sources(partners_ref, me, groups):
    codes, sides = face_sides(partners_ref, me, groups)
    sources = [[jnp.int32(0)] * FACES for _ in range(2)]
    for k in range(2 * FACES):
        rank = jnp.int32(0)
        for other in range(2 * FACES):
            if other != k:
                below = (sides[other] == sides[k]) & (codes[other] < codes[k])
                rank = rank + jnp.where(below, 1, 0)
        for side in range(2):
            for slot in range(FACES):
                hit = (sides[k] == side) & (rank == slot)
                sources[side][slot] = jnp.where(hit, k, sources[side][slot])
    return sources


def receive_slots(partners_ref, me, groups):
    _, sides = face_sides(partners_ref, me, groups)
    slots = []
    for k in range(2 * FACES):
        rank = jnp.int32(0)
        for other in range(k):
            rank = rank + jnp.where(sides[other] == sides[k], 1, 0)
        slots.append(rank)
    return sides, slots


def layer_select(sizes_ref):
    rows = lax.broadcasted_iota(jnp.int32, (LANES, LANES), 0)
    cols = lax.broadcasted_iota(jnp.int32, (LANES, LANES), 1)
    patch = (cols // 4) % 2
    layer = cols % 4
    size_y = jnp.where(patch == 0, sizes_ref[0, 1], sizes_ref[1, 1])
    at = jnp.where(layer < 2, layer, size_y + 1 - layer)
    base = jnp.where(rows == patch * PAD + at, 1.0, 0.0)
    return [jnp.where(cols // 8 == j, base, 0.0).astype(BF16) for j in range(16)]


def row_at(ref, x, depth):
    parts = []
    for c in range(COMPS):
        start = c * PAD * depth + x * depth
        if not isinstance(x, int):
            start = pl.multiple_of(start, depth)
        parts.append(ref[pl.ds(start, depth), :])
    return jnp.concatenate(parts, axis=0)


def send_layers(field, sizes_ref, partners_ref, order, own, to_pair, to_ring, z_pair, z_ring, groups, depth):
    me = lax.axis_index("patch")
    even_section = lax.axis_index("sect") % 2 == 0
    for c in range(COMPS):
        for d in range(HALO):
            low = field[pl.ds(c * PAD * depth + d, PAD, stride=depth), :]
            high = field[pl.ds(c * PAD * depth + depth - HALO + d, PAD, stride=depth), :]
            z_pair[c, d] = jnp.where(even_section, high, low)
            z_ring[c, d] = jnp.where(even_section, low, high)
    outer, inner = row_at(field, 0, depth), row_at(field, 1, depth)
    own[0] = merge(outer, swap_halves(inner))
    own[FACES] = merge(swap_halves(outer), inner)
    outer, inner = [row_at(field, sizes_ref[0, 0] - 1 - i, depth) for i in range(2)]
    own[1] = merge(outer, swap_halves(inner))
    outer, inner = [row_at(field, sizes_ref[1, 0] - 1 - i, depth) for i in range(2)]
    own[FACES + 1] = merge(swap_halves(outer), inner)
    select = jnp.concatenate(layer_select(sizes_ref), axis=0)
    groups_rows = []
    for g in range(4):
        for c in range(COMPS):
            base = c * PAD * depth + 16 * g * depth
            wide = [field[base + j * depth : base + (j + 1) * depth, :] for j in range(16)]
            groups_rows.append(jnp.concatenate(wide, axis=1))
    rows = jnp.concatenate(groups_rows, axis=0)
    count = rows.shape[0]
    row_high, row_low = split(rows)
    picked = dot(jnp.concatenate([row_high, row_low], axis=0), select)
    picked = picked[:count] + picked[count:]
    per = COMPS * depth
    picked = jnp.concatenate([picked[g * per : (g + 1) * per] for g in range(4)], axis=1)
    pick_high, pick_low = split(picked)
    sorted_layers = dot(jnp.concatenate([pick_high, pick_low], axis=0), order[...])
    sorted_layers = sorted_layers[:per] + sorted_layers[per:]
    for p in range(2):
        for f in range(2):
            at = (p * 2 + f) * LANES
            own[p * FACES + 2 + f] = sorted_layers[:, at : at + LANES]
    sources = send_sources(partners_ref, me, groups)
    even = me % 2 == 0
    for slot in range(FACES):
        to_pair[slot] = own[jnp.where(even, sources[1][slot], sources[0][slot])]
        to_ring[slot] = own[jnp.where(even, sources[0][slot], sources[1][slot])]


def active_lanes(sizes_ref):
    lane = lane_iota()
    size_x = jnp.where(lane < PAD, sizes_ref[0, 0], sizes_ref[1, 0])
    size_y = jnp.where(lane < PAD, sizes_ref[0, 1], sizes_ref[1, 1])
    return size_x, (lane % PAD) < size_y


MASS, STIFF, SLOPE = 0, 1, 2
TILES = (
    (((0, MASS), (0, STIFF)), ((0, STIFF), (0, MASS))),
    (((1, MASS), (1, STIFF)), ((1, STIFF), (1, MASS))),
    (((2, MASS), (2, STIFF)), ((2, STIFF), (2, MASS))),
    (((1, MASS), (2, SLOPE)), ((0, SLOPE), (1, MASS))),
    (((0, SLOPE), (1, SLOPE)), ((2, SLOPE), (2, MASS))),
    (((0, MASS), None), ((1, SLOPE), None)),
)
TERMS = {
    ((0, MASS), (0, STIFF)): (MASS, "both"),
    ((0, MASS), (0, MASS)): (STIFF, "mu"),
    ((0, STIFF), (0, MASS)): (MASS, "mu"),
    ((1, MASS), (0, SLOPE)): (SLOPE, "grad"),
    ((2, SLOPE), (0, SLOPE)): (MASS, "grad"),
    ((1, MASS), (1, STIFF)): (MASS, "mu"),
    ((1, MASS), (1, MASS)): (STIFF, "both"),
    ((1, STIFF), (1, MASS)): (MASS, "mu"),
    ((2, SLOPE), (1, MASS)): (SLOPE, "grad"),
    ((0, MASS), (1, SLOPE)): (SLOPE, "grad"),
    ((2, MASS), (2, STIFF)): (MASS, "mu"),
    ((2, MASS), (2, MASS)): (STIFF, "mu"),
    ((2, STIFF), (2, MASS)): (MASS, "both"),
    ((1, SLOPE), (2, MASS)): (SLOPE, "grad"),
    ((0, SLOPE), (2, SLOPE)): (MASS, "grad"),
}
OUT_SCALE = {STIFF: 1.0 / STIFF_DEN, MASS: 1.0 / MASS_DEN, SLOPE: 1.0 / SLOPE_DEN}


def fill_weights(lame_ref, me, weights):
    first = me * 2
    lane = lane_iota()
    tables = in_kernel_bands()

    def per_lane(one, two):
        return jnp.where(lane < PAD, one, two)

    mu = per_lane(lame_ref[0, first], lame_ref[0, first + 1])
    grad = mu + per_lane(lame_ref[1, first], lame_ref[1, first + 1])
    factors = {"mu": mu, "both": mu + grad, "grad": -grad}
    placed = set()
    for t, (sources, targets) in enumerate(TILES):
        for i, source in enumerate(sources):
            for o, target in enumerate(targets):
                term = TERMS.get((source, target))
                if term is None or (source, target) in placed:
                    block = jnp.zeros((LANES, LANES), F32)
                else:
                    placed.add((source, target))
                    block = tables[term[0]] * (factors[term[1]] * OUT_SCALE[target[1]])
                block_high, block_low = split(block)
                cols = slice(o * LANES, (o + 1) * LANES)
                for part, piece in enumerate((block_high, block_high, block_low)):
                    at = part * 2 * LANES + i * LANES
                    weights[t, at : at + LANES, cols] = piece


def start_kernel(
    groups, depth, sizes_any, partners_any, lame_any, disp_any,
    field, own, to_pair, to_ring, z_pair, z_ring, weights, order,
    sizes_ref, partners_ref, lame_ref, disp, sems,
):
    copies = []
    for c in range(COMPS):
        copies.append(pltpu.make_async_copy(disp_any.at[:, c], disp.at[:, c], sems.at[c]))
    small = [
        pltpu.make_async_copy(sizes_any, sizes_ref, sems.at[COMPS]),
        pltpu.make_async_copy(partners_any, partners_ref, sems.at[COMPS + 1]),
        pltpu.make_async_copy(lame_any, lame_ref, sems.at[COMPS + 2]),
    ]
    for copy in small + copies:
        copy.start()
    order[...] = layer_order()
    for copy in small:
        copy.wait()
    fill_weights(lame_ref, lax.axis_index("patch"), weights)
    size_x, in_y = active_lanes(sizes_ref)
    for c in range(COMPS):
        copies[c].wait()
        for k in range(PAD // 2):
            keep_even = in_y & (2 * k < size_x)
            keep_odd = in_y & (2 * k + 1 < size_x)
            one = disp[0, c, :, k * LANES : (k + 1) * LANES]
            two = disp[1, c, :, k * LANES : (k + 1) * LANES]
            even = merge(one, swap_halves(two))
            odd = merge(swap_halves(one), two)
            base = (c * PAD + 2 * k) * depth
            field[base : base + depth, :] = jnp.where(keep_even, even, 0.0)
            field[base + depth : base + 2 * depth, :] = jnp.where(keep_odd, odd, 0.0)
    send_layers(field, sizes_ref, partners_ref, order, own, to_pair, to_ring, z_pair, z_ring, groups, depth)


def plane_sums(fields, weights):
    sums = {}
    for t, (sources, targets) in enumerate(TILES):
        if sources[1] is None:
            high, low = fields[sources[0]]
            weight = jnp.concatenate(
                [weights[t, part * 2 * LANES : part * 2 * LANES + LANES, :LANES] for part in range(3)], axis=0
            )
        else:
            high, low = [jnp.concatenate([fields[s][part] for s in sources], axis=1) for part in range(2)]
            weight = weights[t]
        out = dot(jnp.concatenate([high, low, high], axis=1), weight)
        for o, target in enumerate(targets):
            if target is not None:
                piece = out[:, o * LANES : (o + 1) * LANES]
                sums[target] = piece if target not in sums else sums[target] + piece
    return sums


def band_x(stiff, mass, slope):
    total = STIFF_INT[0] * stiff(0) + MASS_INT[0] * mass(0)
    for d in (1, 2):
        total = total + STIFF_INT[d] * (stiff(d) + stiff(-d))
        total = total + MASS_INT[d] * (mass(d) + mass(-d))
        total = total + SLOPE_INT[d - 1] * (slope(d) - slope(-d))
    return total + ((mass(3) + mass(-3)) - (stiff(3) + stiff(-3))) + (slope(3) - slope(-3))


def volume_kernel(depth, field, z_table, weights, out, sums_ref):
    for i in range(9):
        for x in (0, 1, 2, PAD + 3, PAD + 4, PAD + 5):
            sums_ref[i, x] = jnp.zeros((depth, LANES), F32)

    def along_z(x0):
        fields = {}
        for c in range(COMPS):
            start = (c * PAD + x0) * depth
            wide = jnp.concatenate(
                [field[start + j * depth : start + (j + 1) * depth, :] for j in range(XBLOCK)], axis=1
            )
            high, low = split(wide)
            banded = dot(z_table[...], jnp.concatenate([high, low, high], axis=0))
            parts = split(banded)
            for kind in range(3):
                fields[(c, kind)] = tuple(
                    jnp.concatenate(
                        [
                            part[kind * depth : (kind + 1) * depth, j * LANES : (j + 1) * LANES]
                            for j in range(XBLOCK)
                        ],
                        axis=0,
                    )
                    for part in parts
                )
        return fields

    def along_x(x0, c, z0):
        held = [sums_ref[c * 3 + kind, x0 : x0 + XROWS + 6, z0 : z0 + 8, :] for kind in range(3)]

        def at(kind):
            return lambda d: held[kind][3 + d : 3 + d + XROWS]

        result = band_x(at(STIFF), at(MASS), at(SLOPE))
        for j in range(XROWS):
            start = (c * PAD + x0 + j) * depth + z0
            out[start : start + 8, :] = result[j]

    done = 0
    for block in range(PAD // XBLOCK + 1):
        x0 = block * XBLOCK
        pieces = []
        while done < PAD and (done + XROWS + 3 <= x0 or x0 == PAD):
            pieces += [(done, c, z0) for c in range(COMPS) for z0 in range(0, depth, 8)]
            done += XROWS
        if x0 < PAD:
            sums = plane_sums(along_z(x0), weights)
            for (c, kind), value in sums.items():
                sums_ref[c * 3 + kind, x0 + 3 : x0 + 3 + XBLOCK] = value.reshape(XBLOCK, depth, LANES)
        for piece in pieces:
            along_x(*piece)


def depth_edges(before, after):
    mass, stiff, slope = [], [], []
    for table, den, out, sign in (
        (MASS_INT[1:], MASS_DEN, mass, 1.0),
        (STIFF_INT[1:], STIFF_DEN, stiff, 1.0),
        (SLOPE_INT, SLOPE_DEN, slope, -1.0),
    ):
        coef = [value / den for value in table]
        for z in range(3):
            total = None
            for d in range(z + 1, 4):
                piece = (sign * coef[d - 1]) * before[3 + z - d]
                total = piece if total is None else total + piece
            out.append(total)
        for z in range(3):
            total = None
            for d in range(3 - z, 4):
                piece = coef[d - 1] * after[z + d - 3]
                total = piece if total is None else total + piece
            out.append(total)
    return [jnp.concatenate(parts, axis=0) for parts in (mass, stiff, slope)]


EDGE_X = PAD + 2 * HALO


def finish_kernel(
    groups, depth, last, sizes_any, partners_any, lame_any, volume, own, from_pair, from_ring, z_pair, z_ring,
    transfer, weights, order, result_any, *rest,
):
    if last:
        field, edge, result, sizes_ref, partners_ref, lame_ref, sems = rest
    else:
        field, *sends, edge, result, sizes_ref, partners_ref, lame_ref, sems = rest
    small = [
        pltpu.make_async_copy(sizes_any, sizes_ref, sems.at[0]),
        pltpu.make_async_copy(partners_any, partners_ref, sems.at[1]),
        pltpu.make_async_copy(lame_any, lame_ref, sems.at[2]),
    ]
    for copy in small:
        copy.start()
    me = lax.axis_index("patch")
    pair_side = 1 - me % 2
    even_section = lax.axis_index("sect") % 2 == 0
    fields = {}
    for c in range(COMPS):
        before = [jnp.where(even_section, z_ring[c, d], z_pair[c, d]) for d in range(HALO)]
        after = [jnp.where(even_section, z_pair[c, d], z_ring[c, d]) for d in range(HALO)]
        banded = depth_edges(before, after)
        for kind in range(3):
            fields[(c, kind)] = split(banded[kind])
    sums = plane_sums(fields, weights)
    for (c, kind), value in sums.items():
        base = (c * 3 + kind) * EDGE_X * 8
        edge[base : base + HALO * 8, :] = jnp.zeros((HALO * 8, LANES), F32)
        edge[base + (HALO + PAD) * 8 : base + EDGE_X * 8, :] = jnp.zeros((HALO * 8, LANES), F32)
        for z in range(2 * HALO):
            slot = z if z < HALO else z + 2
            edge[pl.ds(base + HALO * 8 + slot, PAD, stride=8), :] = value[z * PAD : (z + 1) * PAD]
    for copy in small:
        copy.wait()
    sides, slots = receive_slots(partners_ref, me, groups)
    terms = []
    for p in range(2):
        for f in range(FACES):
            k = p * FACES + f
            far = jnp.where(sides[k] == pair_side, from_pair[slots[k]], from_ring[slots[k]])
            mu_face = 0.5 * (lame_ref[0, me * 2 + p] + lame_ref[0, partners_ref[p, f] // FACES])
            mat = transfer[p, f]
            zero = jnp.zeros((PAD, PAD), F32)
            both = jnp.concatenate(
                [jnp.concatenate([mat, zero], axis=1), jnp.concatenate([zero, mat], axis=1)], axis=0
            )
            far_high, far_low = split(far)
            mat_high, mat_low = split(both)
            moved = lax.dot_general(
                jnp.concatenate([far_high, far_low, far_high], axis=1),
                jnp.concatenate([mat_high, mat_high, mat_low], axis=1),
                (((1,), (1,)), ((), ())),
                preferred_element_type=F32,
            )
            terms.append(((PENALTY - 1.5) * mu_face) * (own[k] - moved))
    per = COMPS * depth
    stacked = jnp.concatenate([swap_halves(terms[p * FACES + 2 + f]) for p in range(2) for f in range(2)], axis=1)
    term_high, term_low = split(stacked)
    placed = lax.dot_general(
        jnp.concatenate([term_high, term_low], axis=0),
        order[...],
        (((1,), (1,)), ((), ())),
        preferred_element_type=F32,
    )
    placed = placed[:per] + placed[per:]
    placed = jnp.concatenate([placed[:, g * LANES : (g + 1) * LANES] for g in range(4)], axis=0)
    placed_parts = jnp.concatenate(split(placed), axis=1)
    select = layer_select(sizes_ref)
    for j in range(0, 16, 2):
        pair = jnp.concatenate([select[j], select[j + 1]], axis=0)
        spread = lax.dot_general(
            placed_parts,
            jnp.concatenate([pair, pair], axis=1),
            (((1,), (1,)), ((), ())),
            preferred_element_type=F32,
        )
        for g in range(4):
            for c in range(COMPS):
                for i in range(2):
                    base = (c * PAD + 16 * g + j + i) * depth
                    at = (g * COMPS + c) * depth
                    piece = spread[at : at + depth, i * LANES : (i + 1) * LANES]
                    field[base : base + depth, :] = volume[base : base + depth, :] + piece
    def add_row(x, addend):
        for c in range(COMPS):
            start = c * PAD * depth + x * depth
            if not isinstance(x, int):
                start = pl.multiple_of(start, depth)
            field[pl.ds(start, depth), :] += addend[c * depth : (c + 1) * depth]

    zero = jnp.zeros((per, LANES), F32)
    one, two = terms[0], terms[FACES]
    add_row(0, merge(swap_halves(one), two))
    add_row(1, merge(one, swap_halves(two)))
    one, two = terms[1], terms[FACES + 1]
    add_row(sizes_ref[0, 0] - 1, merge(swap_halves(one), zero))
    add_row(sizes_ref[0, 0] - 2, merge(one, zero))
    add_row(sizes_ref[1, 0] - 1, merge(zero, two))
    add_row(sizes_ref[1, 0] - 2, merge(zero, swap_halves(two)))
    size_x, in_y = active_lanes(sizes_ref)
    slot_rows = lax.broadcasted_iota(jnp.int32, (8, LANES), 0)
    copies = []
    for c in range(COMPS):
        for x0 in range(0, PAD, XROWS):
            held = []
            for kind in range(3):
                base = ((c * 3 + kind) * EDGE_X + x0) * 8
                held.append(edge[base : base + (XROWS + 2 * HALO) * 8, :].reshape(XROWS + 2 * HALO, 8, LANES))

            def at(kind):
                return lambda d: held[kind][HALO + d : HALO + d + XROWS]

            edges = band_x(at(STIFF), at(MASS), at(SLOPE))

            def whole(x):
                start = (c * PAD + x) * depth
                edge_x = edges[x - x0]
                value = jnp.concatenate(
                    [
                        field[start : start + 8, :] + jnp.where(slot_rows < HALO, edge_x, 0.0),
                        field[start + 8 : start + depth - 8, :],
                        field[start + depth - 8 : start + depth, :] + jnp.where(slot_rows >= 8 - HALO, edge_x, 0.0),
                    ],
                    axis=0,
                )
                value = jnp.where(in_y & (x < size_x), value, 0.0)
                if not last:
                    field[start : start + depth, :] = value
                return value

            for k in range(x0 // 2, (x0 + XROWS) // 2):
                even, odd = whole(2 * k), whole(2 * k + 1)
                result[0, c, :, k * LANES : (k + 1) * LANES] = merge(even, swap_halves(odd))
                result[1, c, :, k * LANES : (k + 1) * LANES] = merge(swap_halves(even), odd)
            if (x0 + XROWS) % (PAD // 2) == 0:
                lanes = pl.ds((x0 + XROWS - PAD // 2) * PAD, PAD * PAD // 2)
                copy = pltpu.make_async_copy(
                    result.at[:, c, :, lanes], result_any.at[:, c, :, lanes], sems.at[3 + len(copies)]
                )
                copy.start()
                copies.append(copy)
    if not last:
        send_layers(field, sizes_ref, partners_ref, order, *sends, groups, depth)
    for copy in copies:
        copy.wait()


def shards(displacement, lame_params, patch_sizes, partners, transfer):
    depth = displacement.shape[2]
    groups = lax.axis_size("patch")
    sections = lax.axis_size("sect")
    rows = COMPS * PAD * depth
    per = COMPS * depth
    vmem = pl.BlockSpec(memory_space=pltpu.VMEM)
    away = pl.BlockSpec(memory_space=pl.ANY)
    z_table = jnp.asarray(depth_table(depth))
    lame = lame_params.T

    def shape(*dims, dtype=F32):
        return pltpu.VMEM(dims, dtype)

    def near(values):
        return pltpu.with_memory_space_constraint(values, pltpu.VMEM)

    def far(values):
        return pltpu.with_memory_space_constraint(values, pltpu.HBM)

    def params(mib):
        return pltpu.CompilerParams(vmem_limit_bytes=mib * MIB)

    field_shape = shape(rows, LANES)
    layer_shapes = (
        shape(2 * FACES, per, LANES),
        shape(FACES, per, LANES),
        shape(FACES, per, LANES),
        shape(COMPS, HALO, PAD, LANES),
        shape(COMPS, HALO, PAD, LANES),
    )

    def both_ways(pairs):
        return pairs + [(j, i) for i, j in pairs]

    def exchange(layers):
        own, to_pair, to_ring, z_pair, z_ring = layers
        z_pair = lax.ppermute(z_pair, "sect", both_ways([(i, i + 1) for i in range(0, sections - 1, 2)]))
        z_ring = lax.ppermute(z_ring, "sect", both_ways([(i, i + 1) for i in range(1, sections - 1, 2)]))
        from_pair = lax.ppermute(to_pair, "patch", both_ways([(i, i + 1) for i in range(0, groups, 2)]))
        from_ring = lax.ppermute(to_ring, "patch", both_ways([(i, (i + 1) % groups) for i in range(1, groups, 2)]))
        return own, from_pair, from_ring, z_pair, z_ring

    field, *layers, weights, order = pl.pallas_call(
        functools.partial(start_kernel, groups, depth),
        out_shape=(field_shape,)
        + layer_shapes
        + (shape(len(TILES), 6 * LANES, 2 * LANES, dtype=BF16), shape(512, 512, dtype=BF16)),
        in_specs=[away] * 4,
        out_specs=(vmem,) * 8,
        scratch_shapes=[
            pltpu.SMEM(patch_sizes.shape, jnp.int32),
            pltpu.SMEM(partners.shape, jnp.int32),
            pltpu.SMEM(lame.shape, F32),
            pltpu.VMEM(displacement.shape, F32),
            pltpu.SemaphoreType.DMA((COMPS + 3,)),
        ],
        compiler_params=params(24),
        name="start_layers",
    )(far(patch_sizes), far(partners), far(lame), far(displacement))

    def volume(values):
        return pl.pallas_call(
            functools.partial(volume_kernel, depth),
            out_shape=field_shape,
            in_specs=[vmem] * 3,
            out_specs=vmem,
            scratch_shapes=[pltpu.VMEM((9, PAD + 6, depth, LANES), F32)],
            compiler_params=params(28),
            cost_estimate=pl.CostEstimate(flops=10**10, bytes_accessed=8 * 10**6, transcendentals=0),
            name="volume_terms",
        )(near(values), z_table, near(weights))

    def finish(volume_part, exchanged, last):
        scratch = [
            pltpu.VMEM((9 * EDGE_X * 8, LANES), F32),
            pltpu.VMEM(displacement.shape, F32),
            pltpu.SMEM(patch_sizes.shape, jnp.int32),
            pltpu.SMEM(partners.shape, jnp.int32),
            pltpu.SMEM(lame.shape, F32),
            pltpu.SemaphoreType.DMA((3 + 2 * COMPS,)),
        ]
        out_shape = (jax.ShapeDtypeStruct(displacement.shape, F32),)
        if last:
            scratch = [pltpu.VMEM((rows, LANES), F32)] + scratch
        else:
            out_shape = out_shape + (field_shape,) + layer_shapes
        return pl.pallas_call(
            functools.partial(finish_kernel, groups, depth, last),
            out_shape=out_shape,
            in_specs=[away] * 3 + [vmem] * 9,
            out_specs=(away,) + (vmem,) * (len(out_shape) - 1),
            scratch_shapes=scratch,
            compiler_params=params(28),
            name="finish_last" if last else "finish_first",
        )(
            far(patch_sizes),
            far(partners),
            far(lame),
            near(volume_part),
            *[near(part) for part in exchanged],
            transfer,
            near(weights),
            near(order),
        )

    first_apply, field, *next_layers = finish(volume(field), exchange(layers), False)
    (second_apply,) = finish(volume(field), exchange(next_layers), True)
    return first_apply, second_apply


def solution(mesh):
    return jax.shard_map(
        shards,
        mesh=mesh,
        in_specs=(
            P("patch", None, "sect", None),
            P(),
            P("patch", None),
            P("patch", None),
            P("patch", None, None, None),
        ),
        out_specs=(P("patch", None, "sect", None), P("patch", None, "sect", None)),
        check_vma=False,
    )
```

```python
import functools

import jax
import jax.numpy as jnp
import ml_dtypes
import numpy as np
from jax import lax
from jax.experimental import pallas as pl
from jax.experimental.pallas import tpu as pltpu
from jax.sharding import PartitionSpec as P

PAD = 64
LANES = 128
HALO = 3
COMPS = 3
FACES = 4
MASS_INT = (2416.0, 1191.0, 120.0, 1.0)
STIFF_INT = (80.0, -15.0, -24.0, -1.0)
SLOPE_INT = (245.0, 56.0, 1.0)
MASS_DEN = 5040.0
STIFF_DEN = 120.0
SLOPE_DEN = 720.0
PENALTY = 3.0
XBLOCK = 16
XROWS = 8
MIB = 1024 * 1024
F32 = jnp.float32
BF16 = jnp.bfloat16


def split_np(table):
    high = table.astype(ml_dtypes.bfloat16)
    low = (table - high.astype(np.float64)).astype(ml_dtypes.bfloat16)
    return high, low


def band_np(size, kind):
    table = np.zeros((size, size))
    for i in range(size):
        for d in range(0, 4):
            for sign in (1, -1):
                j = i + sign * d
                if 0 <= j < size:
                    if kind == "slope":
                        if d:
                            table[i, j] = sign * SLOPE_INT[d - 1] / SLOPE_DEN
                    elif kind == "mass":
                        table[i, j] = MASS_INT[d] / MASS_DEN
                    else:
                        table[i, j] = STIFF_INT[d] / STIFF_DEN
    return table


def depth_table(depth):
    table = np.concatenate([band_np(depth, k) for k in ("mass", "stiff", "slope")], axis=0)
    high, low = split_np(table)
    return np.concatenate([high, high, low], axis=1)


def in_kernel_bands():
    rows = lax.broadcasted_iota(jnp.int32, (LANES, LANES), 0)
    cols = lax.broadcasted_iota(jnp.int32, (LANES, LANES), 1)
    ahead = jnp.where(rows // PAD == cols // PAD, rows - cols, PAD)
    apart = jnp.abs(ahead)
    mass = jnp.zeros((LANES, LANES), F32)
    stiff, slope = mass, mass
    for d in range(4):
        mass = jnp.where(apart == d, MASS_INT[d] / MASS_DEN, mass)
        stiff = jnp.where(apart == d, STIFF_INT[d] / STIFF_DEN, stiff)
        if d:
            slope = jnp.where(ahead == d, SLOPE_INT[d - 1] / SLOPE_DEN, slope)
            slope = jnp.where(ahead == -d, -SLOPE_INT[d - 1] / SLOPE_DEN, slope)
    return mass, stiff, slope


def layer_order():
    rows = lax.broadcasted_iota(jnp.int32, (512, 512), 0)
    cols = lax.broadcasted_iota(jnp.int32, (512, 512), 1)
    x = rows // 128 + 4 * ((rows // 8) % 16)
    return jnp.where(cols == (rows % 8) * 64 + x, 1.0, 0.0).astype(BF16)


def split(values):
    high = values.astype(BF16)
    low = (values - high.astype(F32)).astype(BF16)
    return high, low


def lane_iota(shape=(1, LANES)):
    return lax.broadcasted_iota(jnp.int32, shape, len(shape) - 1)


def swap_halves(values):
    return pltpu.roll(values, PAD, axis=values.ndim - 1)


def merge(low_half, high_half):
    return jnp.where(lane_iota() < PAD, low_half, high_half)


def dot(a, b):
    return jnp.dot(a, b, preferred_element_type=F32)


SIZES, SOURCES, SLOTS, SCALARS = 0, 4, 12, 20


def fill_scalars(sizes_ref, partners_ref, lame_ref, scalars, factors, me, groups):
    for p in range(2):
        for axis in range(2):
            scalars[SIZES + 2 * p + axis] = sizes_ref[p, axis]
    before = lax.rem(me + groups - 1, groups)
    pair_side = 1 - me % 2
    codes = [partners_ref[k // FACES, k % FACES] for k in range(2 * FACES)]
    ring = []
    for code in codes:
        side = jnp.where(code // (2 * FACES) == before, 0, 1)
        ring.append(jnp.where(side == pair_side, 0, 1))
    for k in range(2 * FACES):
        sent, read = jnp.int32(0), jnp.int32(0)
        for other in range(2 * FACES):
            if other != k:
                same = ring[other] == ring[k]
                sent = sent + jnp.where(same & (codes[other] < codes[k]), 1, 0)
                if other < k:
                    read = read + jnp.where(same, 1, 0)
        scalars[SOURCES + ring[k] * FACES + sent] = jnp.int32(k)
        scalars[SLOTS + k] = ring[k] * FACES + read
        p = k // FACES
        factors[k] = (PENALTY - 1.5) * (0.5 * (lame_ref[0, me * 2 + p] + lame_ref[0, codes[k] // FACES]))


def layer_select(scalars):
    rows = lax.broadcasted_iota(jnp.int32, (LANES, LANES), 0)
    cols = lax.broadcasted_iota(jnp.int32, (LANES, LANES), 1)
    patch = (cols // 4) % 2
    layer = cols % 4
    size_y = jnp.where(patch == 0, scalars[SIZES + 1], scalars[SIZES + 3])
    at = jnp.where(layer < 2, layer, size_y + 1 - layer)
    base = jnp.where(rows == patch * PAD + at, 1.0, 0.0)
    return [jnp.where(cols // 8 == j, base, 0.0).astype(BF16) for j in range(16)]


def row_at(ref, x, depth):
    parts = []
    for c in range(COMPS):
        start = c * PAD * depth + x * depth
        if not isinstance(x, int):
            start = pl.multiple_of(start, depth)
        parts.append(ref[pl.ds(start, depth), :])
    return jnp.concatenate(parts, axis=0)


def send_layers(field, scalars, order, own, to_pair, to_ring, z_pair, z_ring, depth):
    even_section = lax.axis_index("sect") % 2 == 0
    for c in range(COMPS):
        for d in range(HALO):
            low = field[pl.ds(c * PAD * depth + d, PAD, stride=depth), :]
            high = field[pl.ds(c * PAD * depth + depth - HALO + d, PAD, stride=depth), :]
            z_pair[c, d] = jnp.where(even_section, high, low)
            z_ring[c, d] = jnp.where(even_section, low, high)
    outer, inner = row_at(field, 0, depth), row_at(field, 1, depth)
    own[0] = merge(outer, swap_halves(inner))
    own[FACES] = merge(swap_halves(outer), inner)
    outer, inner = [row_at(field, scalars[SIZES] - 1 - i, depth) for i in range(2)]
    own[1] = merge(outer, swap_halves(inner))
    outer, inner = [row_at(field, scalars[SIZES + 2] - 1 - i, depth) for i in range(2)]
    own[FACES + 1] = merge(swap_halves(outer), inner)
    select = jnp.concatenate(layer_select(scalars), axis=0)
    groups_rows = []
    for g in range(4):
        for c in range(COMPS):
            starts = [(c * PAD + 4 * j + g) * depth for j in range(16)]
            wide = [field[start : start + depth, :] for start in starts]
            groups_rows.append(jnp.concatenate(wide, axis=1))
    rows = jnp.concatenate(groups_rows, axis=0)
    count = rows.shape[0]
    row_high, row_low = split(rows)
    picked = dot(jnp.concatenate([row_high, row_low], axis=0), select)
    picked = picked[:count] + picked[count:]
    per = COMPS * depth
    picked = jnp.concatenate([picked[g * per : (g + 1) * per] for g in range(4)], axis=1)
    pick_high, pick_low = split(picked)
    sorted_layers = dot(jnp.concatenate([pick_high, pick_low], axis=0), order[...])
    sorted_layers = sorted_layers[:per] + sorted_layers[per:]
    for p in range(2):
        for f in range(2):
            at = (p * 2 + f) * LANES
            own[p * FACES + 2 + f] = sorted_layers[:, at : at + LANES]
    for slot in range(FACES):
        to_pair[slot] = own[scalars[SOURCES + slot]]
        to_ring[slot] = own[scalars[SOURCES + FACES + slot]]


def active_lanes(scalars):
    lane = lane_iota()
    size_x = jnp.where(lane < PAD, scalars[SIZES], scalars[SIZES + 2])
    size_y = jnp.where(lane < PAD, scalars[SIZES + 1], scalars[SIZES + 3])
    return size_x, (lane % PAD) < size_y


MASS, STIFF, SLOPE = 0, 1, 2
TILES = (
    (((0, MASS), (0, STIFF)), ((0, STIFF), (0, MASS))),
    (((1, MASS), (1, STIFF)), ((1, STIFF), (1, MASS))),
    (((2, MASS), (2, STIFF)), ((2, STIFF), (2, MASS))),
    (((1, MASS), (2, SLOPE)), ((0, SLOPE), (1, MASS))),
    (((0, SLOPE), (1, SLOPE)), ((2, SLOPE), (2, MASS))),
    (((0, MASS), None), ((1, SLOPE), None)),
)
TERMS = {
    ((0, MASS), (0, STIFF)): (MASS, "both"),
    ((0, MASS), (0, MASS)): (STIFF, "mu"),
    ((0, STIFF), (0, MASS)): (MASS, "mu"),
    ((1, MASS), (0, SLOPE)): (SLOPE, "grad"),
    ((2, SLOPE), (0, SLOPE)): (MASS, "grad"),
    ((1, MASS), (1, STIFF)): (MASS, "mu"),
    ((1, MASS), (1, MASS)): (STIFF, "both"),
    ((1, STIFF), (1, MASS)): (MASS, "mu"),
    ((2, SLOPE), (1, MASS)): (SLOPE, "grad"),
    ((0, MASS), (1, SLOPE)): (SLOPE, "grad"),
    ((2, MASS), (2, STIFF)): (MASS, "mu"),
    ((2, MASS), (2, MASS)): (STIFF, "mu"),
    ((2, STIFF), (2, MASS)): (MASS, "both"),
    ((1, SLOPE), (2, MASS)): (SLOPE, "grad"),
    ((0, SLOPE), (2, SLOPE)): (MASS, "grad"),
}
OUT_SCALE = {STIFF: 1.0 / STIFF_DEN, MASS: 1.0 / MASS_DEN, SLOPE: 1.0 / SLOPE_DEN}


def fill_weights(lame_ref, me, weights):
    first = me * 2
    lane = lane_iota()
    tables = in_kernel_bands()

    def per_lane(one, two):
        return jnp.where(lane < PAD, one, two)

    mu = per_lane(lame_ref[0, first], lame_ref[0, first + 1])
    grad = mu + per_lane(lame_ref[1, first], lame_ref[1, first + 1])
    factors = {"mu": mu, "both": mu + grad, "grad": -grad}
    placed = set()
    for t, (sources, targets) in enumerate(TILES):
        for i, source in enumerate(sources):
            for o, target in enumerate(targets):
                term = TERMS.get((source, target))
                if term is None or (source, target) in placed:
                    block = jnp.zeros((LANES, LANES), F32)
                else:
                    placed.add((source, target))
                    block = tables[term[0]] * (factors[term[1]] * OUT_SCALE[target[1]])
                block_high, block_low = split(block)
                cols = slice(o * LANES, (o + 1) * LANES)
                for part, piece in enumerate((block_high, block_high, block_low)):
                    at = part * 2 * LANES + i * LANES
                    weights[t, at : at + LANES, cols] = piece


def start_kernel(
    groups, depth, sizes_any, partners_any, lame_any, disp_any,
    field, own, to_pair, to_ring, z_pair, z_ring, weights, order, scalars, factors,
    sizes_ref, partners_ref, lame_ref, disp, sems,
):
    copies = []
    for c in range(COMPS):
        copies.append(pltpu.make_async_copy(disp_any.at[:, c], disp.at[:, c], sems.at[c]))
    small = [
        pltpu.make_async_copy(sizes_any, sizes_ref, sems.at[COMPS]),
        pltpu.make_async_copy(partners_any, partners_ref, sems.at[COMPS + 1]),
        pltpu.make_async_copy(lame_any, lame_ref, sems.at[COMPS + 2]),
    ]
    for copy in small + copies:
        copy.start()
    order[...] = layer_order()
    for copy in small:
        copy.wait()
    me = lax.axis_index("patch")
    fill_scalars(sizes_ref, partners_ref, lame_ref, scalars, factors, me, groups)
    fill_weights(lame_ref, me, weights)
    size_x, in_y = active_lanes(scalars)
    for c in range(COMPS):
        copies[c].wait()
        for k in range(PAD // 2):
            keep_even = in_y & (2 * k < size_x)
            keep_odd = in_y & (2 * k + 1 < size_x)
            one = disp[0, c, :, k * LANES : (k + 1) * LANES]
            two = disp[1, c, :, k * LANES : (k + 1) * LANES]
            even = merge(one, swap_halves(two))
            odd = merge(swap_halves(one), two)
            base = (c * PAD + 2 * k) * depth
            field[base : base + depth, :] = jnp.where(keep_even, even, 0.0)
            field[base + depth : base + 2 * depth, :] = jnp.where(keep_odd, odd, 0.0)
    send_layers(field, scalars, order, own, to_pair, to_ring, z_pair, z_ring, depth)


def plane_sums(fields, weights):
    sums = {}
    for t, (sources, targets) in enumerate(TILES):
        if sources[1] is None:
            high, low = fields[sources[0]]
            weight = jnp.concatenate(
                [weights[t, part * 2 * LANES : part * 2 * LANES + LANES, :LANES] for part in range(3)], axis=0
            )
        else:
            high, low = [jnp.concatenate([fields[s][part] for s in sources], axis=1) for part in range(2)]
            weight = weights[t]
        out = dot(jnp.concatenate([high, low, high], axis=1), weight)
        for o, target in enumerate(targets):
            if target is not None:
                piece = out[:, o * LANES : (o + 1) * LANES]
                sums[target] = piece if target not in sums else sums[target] + piece
    return sums


def band_x(stiff, mass, slope):
    total = STIFF_INT[0] * stiff(0) + MASS_INT[0] * mass(0)
    for d in (1, 2):
        total = total + STIFF_INT[d] * (stiff(d) + stiff(-d))
        total = total + MASS_INT[d] * (mass(d) + mass(-d))
        total = total + SLOPE_INT[d - 1] * (slope(d) - slope(-d))
    return total + ((mass(3) + mass(-3)) - (stiff(3) + stiff(-3))) + (slope(3) - slope(-3))


def to_output(result, c, k, even, odd):
    result[0, c, :, k * LANES : (k + 1) * LANES] = merge(even, swap_halves(odd))
    result[1, c, :, k * LANES : (k + 1) * LANES] = merge(swap_halves(even), odd)


def send_output(result, result_any, sems, part, parts):
    lanes = pl.ds(part * (PAD * PAD // parts), PAD * PAD // parts)
    copy = pltpu.make_async_copy(result.at[:, :, :, lanes], result_any.at[:, :, :, lanes], sems.at[part])
    copy.start()
    return copy


OUT_PARTS = 4


def volume_kernel(depth, field, z_table, weights, out, *rest):
    result_any, sums_ref, result, sems = rest if len(rest) > 1 else (None, *rest, None, None)
    for i in range(9):
        for x in (0, 1, 2, PAD + 3, PAD + 4, PAD + 5):
            sums_ref[i, x] = jnp.zeros((depth, LANES), F32)

    def along_z(x0):
        fields = {}
        for c in range(COMPS):
            start = (c * PAD + x0) * depth
            wide = jnp.concatenate(
                [field[start + j * depth : start + (j + 1) * depth, :] for j in range(XBLOCK)], axis=1
            )
            high, low = split(wide)
            banded = dot(z_table[...], jnp.concatenate([high, low, high], axis=0))
            parts = split(banded)
            for kind in range(3):
                fields[(c, kind)] = tuple(
                    jnp.concatenate(
                        [
                            part[kind * depth : (kind + 1) * depth, j * LANES : (j + 1) * LANES]
                            for j in range(XBLOCK)
                        ],
                        axis=0,
                    )
                    for part in parts
                )
        return fields

    def along_x(x0, c, z0):
        held = [sums_ref[c * 3 + kind, x0 : x0 + XROWS + 6, z0 : z0 + 8, :] for kind in range(3)]

        def at(kind):
            return lambda d: held[kind][3 + d : 3 + d + XROWS]

        result = band_x(at(STIFF), at(MASS), at(SLOPE))
        for j in range(XROWS):
            start = (c * PAD + x0 + j) * depth + z0
            out[start : start + 8, :] = result[j]

    done = 0
    copies = []
    for block in range(PAD // XBLOCK + 1):
        x0 = block * XBLOCK
        pieces = []
        while done < PAD and (done + XROWS + 3 <= x0 or x0 == PAD):
            pieces += [(done, c, z0) for c in range(COMPS) for z0 in range(0, depth, 8)]
            done += XROWS
        if x0 < PAD:
            sums = plane_sums(along_z(x0), weights)
            for (c, kind), value in sums.items():
                sums_ref[c * 3 + kind, x0 + 3 : x0 + 3 + XBLOCK] = value.reshape(XBLOCK, depth, LANES)
        for piece in pieces:
            along_x(*piece)
        if result_any is not None and x0 < PAD:
            for k in range(x0 // 2, (x0 + XBLOCK) // 2):
                for c in range(COMPS):
                    start = (c * PAD + 2 * k) * depth
                    to_output(result, c, k, field[start : start + depth, :], field[start + depth : start + 2 * depth, :])
            copies.append(send_output(result, result_any, sems, block, PAD // XBLOCK))
    for copy in copies:
        copy.wait()


def depth_edges(before, after):
    mass, stiff, slope = [], [], []
    for table, den, out, sign in (
        (MASS_INT[1:], MASS_DEN, mass, 1.0),
        (STIFF_INT[1:], STIFF_DEN, stiff, 1.0),
        (SLOPE_INT, SLOPE_DEN, slope, -1.0),
    ):
        coef = [value / den for value in table]
        for z in range(3):
            total = None
            for d in range(z + 1, 4):
                piece = (sign * coef[d - 1]) * before[3 + z - d]
                total = piece if total is None else total + piece
            out.append(total)
        for z in range(3):
            total = None
            for d in range(3 - z, 4):
                piece = coef[d - 1] * after[z + d - 3]
                total = piece if total is None else total + piece
            out.append(total)
    return [jnp.concatenate(parts, axis=0) for parts in (mass, stiff, slope)]


EDGE_X = PAD + 2 * HALO


def finish_kernel(
    depth, last, scalars, factors, volume, own, from_pair, from_ring, z_pair, z_ring, transfer, weights, order,
    field, *rest,
):
    if last:
        result_any, edge, result, sems = rest
    else:
        *sends, edge = rest
    even_section = lax.axis_index("sect") % 2 == 0
    terms = []
    for k in range(2 * FACES):
        slot = scalars[SLOTS + k]
        far = jnp.where(slot < FACES, from_pair[lax.rem(slot, FACES)], from_ring[lax.rem(slot, FACES)])
        mat = transfer[k // FACES, k % FACES]
        zero = jnp.zeros((PAD, PAD), F32)
        both = jnp.concatenate(
            [jnp.concatenate([mat, zero], axis=1), jnp.concatenate([zero, mat], axis=1)], axis=0
        )
        far_high, far_low = split(far)
        mat_high, mat_low = split(both)
        moved = lax.dot_general(
            jnp.concatenate([far_high, far_low, far_high], axis=1),
            jnp.concatenate([mat_high, mat_high, mat_low], axis=1),
            (((1,), (1,)), ((), ())),
            preferred_element_type=F32,
        )
        terms.append(factors[k] * (own[k] - moved))
    fields = {}
    for c in range(COMPS):
        before = [jnp.where(even_section, z_ring[c, d], z_pair[c, d]) for d in range(HALO)]
        after = [jnp.where(even_section, z_pair[c, d], z_ring[c, d]) for d in range(HALO)]
        banded = depth_edges(before, after)
        for kind in range(3):
            fields[(c, kind)] = split(banded[kind])
    sums = plane_sums(fields, weights)
    for (c, kind), value in sums.items():
        base = (c * 3 + kind) * EDGE_X * 8
        edge[base : base + HALO * 8, :] = jnp.zeros((HALO * 8, LANES), F32)
        edge[base + (HALO + PAD) * 8 : base + EDGE_X * 8, :] = jnp.zeros((HALO * 8, LANES), F32)
        for z in range(2 * HALO):
            slot = z if z < HALO else z + 2
            edge[pl.ds(base + HALO * 8 + slot, PAD, stride=8), :] = value[z * PAD : (z + 1) * PAD]
    per = COMPS * depth
    stacked = jnp.concatenate([swap_halves(terms[p * FACES + 2 + f]) for p in range(2) for f in range(2)], axis=1)
    term_high, term_low = split(stacked)
    placed = lax.dot_general(
        jnp.concatenate([term_high, term_low], axis=0),
        order[...],
        (((1,), (1,)), ((), ())),
        preferred_element_type=F32,
    )
    placed = placed[:per] + placed[per:]
    placed = jnp.concatenate([placed[:, g * LANES : (g + 1) * LANES] for g in range(4)], axis=0)
    placed_parts = jnp.concatenate(split(placed), axis=1)
    select = layer_select(scalars)

    def add_row(x, addend):
        for c in range(COMPS):
            start = c * PAD * depth + x * depth
            if not isinstance(x, int):
                start = pl.multiple_of(start, depth)
            field[pl.ds(start, depth), :] += addend[c * depth : (c + 1) * depth]

    zero = jnp.zeros((per, LANES), F32)
    one, two = terms[0], terms[FACES]
    add_row(0, merge(swap_halves(one), two))
    add_row(1, merge(one, swap_halves(two)))
    one, two = terms[1], terms[FACES + 1]
    add_row(scalars[SIZES] - 1, merge(swap_halves(one), zero))
    add_row(scalars[SIZES] - 2, merge(one, zero))
    add_row(scalars[SIZES + 2] - 1, merge(zero, two))
    add_row(scalars[SIZES + 2] - 2, merge(zero, swap_halves(two)))
    size_x, in_y = active_lanes(scalars)
    slot_rows = lax.broadcasted_iota(jnp.int32, (8, LANES), 0)
    copies = []
    for x0 in range(0, PAD, XROWS):
        j = x0 // 4
        pair = jnp.concatenate([select[j], select[j + 1]], axis=0)
        spread = lax.dot_general(
            placed_parts,
            jnp.concatenate([pair, pair], axis=1),
            (((1,), (1,)), ((), ())),
            preferred_element_type=F32,
        )
        for c in range(COMPS):
            held = []
            for kind in range(3):
                base = ((c * 3 + kind) * EDGE_X + x0) * 8
                held.append(edge[base : base + (XROWS + 2 * HALO) * 8, :].reshape(XROWS + 2 * HALO, 8, LANES))

            def at(kind):
                return lambda d: held[kind][HALO + d : HALO + d + XROWS]

            edges = band_x(at(STIFF), at(MASS), at(SLOPE))

            def whole(x):
                start = (c * PAD + x) * depth
                row, col = ((x % 4) * COMPS + c) * depth, ((x - x0) // 4) * LANES
                value = field[start : start + depth, :] + spread[row : row + depth, col : col + LANES]
                edge_x = edges[x - x0]
                value = jnp.concatenate(
                    [
                        value[:8] + jnp.where(slot_rows < HALO, edge_x, 0.0),
                        value[8 : depth - 8],
                        value[depth - 8 :] + jnp.where(slot_rows >= 8 - HALO, edge_x, 0.0),
                    ],
                    axis=0,
                )
                value = jnp.where(in_y & (x < size_x), value, 0.0)
                if not last:
                    field[start : start + depth, :] = value
                return value

            for k in range(x0 // 2, (x0 + XROWS) // 2):
                even, odd = whole(2 * k), whole(2 * k + 1)
                if last:
                    to_output(result, c, k, even, odd)
        if last and (x0 + XROWS) % (PAD // OUT_PARTS) == 0:
            copies.append(send_output(result, result_any, sems, x0 // (PAD // OUT_PARTS), OUT_PARTS))
    if not last:
        send_layers(field, scalars, order, *sends, depth)
    for copy in copies:
        copy.wait()


def shards(displacement, lame_params, patch_sizes, partners, transfer):
    depth = displacement.shape[2]
    groups = lax.axis_size("patch")
    sections = lax.axis_size("sect")
    rows = COMPS * PAD * depth
    per = COMPS * depth
    smem = pl.BlockSpec(memory_space=pltpu.SMEM)
    vmem = pl.BlockSpec(memory_space=pltpu.VMEM)
    away = pl.BlockSpec(memory_space=pl.ANY)
    z_table = jnp.asarray(depth_table(depth))
    lame = lame_params.T

    def shape(*dims, dtype=F32):
        return pltpu.VMEM(dims, dtype)

    def near(values):
        return pltpu.with_memory_space_constraint(values, pltpu.VMEM)

    def scalar(values):
        return pltpu.with_memory_space_constraint(values, pltpu.SMEM)

    def far(values):
        return pltpu.with_memory_space_constraint(values, pltpu.HBM)

    def params(mib):
        return pltpu.CompilerParams(vmem_limit_bytes=mib * MIB)

    field_shape = shape(rows, LANES)
    layer_shapes = (
        shape(2 * FACES, per, LANES),
        shape(FACES, per, LANES),
        shape(FACES, per, LANES),
        shape(COMPS, HALO, PAD, LANES),
        shape(COMPS, HALO, PAD, LANES),
    )

    def both_ways(pairs):
        return pairs + [(j, i) for i, j in pairs]

    def exchange(layers):
        own, to_pair, to_ring, z_pair, z_ring = layers
        z_pair = lax.ppermute(z_pair, "sect", both_ways([(i, i + 1) for i in range(0, sections - 1, 2)]))
        z_ring = lax.ppermute(z_ring, "sect", both_ways([(i, i + 1) for i in range(1, sections - 1, 2)]))
        from_pair = lax.ppermute(to_pair, "patch", both_ways([(i, i + 1) for i in range(0, groups, 2)]))
        from_ring = lax.ppermute(to_ring, "patch", both_ways([(i, (i + 1) % groups) for i in range(1, groups, 2)]))
        return own, from_pair, from_ring, z_pair, z_ring

    field, *layers, weights, order, scalars, factors = pl.pallas_call(
        functools.partial(start_kernel, groups, depth),
        out_shape=(field_shape,)
        + layer_shapes
        + (shape(len(TILES), 6 * LANES, 2 * LANES, dtype=BF16), shape(512, 512, dtype=BF16))
        + (pltpu.SMEM((SCALARS,), jnp.int32), pltpu.SMEM((2 * FACES,), F32)),
        in_specs=[away] * 4,
        out_specs=(vmem,) * 8 + (smem,) * 2,
        scratch_shapes=[
            pltpu.SMEM(patch_sizes.shape, jnp.int32),
            pltpu.SMEM(partners.shape, jnp.int32),
            pltpu.SMEM(lame.shape, F32),
            pltpu.VMEM(displacement.shape, F32),
            pltpu.SemaphoreType.DMA((COMPS + 3,)),
        ],
        compiler_params=params(24),
        name="start_layers",
    )(far(patch_sizes), far(partners), far(lame), far(displacement))

    def volume(values, with_output):
        out_shape = (field_shape,)
        scratch = [pltpu.VMEM((9, PAD + 6, depth, LANES), F32)]
        if with_output:
            out_shape = out_shape + (jax.ShapeDtypeStruct(displacement.shape, F32),)
            scratch = scratch + [
                pltpu.VMEM(displacement.shape, F32),
                pltpu.SemaphoreType.DMA((PAD // XBLOCK,)),
            ]
        return pl.pallas_call(
            functools.partial(volume_kernel, depth),
            out_shape=out_shape,
            in_specs=[vmem] * 3,
            out_specs=(vmem, away)[: len(out_shape)],
            scratch_shapes=scratch,
            compiler_params=params(28),
            cost_estimate=pl.CostEstimate(flops=10**10, bytes_accessed=8 * 10**6, transcendentals=0),
            name="volume_and_output" if with_output else "volume_terms",
        )(near(values), z_table, near(weights))

    def finish(volume_part, exchanged, last):
        scratch = [pltpu.VMEM((9 * EDGE_X * 8, LANES), F32)]
        if last:
            out_shape = (field_shape, jax.ShapeDtypeStruct(displacement.shape, F32))
            out_specs = (vmem, away)
            scratch = scratch + [
                pltpu.VMEM(displacement.shape, F32),
                pltpu.SemaphoreType.DMA((OUT_PARTS,)),
            ]
        else:
            out_shape = (field_shape,) + layer_shapes
            out_specs = (vmem,) * 6
        return pl.pallas_call(
            functools.partial(finish_kernel, depth, last),
            out_shape=out_shape,
            in_specs=[smem] * 2 + [vmem] * 9,
            out_specs=out_specs,
            scratch_shapes=scratch,
            input_output_aliases={2: 0},
            compiler_params=params(28),
            name="finish_last" if last else "finish_first",
        )(
            scalar(scalars),
            scalar(factors),
            near(volume_part),
            *[near(part) for part in exchanged],
            transfer,
            near(weights),
            near(order),
        )

    (volume_part,) = volume(field, False)
    field, *next_layers = finish(volume_part, exchange(layers), False)
    volume_part, first_apply = volume(field, True)
    _, second_apply = finish(volume_part, exchange(next_layers), True)
    return first_apply, second_apply


def solution(mesh):
    return jax.shard_map(
        shards,
        mesh=mesh,
        in_specs=(
            P("patch", None, "sect", None),
            P(),
            P("patch", None),
            P("patch", None),
            P("patch", None, None, None),
        ),
        out_specs=(P("patch", None, "sect", None), P("patch", None, "sect", None)),
        check_vma=False,
    )
```

```python
import functools

import jax
import jax.numpy as jnp
import ml_dtypes
import numpy as np
from jax import lax
from jax.experimental import pallas as pl
from jax.experimental.pallas import tpu as pltpu
from jax.sharding import PartitionSpec as P

PAD = 64
LANES = 128
HALO = 3
COMPS = 3
MAXN = 61
FACES = 4
MASS_INT = (2416.0, 1191.0, 120.0, 1.0)
STIFF_INT = (80.0, -15.0, -24.0, -1.0)
SLOPE_INT = (245.0, 56.0, 1.0)
MASS_DEN = 5040.0
STIFF_DEN = 120.0
SLOPE_DEN = 720.0
PENALTY = 3.0
PAIRS = PAD // 2
KEEP = (MAXN + 1) // 2
KBLOCK = 16
KROWS = 8
MIB = 1024 * 1024
F32 = jnp.float32
BF16 = jnp.bfloat16


def split_np(table):
    high = table.astype(ml_dtypes.bfloat16)
    low = (table - high.astype(np.float64)).astype(ml_dtypes.bfloat16)
    return high, low


def band_np(size, kind):
    table = np.zeros((size, size))
    for i in range(size):
        for d in range(0, 4):
            for sign in (1, -1):
                j = i + sign * d
                if 0 <= j < size:
                    if kind == "slope":
                        if d:
                            table[i, j] = sign * SLOPE_INT[d - 1] / SLOPE_DEN
                    elif kind == "mass":
                        table[i, j] = MASS_INT[d] / MASS_DEN
                    else:
                        table[i, j] = STIFF_INT[d] / STIFF_DEN
    return table


def depth_table(depth):
    table = np.concatenate([band_np(depth, k) for k in ("mass", "stiff", "slope")], axis=0)
    high, low = split_np(table)
    return np.concatenate([high, high, low], axis=1)


def in_kernel_bands():
    rows = lax.broadcasted_iota(jnp.int32, (LANES, LANES), 0)
    cols = lax.broadcasted_iota(jnp.int32, (LANES, LANES), 1)
    ahead = jnp.where(rows // PAD == cols // PAD, rows - cols, PAD)
    apart = jnp.abs(ahead)
    mass = jnp.zeros((LANES, LANES), F32)
    stiff, slope = mass, mass
    for d in range(4):
        mass = jnp.where(apart == d, MASS_INT[d] / MASS_DEN, mass)
        stiff = jnp.where(apart == d, STIFF_INT[d] / STIFF_DEN, stiff)
        if d:
            slope = jnp.where(ahead == d, SLOPE_INT[d - 1] / SLOPE_DEN, slope)
            slope = jnp.where(ahead == -d, -SLOPE_INT[d - 1] / SLOPE_DEN, slope)
    return mass, stiff, slope


def layer_order():
    rows = lax.broadcasted_iota(jnp.int32, (512, 512), 0)
    cols = lax.broadcasted_iota(jnp.int32, (512, 512), 1)
    x = 8 * ((rows // 8) % 8) + 2 * (rows // 128) + (rows // 4) % 2
    patch_layer = 4 * ((rows // 64) % 2) + rows % 4
    return jnp.where(cols == patch_layer * 64 + x, 1.0, 0.0).astype(BF16)


def split(values):
    high = values.astype(BF16)
    low = (values - high.astype(F32)).astype(BF16)
    return high, low


def lane_iota(shape=(1, LANES)):
    return lax.broadcasted_iota(jnp.int32, shape, len(shape) - 1)


def swap_halves(values):
    return pltpu.roll(values, PAD, axis=values.ndim - 1)


def merge(low_half, high_half):
    return jnp.where(lane_iota() < PAD, low_half, high_half)


def dot(a, b):
    return jnp.dot(a, b, preferred_element_type=F32)


SIZES, SOURCES, SLOTS, SCALARS = 0, 4, 12, 20


def fill_scalars(sizes_ref, partners_ref, lame_ref, scalars, factors, me, groups):
    for p in range(2):
        for axis in range(2):
            scalars[SIZES + 2 * p + axis] = sizes_ref[p, axis]
    before = lax.rem(me + groups - 1, groups)
    pair_side = 1 - me % 2
    codes = [partners_ref[k // FACES, k % FACES] for k in range(2 * FACES)]
    ring = []
    for code in codes:
        side = jnp.where(code // (2 * FACES) == before, 0, 1)
        ring.append(jnp.where(side == pair_side, 0, 1))
    for k in range(2 * FACES):
        sent, read = jnp.int32(0), jnp.int32(0)
        for other in range(2 * FACES):
            if other != k:
                same = ring[other] == ring[k]
                sent = sent + jnp.where(same & (codes[other] < codes[k]), 1, 0)
                if other < k:
                    read = read + jnp.where(same, 1, 0)
        scalars[SOURCES + ring[k] * FACES + sent] = jnp.int32(k)
        scalars[SLOTS + k] = ring[k] * FACES + read
        p = k // FACES
        factors[k] = (PENALTY - 1.5) * (0.5 * (lame_ref[0, me * 2 + p] + lame_ref[0, codes[k] // FACES]))


def layer_select(scalars):
    rows = lax.broadcasted_iota(jnp.int32, (LANES, LANES), 0)
    cols = lax.broadcasted_iota(jnp.int32, (LANES, LANES), 1)
    layer = cols % 4
    size_y = jnp.where(cols < PAD, scalars[SIZES + 1], scalars[SIZES + 3])
    at = jnp.where(layer < 2, layer, size_y + 1 - layer)
    base = jnp.where(rows == ((cols // 4) % 2) * PAD + at, 1.0, 0.0)
    return [jnp.where(cols // 8 == j, base, 0.0).astype(BF16) for j in range(16)]


def row_of(p, c, k, depth):
    row = ((p * COMPS + c) * PAIRS + k) * depth
    return row if isinstance(row, int) else pl.multiple_of(row, depth)


def pair_at(field, p, k, depth):
    return jnp.concatenate([field[pl.ds(row_of(p, c, k, depth), depth), :] for c in range(COMPS)], axis=0)


def last_pairs(scalars, p):
    size = scalars[SIZES + 2 * p]
    return lax.div(size - 1, 2), lax.div(size - 2, 2), lax.rem(size, 2) == 0


def send_layers(field, scalars, order, own, to_pair, to_ring, z_pair, z_ring, depth):
    even_section = lax.axis_index("sect") % 2 == 0
    for p in range(2):
        for c in range(COMPS):
            for d in range(HALO):
                start = row_of(p, c, 0, depth)
                low = field[pl.ds(start + d, PAIRS, stride=depth), :]
                high = field[pl.ds(start + depth - HALO + d, PAIRS, stride=depth), :]
                z_pair[p, c, d] = jnp.where(even_section, high, low)
                z_ring[p, c, d] = jnp.where(even_section, low, high)
        own[p * FACES] = pair_at(field, p, 0, depth)
        outer_pair, inner_pair, same = last_pairs(scalars, p)
        outer, inner = pair_at(field, p, outer_pair, depth), pair_at(field, p, inner_pair, depth)
        own[p * FACES + 1] = jnp.where(same, swap_halves(outer), merge(outer, inner))
    select = jnp.concatenate(layer_select(scalars), axis=0)
    groups_rows = []
    for g in range(4):
        for c in range(COMPS):
            starts = [row_of(p, c, 4 * j + g, depth) for p in range(2) for j in range(8)]
            groups_rows.append(jnp.concatenate([field[start : start + depth, :] for start in starts], axis=1))
    rows = jnp.concatenate(groups_rows, axis=0)
    count = rows.shape[0]
    row_high, row_low = split(rows)
    picked = dot(jnp.concatenate([row_high, row_low], axis=0), select)
    picked = picked[:count] + picked[count:]
    per = COMPS * depth
    picked = jnp.concatenate([picked[g * per : (g + 1) * per] for g in range(4)], axis=1)
    pick_high, pick_low = split(picked)
    sorted_layers = dot(jnp.concatenate([pick_high, pick_low], axis=0), order[...])
    sorted_layers = sorted_layers[:per] + sorted_layers[per:]
    for p in range(2):
        for f in range(2):
            at = (p * 2 + f) * LANES
            own[p * FACES + 2 + f] = sorted_layers[:, at : at + LANES]
    for slot in range(FACES):
        to_pair[slot] = own[scalars[SOURCES + slot]]
        to_ring[slot] = own[scalars[SOURCES + FACES + slot]]


def active_lanes(scalars, p):
    lane = lane_iota()
    in_y = (lane % PAD) < scalars[SIZES + 2 * p + 1]
    x_left = scalars[SIZES + 2 * p] - lane // PAD
    return lambda k: in_y & (x_left > 2 * k)


MASS, STIFF, SLOPE = 0, 1, 2
TILES = (
    (((0, MASS), (0, STIFF)), ((0, STIFF), (0, MASS))),
    (((1, MASS), (2, SLOPE)), ((0, SLOPE), (1, MASS))),
    (((1, MASS), (1, STIFF)), ((1, STIFF), (1, MASS))),
    (((0, MASS), None), ((1, SLOPE), None)),
    (((2, MASS), (2, STIFF)), ((2, STIFF), (2, MASS))),
    (((0, SLOPE), (1, SLOPE)), ((2, SLOPE), (2, MASS))),
)
TERMS = {
    ((0, MASS), (0, STIFF)): (MASS, "both"),
    ((0, MASS), (0, MASS)): (STIFF, "mu"),
    ((0, STIFF), (0, MASS)): (MASS, "mu"),
    ((1, MASS), (0, SLOPE)): (SLOPE, "grad"),
    ((2, SLOPE), (0, SLOPE)): (MASS, "grad"),
    ((1, MASS), (1, STIFF)): (MASS, "mu"),
    ((1, MASS), (1, MASS)): (STIFF, "both"),
    ((1, STIFF), (1, MASS)): (MASS, "mu"),
    ((2, SLOPE), (1, MASS)): (SLOPE, "grad"),
    ((0, MASS), (1, SLOPE)): (SLOPE, "grad"),
    ((2, MASS), (2, STIFF)): (MASS, "mu"),
    ((2, MASS), (2, MASS)): (STIFF, "mu"),
    ((2, STIFF), (2, MASS)): (MASS, "both"),
    ((1, SLOPE), (2, MASS)): (SLOPE, "grad"),
    ((0, SLOPE), (2, SLOPE)): (MASS, "grad"),
}
OUT_SCALE = {STIFF: 1.0 / STIFF_DEN, MASS: 1.0 / MASS_DEN, SLOPE: 1.0 / SLOPE_DEN}


def fill_weights(lame_ref, me, weights):
    tables = in_kernel_bands()
    for p in range(2):
        mu = lame_ref[0, me * 2 + p]
        grad = mu + lame_ref[1, me * 2 + p]
        factors = {"mu": mu, "both": mu + grad, "grad": -grad}
        placed = set()
        for t, (sources, targets) in enumerate(TILES):
            for i, source in enumerate(sources):
                for o, target in enumerate(targets):
                    term = TERMS.get((source, target))
                    if term is None or (source, target) in placed:
                        block = jnp.zeros((LANES, LANES), F32)
                    else:
                        placed.add((source, target))
                        block = tables[term[0]] * (factors[term[1]] * OUT_SCALE[target[1]])
                    block_high, block_low = split(block)
                    cols = slice(o * LANES, (o + 1) * LANES)
                    for part, piece in enumerate((block_high, block_high, block_low)):
                        at = part * 2 * LANES + i * LANES
                        weights[p * len(TILES) + t, at : at + LANES, cols] = piece


def start_kernel(
    groups, depth, sizes_any, partners_any, lame_any, disp_any,
    field, own, to_pair, to_ring, z_pair, z_ring, weights, order, scalars, factors,
    sizes_ref, partners_ref, lame_ref, disp, sems,
):
    copies = []
    for c in range(COMPS):
        copies.append(pltpu.make_async_copy(disp_any.at[:, c], disp.at[:, c], sems.at[c]))
    small = [
        pltpu.make_async_copy(sizes_any, sizes_ref, sems.at[COMPS]),
        pltpu.make_async_copy(partners_any, partners_ref, sems.at[COMPS + 1]),
        pltpu.make_async_copy(lame_any, lame_ref, sems.at[COMPS + 2]),
    ]
    for copy in small + copies:
        copy.start()
    order[...] = layer_order()
    for copy in small:
        copy.wait()
    me = lax.axis_index("patch")
    fill_scalars(sizes_ref, partners_ref, lame_ref, scalars, factors, me, groups)
    fill_weights(lame_ref, me, weights)
    keeps = [active_lanes(scalars, p) for p in range(2)]
    for c in range(COMPS):
        copies[c].wait()
        for p in range(2):
            for k in range(PAIRS):
                start = row_of(p, c, k, depth)
                value = disp[p, c, :, k * LANES : (k + 1) * LANES]
                field[start : start + depth, :] = jnp.where(keeps[p](k), value, 0.0)
    send_layers(field, scalars, order, own, to_pair, to_ring, z_pair, z_ring, depth)


def plane_sums(fields, weights, p, complete=None):
    sums = {}
    for t, (sources, targets) in enumerate(TILES):
        if sources[1] is None:
            high, low = fields[sources[0]]
            weight = jnp.concatenate(
                [weights[p * len(TILES) + t, part * 2 * LANES : part * 2 * LANES + LANES, :LANES] for part in range(3)],
                axis=0,
            )
        else:
            high, low = [jnp.concatenate([fields[s][part] for s in sources], axis=1) for part in range(2)]
            weight = weights[p * len(TILES) + t]
        out = dot(jnp.concatenate([high, low, high], axis=1), weight)
        for o, target in enumerate(targets):
            if target is not None:
                piece = out[:, o * LANES : (o + 1) * LANES]
                sums[target] = piece if target not in sums else sums[target] + piece
        if complete is not None and t % 2 == 1:
            complete(t // 2, [sums[(t // 2, kind)] for kind in range(3)])
    return sums


def band_x(stiff, mass, slope, count):
    def at(values, d, extra=0):
        return values[2 + d : 2 + d + count + extra]

    total = STIFF_INT[0] * at(stiff, 0) + MASS_INT[0] * at(mass, 0)
    total = total + STIFF_INT[2] * (at(stiff, 1) + at(stiff, -1))
    total = total + MASS_INT[2] * (at(mass, 1) + at(mass, -1))
    total = total + SLOPE_INT[1] * (at(slope, 1) - at(slope, -1))
    odd = STIFF_INT[1] * (at(stiff, 0, 1) + at(stiff, -1, 1))
    odd = odd + MASS_INT[1] * (at(mass, 0, 1) + at(mass, -1, 1))
    odd = odd + SLOPE_INT[0] * (at(slope, 0, 1) - at(slope, -1, 1))
    odd = odd + ((at(mass, 1, 1) + at(mass, -2, 1)) - (at(stiff, 1, 1) + at(stiff, -2, 1)))
    odd = odd + (at(slope, 1, 1) - at(slope, -2, 1))
    return total + swap_halves(merge(odd[1:], odd[:-1]))


def send_output(result, result_any, sems, part, parts):
    lanes = pl.ds(part * (PAD * PAD // parts), PAD * PAD // parts)
    copy = pltpu.make_async_copy(result.at[:, :, :, lanes], result_any.at[:, :, :, lanes], sems.at[part])
    copy.start()
    return copy


OUT_PARTS = 4
SUMS = (18, KEEP + 4)


def volume_kernel(depth, field, z_table, weights, *rest):
    copy = None
    if len(rest) == 2:
        out, sums_ref = rest
    else:
        finished, out, finished_any, sums_ref, sem = rest
        copy = pltpu.make_async_copy(finished, finished_any, sem)
        copy.start()
    for i in range(18):
        for k in (0, 1, KEEP + 2, KEEP + 3):
            sums_ref[i, k] = jnp.zeros((depth, LANES), F32)

    def along_z(p, k0, count):
        fields = {}
        for c in range(COMPS):
            starts = [row_of(p, c, k0 + j, depth) for j in range(count)]
            rows = [field[start : start + depth, :] for start in starts]
            high, low = split(jnp.concatenate(rows, axis=1))
            banded = dot(z_table[...], jnp.concatenate([high, low, high], axis=0))
            parts = split(banded)
            for kind in range(3):
                fields[(c, kind)] = tuple(
                    jnp.concatenate(
                        [
                            part[kind * depth : (kind + 1) * depth, j * LANES : (j + 1) * LANES]
                            for j in range(count)
                        ],
                        axis=0,
                    )
                    for part in parts
                )
        return fields

    def along_x(p, k0, count, c, z0):
        held = [sums_ref[p * 9 + c * 3 + kind, k0 : k0 + count + 4, z0 : z0 + 8, :] for kind in range(3)]
        total = band_x(held[STIFF], held[MASS], held[SLOPE], count)
        for j in range(count):
            start = row_of(p, c, k0 + j, depth) + z0
            out[start : start + 8, :] = total[j]

    blocks = [(p, k0, min(KBLOCK, KEEP - k0)) for p in range(2) for k0 in range(0, KEEP, KBLOCK)]
    done = [0, 0]
    ahead = along_z(*blocks[0])
    for i, (p, k0, count) in enumerate(blocks):
        fields = ahead
        if i + 1 < len(blocks):
            ahead = along_z(*blocks[i + 1])
        ready = KEEP if k0 + count == KEEP else k0 + count - 2
        first = done[p]
        while done[p] < KEEP and min(done[p] + KROWS, KEEP) <= ready:
            done[p] = min(done[p] + KROWS, KEEP)

        def complete(c, values):
            for kind in range(3):
                sums_ref[p * 9 + c * 3 + kind, k0 + 2 : k0 + 2 + count] = values[kind].reshape(count, depth, LANES)
            for k in range(first, done[p], KROWS):
                for z0 in range(0, depth, 8):
                    along_x(p, k, min(KROWS, KEEP - k), c, z0)

        plane_sums(fields, weights, p, complete)
    if copy is not None:
        copy.wait()


def depth_edges(before, after):
    mass, stiff, slope = [], [], []
    for table, den, out, sign in (
        (MASS_INT[1:], MASS_DEN, mass, 1.0),
        (STIFF_INT[1:], STIFF_DEN, stiff, 1.0),
        (SLOPE_INT, SLOPE_DEN, slope, -1.0),
    ):
        coef = [value / den for value in table]
        for z in range(3):
            total = None
            for d in range(z + 1, 4):
                piece = (sign * coef[d - 1]) * before[3 + z - d]
                total = piece if total is None else total + piece
            out.append(total)
        for z in range(3):
            total = None
            for d in range(3 - z, 4):
                piece = coef[d - 1] * after[z + d - 3]
                total = piece if total is None else total + piece
            out.append(total)
    return [jnp.concatenate(parts, axis=0) for parts in (mass, stiff, slope)]


EDGE_K = PAIRS + 4


def finish_kernel(
    depth, last, scalars, factors, volume, own, from_pair, from_ring, z_pair, z_ring, transfer, weights, order,
    field, *rest,
):
    if last:
        result_any, edge, result, sems = rest
    else:
        *sends, result, edge = rest
    even_section = lax.axis_index("sect") % 2 == 0
    terms = []
    for k in range(2 * FACES):
        slot = scalars[SLOTS + k]
        far = jnp.where(slot < FACES, from_pair[lax.rem(slot, FACES)], from_ring[lax.rem(slot, FACES)])
        mat = transfer[k // FACES, k % FACES]
        zero = jnp.zeros((PAD, PAD), F32)
        both = jnp.concatenate(
            [jnp.concatenate([mat, zero], axis=1), jnp.concatenate([zero, mat], axis=1)], axis=0
        )
        far_high, far_low = split(far)
        mat_high, mat_low = split(both)
        moved = lax.dot_general(
            jnp.concatenate([far_high, far_low, far_high], axis=1),
            jnp.concatenate([mat_high, mat_high, mat_low], axis=1),
            (((1,), (1,)), ((), ())),
            preferred_element_type=F32,
        )
        terms.append(factors[k] * (own[k] - moved))
    for p in range(2):
        fields = {}
        for c in range(COMPS):
            before = [jnp.where(even_section, z_ring[p, c, d], z_pair[p, c, d]) for d in range(HALO)]
            after = [jnp.where(even_section, z_pair[p, c, d], z_ring[p, c, d]) for d in range(HALO)]
            banded = depth_edges(before, after)
            for kind in range(3):
                fields[(c, kind)] = split(banded[kind])
        sums = plane_sums(fields, weights, p)
        for (c, kind), value in sums.items():
            base = (p * 9 + c * 3 + kind) * EDGE_K * 8
            edge[base : base + 16, :] = jnp.zeros((16, LANES), F32)
            edge[base + (2 + PAIRS) * 8 : base + EDGE_K * 8, :] = jnp.zeros((16, LANES), F32)
            for z in range(2 * HALO):
                slot = z if z < HALO else z + 2
                edge[pl.ds(base + 16 + slot, PAIRS, stride=8), :] = value[z * PAIRS : (z + 1) * PAIRS]
    per = COMPS * depth
    stacked = jnp.concatenate([swap_halves(terms[p * FACES + 2 + f]) for p in range(2) for f in range(2)], axis=1)
    term_high, term_low = split(stacked)
    placed = lax.dot_general(
        jnp.concatenate([term_high, term_low], axis=0),
        order[...],
        (((1,), (1,)), ((), ())),
        preferred_element_type=F32,
    )
    placed = placed[:per] + placed[per:]
    placed = jnp.concatenate([placed[:, g * LANES : (g + 1) * LANES] for g in range(4)], axis=0)
    placed_parts = jnp.concatenate(split(placed), axis=1)
    select = layer_select(scalars)

    def add_pair(p, k, addend):
        for c in range(COMPS):
            field[pl.ds(row_of(p, c, k, depth), depth), :] += addend[c * depth : (c + 1) * depth]

    zero = jnp.zeros((per, LANES), F32)
    for p in range(2):
        add_pair(p, 0, swap_halves(terms[p * FACES]))
        outer_pair, inner_pair, same = last_pairs(scalars, p)
        term = terms[p * FACES + 1]
        add_pair(p, outer_pair, jnp.where(same, term, merge(swap_halves(term), zero)))
        add_pair(p, inner_pair, jnp.where(same, zero, merge(zero, swap_halves(term))))
    keeps = [active_lanes(scalars, p) for p in range(2)]
    slot_rows = lax.broadcasted_iota(jnp.int32, (8, LANES), 0)
    copies = []
    for j in range(8):
        both = jnp.concatenate([select[j], select[8 + j]], axis=0)
        spread = lax.dot_general(
            placed_parts,
            jnp.concatenate([both, both], axis=1),
            (((1,), (1,)), ((), ())),
            preferred_element_type=F32,
        )
        for p in range(2):
            for c in range(COMPS):
                held = []
                for kind in range(3):
                    base = ((p * 9 + c * 3 + kind) * EDGE_K + 4 * j) * 8
                    held.append(edge[base : base + 64, :].reshape(8, 8, LANES))
                edges = band_x(held[STIFF], held[MASS], held[SLOPE], 4)
                for g in range(4):
                    k = 4 * j + g
                    start = row_of(p, c, k, depth)
                    row = (g * COMPS + c) * depth
                    value = field[start : start + depth, :] + spread[row : row + depth, p * LANES : (p + 1) * LANES]
                    value = jnp.concatenate(
                        [
                            value[:8] + jnp.where(slot_rows < HALO, edges[g], 0.0),
                            value[8 : depth - 8],
                            value[depth - 8 :] + jnp.where(slot_rows >= 8 - HALO, edges[g], 0.0),
                        ],
                        axis=0,
                    )
                    value = jnp.where(keeps[p](k), value, 0.0)
                    result[p, c, :, k * LANES : (k + 1) * LANES] = value
                    if not last:
                        field[start : start + depth, :] = value
        if last and (j + 1) % (8 // OUT_PARTS) == 0:
            copies.append(send_output(result, result_any, sems, j // (8 // OUT_PARTS), OUT_PARTS))
    if not last:
        send_layers(field, scalars, order, *sends, depth)
    for copy in copies:
        copy.wait()


def shards(displacement, lame_params, patch_sizes, partners, transfer):
    depth = displacement.shape[2]
    groups = lax.axis_size("patch")
    sections = lax.axis_size("sect")
    rows = 2 * COMPS * PAIRS * depth
    per = COMPS * depth
    smem = pl.BlockSpec(memory_space=pltpu.SMEM)
    vmem = pl.BlockSpec(memory_space=pltpu.VMEM)
    away = pl.BlockSpec(memory_space=pl.ANY)
    z_table = jnp.asarray(depth_table(depth))
    lame = lame_params.T

    def shape(*dims, dtype=F32):
        return pltpu.VMEM(dims, dtype)

    def near(values):
        return pltpu.with_memory_space_constraint(values, pltpu.VMEM)

    def scalar(values):
        return pltpu.with_memory_space_constraint(values, pltpu.SMEM)

    def far(values):
        return pltpu.with_memory_space_constraint(values, pltpu.HBM)

    def params(mib):
        return pltpu.CompilerParams(vmem_limit_bytes=mib * MIB)

    field_shape = shape(rows, LANES)
    layer_shapes = (
        shape(2 * FACES, per, LANES),
        shape(FACES, per, LANES),
        shape(FACES, per, LANES),
        shape(2, COMPS, HALO, PAIRS, LANES),
        shape(2, COMPS, HALO, PAIRS, LANES),
    )

    def both_ways(pairs):
        return pairs + [(j, i) for i, j in pairs]

    def exchange(layers):
        own, to_pair, to_ring, z_pair, z_ring = layers
        z_pair = lax.ppermute(z_pair, "sect", both_ways([(i, i + 1) for i in range(0, sections - 1, 2)]))
        z_ring = lax.ppermute(z_ring, "sect", both_ways([(i, i + 1) for i in range(1, sections - 1, 2)]))
        from_pair = lax.ppermute(to_pair, "patch", both_ways([(i, i + 1) for i in range(0, groups, 2)]))
        from_ring = lax.ppermute(to_ring, "patch", both_ways([(i, (i + 1) % groups) for i in range(1, groups, 2)]))
        return own, from_pair, from_ring, z_pair, z_ring

    field, *layers, weights, order, scalars, factors = pl.pallas_call(
        functools.partial(start_kernel, groups, depth),
        out_shape=(field_shape,)
        + layer_shapes
        + (shape(2 * len(TILES), 6 * LANES, 2 * LANES, dtype=BF16), shape(512, 512, dtype=BF16))
        + (pltpu.SMEM((SCALARS,), jnp.int32), pltpu.SMEM((2 * FACES,), F32)),
        in_specs=[away] * 4,
        out_specs=(vmem,) * 8 + (smem,) * 2,
        scratch_shapes=[
            pltpu.SMEM(patch_sizes.shape, jnp.int32),
            pltpu.SMEM(partners.shape, jnp.int32),
            pltpu.SMEM(lame.shape, F32),
            pltpu.VMEM(displacement.shape, F32),
            pltpu.SemaphoreType.DMA((COMPS + 3,)),
        ],
        compiler_params=params(24),
        name="start_layers",
    )(far(patch_sizes), far(partners), far(lame), far(displacement))

    def volume(values, finished=None):
        out_shape = (field_shape,)
        operands = (near(values), z_table, near(weights))
        scratch = [pltpu.VMEM(SUMS + (depth, LANES), F32)]
        if finished is not None:
            out_shape = out_shape + (jax.ShapeDtypeStruct(displacement.shape, F32),)
            operands = operands + (near(finished),)
            scratch = scratch + [pltpu.SemaphoreType.DMA(())]
        return pl.pallas_call(
            functools.partial(volume_kernel, depth),
            out_shape=out_shape,
            in_specs=[vmem] * len(operands),
            out_specs=(vmem, away)[: len(out_shape)],
            scratch_shapes=scratch,
            compiler_params=params(30),
            cost_estimate=pl.CostEstimate(flops=10**10, bytes_accessed=8 * 10**6, transcendentals=0),
            name="volume_terms" if finished is None else "volume_and_output",
        )(*operands)

    def finish(volume_part, exchanged, last):
        scratch = [pltpu.VMEM((18 * EDGE_K * 8, LANES), F32)]
        if last:
            out_shape = (field_shape, jax.ShapeDtypeStruct(displacement.shape, F32))
            out_specs = (vmem, away)
            scratch = scratch + [
                pltpu.VMEM(displacement.shape, F32),
                pltpu.SemaphoreType.DMA((OUT_PARTS,)),
            ]
        else:
            out_shape = (field_shape,) + layer_shapes + (shape(*displacement.shape),)
            out_specs = (vmem,) * 7
        return pl.pallas_call(
            functools.partial(finish_kernel, depth, last),
            out_shape=out_shape,
            in_specs=[smem] * 2 + [vmem] * 9,
            out_specs=out_specs,
            scratch_shapes=scratch,
            input_output_aliases={2: 0},
            compiler_params=params(30),
            name="finish_last" if last else "finish_first",
        )(
            scalar(scalars),
            scalar(factors),
            near(volume_part),
            *[near(part) for part in exchanged],
            transfer,
            near(weights),
            near(order),
        )

    (volume_part,) = volume(field)
    field, *next_layers, finished = finish(volume_part, exchange(layers), False)
    volume_part, first_apply = volume(field, finished)
    _, second_apply = finish(volume_part, exchange(next_layers), True)
    return first_apply, second_apply


def solution(mesh):
    return jax.shard_map(
        shards,
        mesh=mesh,
        in_specs=(
            P("patch", None, "sect", None),
            P(),
            P("patch", None),
            P("patch", None),
            P("patch", None, None, None),
        ),
        out_specs=(P("patch", None, "sect", None), P("patch", None, "sect", None)),
        check_vma=False,
    )
```

```python
import functools

import jax
import jax.numpy as jnp
import ml_dtypes
import numpy as np
from jax import lax
from jax.experimental import pallas as pl
from jax.experimental.pallas import tpu as pltpu
from jax.sharding import PartitionSpec as P

PAD = 64
LANES = 128
HALO = 3
COMPS = 3
MAXN = 61
FACES = 4
MASS_INT = (2416.0, 1191.0, 120.0, 1.0)
STIFF_INT = (80.0, -15.0, -24.0, -1.0)
SLOPE_INT = (245.0, 56.0, 1.0)
MASS_DEN = 5040.0
STIFF_DEN = 120.0
SLOPE_DEN = 720.0
PENALTY = 3.0
PAIRS = PAD // 2
KEEP = (MAXN + 1) // 2
KBLOCK = 16
KROWS = 8
MIB = 1024 * 1024
F32 = jnp.float32
BF16 = jnp.bfloat16


def split_np(table):
    high = table.astype(ml_dtypes.bfloat16)
    low = (table - high.astype(np.float64)).astype(ml_dtypes.bfloat16)
    return high, low


def band_np(size, kind):
    table = np.zeros((size, size))
    for i in range(size):
        for d in range(0, 4):
            for sign in (1, -1):
                j = i + sign * d
                if 0 <= j < size:
                    if kind == "slope":
                        if d:
                            table[i, j] = sign * SLOPE_INT[d - 1] / SLOPE_DEN
                    elif kind == "mass":
                        table[i, j] = MASS_INT[d] / MASS_DEN
                    else:
                        table[i, j] = STIFF_INT[d] / STIFF_DEN
    return table


def depth_table(depth):
    table = np.concatenate([band_np(depth, k) for k in ("mass", "stiff", "slope")], axis=0)
    high, low = split_np(table)
    return np.concatenate([high, high, low], axis=1)


def in_kernel_bands():
    rows = lax.broadcasted_iota(jnp.int32, (LANES, LANES), 0)
    cols = lax.broadcasted_iota(jnp.int32, (LANES, LANES), 1)
    ahead = jnp.where(rows // PAD == cols // PAD, rows - cols, PAD)
    apart = jnp.abs(ahead)
    mass = jnp.zeros((LANES, LANES), F32)
    stiff, slope = mass, mass
    for d in range(4):
        mass = jnp.where(apart == d, MASS_INT[d] / MASS_DEN, mass)
        stiff = jnp.where(apart == d, STIFF_INT[d] / STIFF_DEN, stiff)
        if d:
            slope = jnp.where(ahead == d, SLOPE_INT[d - 1] / SLOPE_DEN, slope)
            slope = jnp.where(ahead == -d, -SLOPE_INT[d - 1] / SLOPE_DEN, slope)
    return mass, stiff, slope


def layer_order():
    rows = lax.broadcasted_iota(jnp.int32, (512, 512), 0)
    cols = lax.broadcasted_iota(jnp.int32, (512, 512), 1)
    x = 8 * ((rows // 8) % 8) + 2 * (rows // 128) + (rows // 4) % 2
    patch_layer = 4 * ((rows // 64) % 2) + rows % 4
    return jnp.where(cols == patch_layer * 64 + x, 1.0, 0.0).astype(BF16)


def split(values):
    high = values.astype(BF16)
    low = (values - high.astype(F32)).astype(BF16)
    return high, low


def lane_iota(shape=(1, LANES)):
    return lax.broadcasted_iota(jnp.int32, shape, len(shape) - 1)


def swap_halves(values):
    return pltpu.roll(values, PAD, axis=values.ndim - 1)


def merge(low_half, high_half):
    return jnp.where(lane_iota() < PAD, low_half, high_half)


def dot(a, b):
    return jnp.dot(a, b, preferred_element_type=F32)


SIZES, SOURCES, SLOTS, SCALARS = 0, 4, 12, 20


def fill_scalars(sizes_ref, partners_ref, lame_ref, scalars, factors, me, groups):
    for p in range(2):
        for axis in range(2):
            scalars[SIZES + 2 * p + axis] = sizes_ref[p, axis]
    before = lax.rem(me + groups - 1, groups)
    pair_side = 1 - me % 2
    codes = [partners_ref[k // FACES, k % FACES] for k in range(2 * FACES)]
    ring = []
    for code in codes:
        side = jnp.where(code // (2 * FACES) == before, 0, 1)
        ring.append(jnp.where(side == pair_side, 0, 1))
    for k in range(2 * FACES):
        sent, read = jnp.int32(0), jnp.int32(0)
        for other in range(2 * FACES):
            if other != k:
                same = ring[other] == ring[k]
                sent = sent + jnp.where(same & (codes[other] < codes[k]), 1, 0)
                if other < k:
                    read = read + jnp.where(same, 1, 0)
        scalars[SOURCES + ring[k] * FACES + sent] = jnp.int32(k)
        scalars[SLOTS + k] = ring[k] * FACES + read
        p = k // FACES
        factors[k] = (PENALTY - 1.5) * (0.5 * (lame_ref[0, me * 2 + p] + lame_ref[0, codes[k] // FACES]))


def layer_select(scalars):
    rows = lax.broadcasted_iota(jnp.int32, (LANES, LANES), 0)
    cols = lax.broadcasted_iota(jnp.int32, (LANES, LANES), 1)
    layer = cols % 4
    size_y = jnp.where(cols < PAD, scalars[SIZES + 1], scalars[SIZES + 3])
    at = jnp.where(layer < 2, layer, size_y + 1 - layer)
    base = jnp.where(rows == ((cols // 4) % 2) * PAD + at, 1.0, 0.0)
    return [jnp.where(cols // 8 == j, base, 0.0).astype(BF16) for j in range(16)]


def row_of(p, c, k, depth):
    row = ((p * COMPS + c) * PAIRS + k) * depth
    return row if isinstance(row, int) else pl.multiple_of(row, depth)


def pair_at(field, p, k, depth):
    return jnp.concatenate([field[pl.ds(row_of(p, c, k, depth), depth), :] for c in range(COMPS)], axis=0)


def last_pairs(scalars, p):
    size = scalars[SIZES + 2 * p]
    return lax.div(size - 1, 2), lax.div(size - 2, 2), lax.rem(size, 2) == 0


def send_layers(field, scalars, order, own, to_pair, to_ring, z_pair, z_ring, depth):
    even_section = lax.axis_index("sect") % 2 == 0
    for p in range(2):
        for c in range(COMPS):
            for d in range(HALO):
                start = row_of(p, c, 0, depth)
                low = field[pl.ds(start + d, PAIRS, stride=depth), :]
                high = field[pl.ds(start + depth - HALO + d, PAIRS, stride=depth), :]
                z_pair[p, c, d] = jnp.where(even_section, high, low)
                z_ring[p, c, d] = jnp.where(even_section, low, high)
        own[p * FACES] = pair_at(field, p, 0, depth)
        outer_pair, inner_pair, same = last_pairs(scalars, p)
        outer, inner = pair_at(field, p, outer_pair, depth), pair_at(field, p, inner_pair, depth)
        own[p * FACES + 1] = jnp.where(same, swap_halves(outer), merge(outer, inner))
    select = jnp.concatenate(layer_select(scalars), axis=0)
    groups_rows = []
    for g in range(4):
        for c in range(COMPS):
            starts = [row_of(p, c, 4 * j + g, depth) for p in range(2) for j in range(8)]
            groups_rows.append(jnp.concatenate([field[start : start + depth, :] for start in starts], axis=1))
    rows = jnp.concatenate(groups_rows, axis=0)
    count = rows.shape[0]
    row_high, row_low = split(rows)
    picked = dot(jnp.concatenate([row_high, row_low], axis=0), select)
    picked = picked[:count] + picked[count:]
    per = COMPS * depth
    picked = jnp.concatenate([picked[g * per : (g + 1) * per] for g in range(4)], axis=1)
    pick_high, pick_low = split(picked)
    sorted_layers = dot(jnp.concatenate([pick_high, pick_low], axis=0), order[...])
    sorted_layers = sorted_layers[:per] + sorted_layers[per:]
    for p in range(2):
        for f in range(2):
            at = (p * 2 + f) * LANES
            own[p * FACES + 2 + f] = sorted_layers[:, at : at + LANES]
    for slot in range(FACES):
        to_pair[slot] = own[scalars[SOURCES + slot]]
        to_ring[slot] = own[scalars[SOURCES + FACES + slot]]


def active_lanes(scalars, p):
    lane = lane_iota()
    in_y = (lane % PAD) < scalars[SIZES + 2 * p + 1]
    x_left = scalars[SIZES + 2 * p] - lane // PAD
    return lambda k: in_y & (x_left > 2 * k)


MASS, STIFF, SLOPE = 0, 1, 2
TILES = (
    (((0, MASS), (0, STIFF)), ((0, STIFF), (0, MASS))),
    (((1, MASS), (2, SLOPE)), ((0, SLOPE), (1, MASS))),
    (((1, MASS), (1, STIFF)), ((1, STIFF), (1, MASS))),
    (((0, MASS), None), ((1, SLOPE), None)),
    (((2, MASS), (2, STIFF)), ((2, STIFF), (2, MASS))),
    (((0, SLOPE), (1, SLOPE)), ((2, SLOPE), (2, MASS))),
)
TERMS = {
    ((0, MASS), (0, STIFF)): (MASS, "both"),
    ((0, MASS), (0, MASS)): (STIFF, "mu"),
    ((0, STIFF), (0, MASS)): (MASS, "mu"),
    ((1, MASS), (0, SLOPE)): (SLOPE, "grad"),
    ((2, SLOPE), (0, SLOPE)): (MASS, "grad"),
    ((1, MASS), (1, STIFF)): (MASS, "mu"),
    ((1, MASS), (1, MASS)): (STIFF, "both"),
    ((1, STIFF), (1, MASS)): (MASS, "mu"),
    ((2, SLOPE), (1, MASS)): (SLOPE, "grad"),
    ((0, MASS), (1, SLOPE)): (SLOPE, "grad"),
    ((2, MASS), (2, STIFF)): (MASS, "mu"),
    ((2, MASS), (2, MASS)): (STIFF, "mu"),
    ((2, STIFF), (2, MASS)): (MASS, "both"),
    ((1, SLOPE), (2, MASS)): (SLOPE, "grad"),
    ((0, SLOPE), (2, SLOPE)): (MASS, "grad"),
}
OUT_SCALE = {STIFF: 1.0 / STIFF_DEN, MASS: 1.0 / MASS_DEN, SLOPE: 1.0 / SLOPE_DEN}


def fill_weights(lame_ref, me, weights):
    tables = in_kernel_bands()
    for p in range(2):
        mu = lame_ref[0, me * 2 + p]
        grad = mu + lame_ref[1, me * 2 + p]
        factors = {"mu": mu, "both": mu + grad, "grad": -grad}
        placed = set()
        for t, (sources, targets) in enumerate(TILES):
            for i, source in enumerate(sources):
                for o, target in enumerate(targets):
                    term = TERMS.get((source, target))
                    if term is None or (source, target) in placed:
                        block = jnp.zeros((LANES, LANES), F32)
                    else:
                        placed.add((source, target))
                        block = tables[term[0]] * (factors[term[1]] * OUT_SCALE[target[1]])
                    block_high, block_low = split(block)
                    cols = slice(o * LANES, (o + 1) * LANES)
                    for part, piece in enumerate((block_high, block_high, block_low)):
                        at = part * 2 * LANES + i * LANES
                        weights[p * len(TILES) + t, at : at + LANES, cols] = piece


def start_kernel(
    groups, depth, sizes_any, partners_any, lame_any, disp_any,
    field, own, to_pair, to_ring, z_pair, z_ring, weights, order, scalars, factors,
    sizes_ref, partners_ref, lame_ref, disp, sems,
):
    copies = []
    for c in range(COMPS):
        copies.append(pltpu.make_async_copy(disp_any.at[:, c], disp.at[:, c], sems.at[c]))
    small = [
        pltpu.make_async_copy(sizes_any, sizes_ref, sems.at[COMPS]),
        pltpu.make_async_copy(partners_any, partners_ref, sems.at[COMPS + 1]),
        pltpu.make_async_copy(lame_any, lame_ref, sems.at[COMPS + 2]),
    ]
    for copy in small + copies:
        copy.start()
    order[...] = layer_order()
    for copy in small:
        copy.wait()
    me = lax.axis_index("patch")
    fill_scalars(sizes_ref, partners_ref, lame_ref, scalars, factors, me, groups)
    fill_weights(lame_ref, me, weights)
    keeps = [active_lanes(scalars, p) for p in range(2)]
    for c in range(COMPS):
        copies[c].wait()
        for p in range(2):
            for k in range(PAIRS):
                start = row_of(p, c, k, depth)
                value = disp[p, c, :, k * LANES : (k + 1) * LANES]
                field[start : start + depth, :] = jnp.where(keeps[p](k), value, 0.0)
    send_layers(field, scalars, order, own, to_pair, to_ring, z_pair, z_ring, depth)


def plane_sums(fields, weights, p, complete=None):
    sums = {}
    for t, (sources, targets) in enumerate(TILES):
        if sources[1] is None:
            high, low = fields[sources[0]]
            weight = jnp.concatenate(
                [weights[p * len(TILES) + t, part * 2 * LANES : part * 2 * LANES + LANES, :LANES] for part in range(3)],
                axis=0,
            )
        else:
            high, low = [jnp.concatenate([fields[s][part] for s in sources], axis=1) for part in range(2)]
            weight = weights[p * len(TILES) + t]
        out = dot(jnp.concatenate([high, low, high], axis=1), weight)
        for o, target in enumerate(targets):
            if target is not None:
                piece = out[:, o * LANES : (o + 1) * LANES]
                sums[target] = piece if target not in sums else sums[target] + piece
        if complete is not None and t % 2 == 1:
            complete(t // 2, [sums[(t // 2, kind)] for kind in range(3)])
    return sums


def band_x(stiff, mass, slope, count):
    def at(values, d, extra=0):
        return values[2 + d : 2 + d + count + extra]

    total = STIFF_INT[0] * at(stiff, 0) + MASS_INT[0] * at(mass, 0)
    total = total + STIFF_INT[2] * (at(stiff, 1) + at(stiff, -1))
    total = total + MASS_INT[2] * (at(mass, 1) + at(mass, -1))
    total = total + SLOPE_INT[1] * (at(slope, 1) - at(slope, -1))
    odd = STIFF_INT[1] * (at(stiff, 0, 1) + at(stiff, -1, 1))
    odd = odd + MASS_INT[1] * (at(mass, 0, 1) + at(mass, -1, 1))
    odd = odd + SLOPE_INT[0] * (at(slope, 0, 1) - at(slope, -1, 1))
    odd = odd + ((at(mass, 1, 1) + at(mass, -2, 1)) - (at(stiff, 1, 1) + at(stiff, -2, 1)))
    odd = odd + (at(slope, 1, 1) - at(slope, -2, 1))
    return total + swap_halves(merge(odd[1:], odd[:-1]))


def send_output(result, result_any, sems, part, parts):
    lanes = pl.ds(part * (PAD * PAD // parts), PAD * PAD // parts)
    copy = pltpu.make_async_copy(result.at[:, :, :, lanes], result_any.at[:, :, :, lanes], sems.at[part])
    copy.start()
    return copy


OUT_PARTS = 4
SUMS = (18, KEEP + 4)


def volume_kernel(depth, field, z_table, weights, *rest):
    copy = None
    if len(rest) == 2:
        out, sums_ref = rest
    else:
        finished, out, finished_any, sums_ref, sem = rest
        copy = pltpu.make_async_copy(finished, finished_any, sem)
        copy.start()
    for i in range(18):
        for k in (0, 1, KEEP + 2, KEEP + 3):
            sums_ref[i, k] = jnp.zeros((depth, LANES), F32)

    def along_z(p, k0, count):
        fields = {}
        for c in range(COMPS):
            starts = [row_of(p, c, k0 + j, depth) for j in range(count)]
            rows = [field[start : start + depth, :] for start in starts]
            high, low = split(jnp.concatenate(rows, axis=1))
            banded = dot(z_table[...], jnp.concatenate([high, low, high], axis=0))
            parts = split(banded)
            for kind in range(3):
                fields[(c, kind)] = tuple(
                    jnp.concatenate(
                        [
                            part[kind * depth : (kind + 1) * depth, j * LANES : (j + 1) * LANES]
                            for j in range(count)
                        ],
                        axis=0,
                    )
                    for part in parts
                )
        return fields

    def along_x(p, k0, count, c, z0):
        held = [sums_ref[p * 9 + c * 3 + kind, k0 : k0 + count + 4, z0 : z0 + 8, :] for kind in range(3)]
        total = band_x(held[STIFF], held[MASS], held[SLOPE], count)
        for j in range(count):
            start = row_of(p, c, k0 + j, depth) + z0
            out[start : start + 8, :] = total[j]

    blocks = [(p, k0, min(KBLOCK, KEEP - k0)) for p in range(2) for k0 in range(0, KEEP, KBLOCK)]
    done = [0, 0]
    ahead = along_z(*blocks[0])
    for i, (p, k0, count) in enumerate(blocks):
        fields = ahead
        if i + 1 < len(blocks):
            ahead = along_z(*blocks[i + 1])
        ready = KEEP if k0 + count == KEEP else k0 + count - 2
        first = done[p]
        while done[p] < KEEP and min(done[p] + KROWS, KEEP) <= ready:
            done[p] = min(done[p] + KROWS, KEEP)

        def complete(c, values):
            for kind in range(3):
                sums_ref[p * 9 + c * 3 + kind, k0 + 2 : k0 + 2 + count] = values[kind].reshape(count, depth, LANES)
            for k in range(first, done[p], KROWS):
                for z0 in range(0, depth, 8):
                    along_x(p, k, min(KROWS, KEEP - k), c, z0)

        plane_sums(fields, weights, p, complete)
    if copy is not None:
        copy.wait()


def depth_edges(before, after):
    mass, stiff, slope = [], [], []
    for table, den, out, sign in (
        (MASS_INT[1:], MASS_DEN, mass, 1.0),
        (STIFF_INT[1:], STIFF_DEN, stiff, 1.0),
        (SLOPE_INT, SLOPE_DEN, slope, -1.0),
    ):
        coef = [value / den for value in table]
        for z in range(3):
            total = None
            for d in range(z + 1, 4):
                piece = (sign * coef[d - 1]) * before[3 + z - d]
                total = piece if total is None else total + piece
            out.append(total)
        for z in range(3):
            total = None
            for d in range(3 - z, 4):
                piece = coef[d - 1] * after[z + d - 3]
                total = piece if total is None else total + piece
            out.append(total)
    return [jnp.concatenate(parts, axis=0) for parts in (mass, stiff, slope)]


EDGE_K = PAIRS + 4


def finish_kernel(
    depth, last, scalars, factors, volume, own, from_pair, z_ring, from_ring, z_pair, transfer, weights, order,
    field, *rest,
):
    if last:
        result_any, edge, result, sems = rest
    else:
        *sends, result, edge = rest
    section, sections = lax.axis_index("sect"), lax.axis_size("sect")
    even_section = section % 2 == 0
    terms = []
    for k in range(2 * FACES):
        slot = scalars[SLOTS + k]
        far = jnp.where(slot < FACES, from_pair[lax.rem(slot, FACES)], from_ring[lax.rem(slot, FACES)])
        mat = transfer[k // FACES, k % FACES]
        zero = jnp.zeros((PAD, PAD), F32)
        both = jnp.concatenate(
            [jnp.concatenate([mat, zero], axis=1), jnp.concatenate([zero, mat], axis=1)], axis=0
        )
        far_high, far_low = split(far)
        mat_high, mat_low = split(both)
        moved = lax.dot_general(
            jnp.concatenate([far_high, far_low, far_high], axis=1),
            jnp.concatenate([mat_high, mat_high, mat_low], axis=1),
            (((1,), (1,)), ((), ())),
            preferred_element_type=F32,
        )
        terms.append(factors[k] * (own[k] - moved))
    for p in range(2):
        fields = {}
        for c in range(COMPS):
            before, after = [], []
            for d in range(HALO):
                paired, ringed = z_pair[p, c, d], z_ring[p, c, d]
                before.append(jnp.where(section == 0, 0.0, jnp.where(even_section, ringed, paired)))
                after.append(jnp.where(section == sections - 1, 0.0, jnp.where(even_section, paired, ringed)))
            banded = depth_edges(before, after)
            for kind in range(3):
                fields[(c, kind)] = split(banded[kind])
        sums = plane_sums(fields, weights, p)
        for (c, kind), value in sums.items():
            base = (p * 9 + c * 3 + kind) * EDGE_K * 8
            edge[base : base + 16, :] = jnp.zeros((16, LANES), F32)
            edge[base + (2 + PAIRS) * 8 : base + EDGE_K * 8, :] = jnp.zeros((16, LANES), F32)
            for z in range(2 * HALO):
                slot = z if z < HALO else z + 2
                edge[pl.ds(base + 16 + slot, PAIRS, stride=8), :] = value[z * PAIRS : (z + 1) * PAIRS]
    per = COMPS * depth
    stacked = jnp.concatenate([swap_halves(terms[p * FACES + 2 + f]) for p in range(2) for f in range(2)], axis=1)
    term_high, term_low = split(stacked)
    placed = lax.dot_general(
        jnp.concatenate([term_high, term_low], axis=0),
        order[...],
        (((1,), (1,)), ((), ())),
        preferred_element_type=F32,
    )
    placed = placed[:per] + placed[per:]
    placed = jnp.concatenate([placed[:, g * LANES : (g + 1) * LANES] for g in range(4)], axis=0)
    placed_parts = jnp.concatenate(split(placed), axis=1)
    select = layer_select(scalars)

    def add_pair(p, k, addend):
        for c in range(COMPS):
            field[pl.ds(row_of(p, c, k, depth), depth), :] += addend[c * depth : (c + 1) * depth]

    zero = jnp.zeros((per, LANES), F32)
    for p in range(2):
        add_pair(p, 0, swap_halves(terms[p * FACES]))
        outer_pair, inner_pair, same = last_pairs(scalars, p)
        term = terms[p * FACES + 1]
        add_pair(p, outer_pair, jnp.where(same, term, merge(swap_halves(term), zero)))
        add_pair(p, inner_pair, jnp.where(same, zero, merge(zero, swap_halves(term))))
    keeps = [active_lanes(scalars, p) for p in range(2)]
    slot_rows = lax.broadcasted_iota(jnp.int32, (8, LANES), 0)
    copies = []
    for j in range(8):
        both = jnp.concatenate([select[j], select[8 + j]], axis=0)
        spread = lax.dot_general(
            placed_parts,
            jnp.concatenate([both, both], axis=1),
            (((1,), (1,)), ((), ())),
            preferred_element_type=F32,
        )
        for p in range(2):
            for c in range(COMPS):
                held = []
                for kind in range(3):
                    base = ((p * 9 + c * 3 + kind) * EDGE_K + 4 * j) * 8
                    held.append(edge[base : base + 64, :].reshape(8, 8, LANES))
                edges = band_x(held[STIFF], held[MASS], held[SLOPE], 4)
                for g in range(4):
                    k = 4 * j + g
                    start = row_of(p, c, k, depth)
                    row = (g * COMPS + c) * depth
                    value = field[start : start + depth, :] + spread[row : row + depth, p * LANES : (p + 1) * LANES]
                    value = jnp.concatenate(
                        [
                            value[:8] + jnp.where(slot_rows < HALO, edges[g], 0.0),
                            value[8 : depth - 8],
                            value[depth - 8 :] + jnp.where(slot_rows >= 8 - HALO, edges[g], 0.0),
                        ],
                        axis=0,
                    )
                    value = jnp.where(keeps[p](k), value, 0.0)
                    result[p, c, :, k * LANES : (k + 1) * LANES] = value
                    if not last:
                        field[start : start + depth, :] = value
        if last and (j + 1) % (8 // OUT_PARTS) == 0:
            copies.append(send_output(result, result_any, sems, j // (8 // OUT_PARTS), OUT_PARTS))
    if not last:
        send_layers(field, scalars, order, *sends, depth)
    for copy in copies:
        copy.wait()


def shards(displacement, lame_params, patch_sizes, partners, transfer):
    depth = displacement.shape[2]
    groups = lax.axis_size("patch")
    sections = lax.axis_size("sect")
    rows = 2 * COMPS * PAIRS * depth
    per = COMPS * depth
    smem = pl.BlockSpec(memory_space=pltpu.SMEM)
    vmem = pl.BlockSpec(memory_space=pltpu.VMEM)
    away = pl.BlockSpec(memory_space=pl.ANY)
    z_table = jnp.asarray(depth_table(depth))
    lame = lame_params.T

    def shape(*dims, dtype=F32):
        return pltpu.VMEM(dims, dtype)

    def near(values):
        return pltpu.with_memory_space_constraint(values, pltpu.VMEM)

    def scalar(values):
        return pltpu.with_memory_space_constraint(values, pltpu.SMEM)

    def far(values):
        return pltpu.with_memory_space_constraint(values, pltpu.HBM)

    def params(mib):
        return pltpu.CompilerParams(vmem_limit_bytes=mib * MIB)

    field_shape = shape(rows, LANES)
    layer_shapes = (
        shape(2 * FACES, per, LANES),
        shape(FACES, per, LANES),
        shape(FACES, per, LANES),
        shape(2, COMPS, HALO, PAIRS, LANES),
        shape(2, COMPS, HALO, PAIRS, LANES),
    )

    def both_ways(pairs):
        return pairs + [(j, i) for i, j in pairs]

    def exchange(layers):
        own, to_pair, to_ring, z_pair, z_ring = layers
        z_pair = lax.ppermute(z_pair, "sect", both_ways([(i, i + 1) for i in range(0, sections, 2)]))
        z_ring = lax.ppermute(z_ring, "sect", both_ways([(i, (i + 1) % sections) for i in range(1, sections, 2)]))
        from_pair = lax.ppermute(to_pair, "patch", both_ways([(i, i + 1) for i in range(0, groups, 2)]))
        from_ring = lax.ppermute(to_ring, "patch", both_ways([(i, (i + 1) % groups) for i in range(1, groups, 2)]))
        return own, from_pair, z_ring, from_ring, z_pair

    field, *layers, weights, order, scalars, factors = pl.pallas_call(
        functools.partial(start_kernel, groups, depth),
        out_shape=(field_shape,)
        + layer_shapes
        + (shape(2 * len(TILES), 6 * LANES, 2 * LANES, dtype=BF16), shape(512, 512, dtype=BF16))
        + (pltpu.SMEM((SCALARS,), jnp.int32), pltpu.SMEM((2 * FACES,), F32)),
        in_specs=[away] * 4,
        out_specs=(vmem,) * 8 + (smem,) * 2,
        scratch_shapes=[
            pltpu.SMEM(patch_sizes.shape, jnp.int32),
            pltpu.SMEM(partners.shape, jnp.int32),
            pltpu.SMEM(lame.shape, F32),
            pltpu.VMEM(displacement.shape, F32),
            pltpu.SemaphoreType.DMA((COMPS + 3,)),
        ],
        compiler_params=params(24),
        name="start_layers",
    )(far(patch_sizes), far(partners), far(lame), far(displacement))

    def volume(values, finished=None):
        out_shape = (field_shape,)
        operands = (near(values), z_table, near(weights))
        scratch = [pltpu.VMEM(SUMS + (depth, LANES), F32)]
        if finished is not None:
            out_shape = out_shape + (jax.ShapeDtypeStruct(displacement.shape, F32),)
            operands = operands + (near(finished),)
            scratch = scratch + [pltpu.SemaphoreType.DMA(())]
        return pl.pallas_call(
            functools.partial(volume_kernel, depth),
            out_shape=out_shape,
            in_specs=[vmem] * len(operands),
            out_specs=(vmem, away)[: len(out_shape)],
            scratch_shapes=scratch,
            compiler_params=params(30),
            cost_estimate=pl.CostEstimate(flops=10**10, bytes_accessed=8 * 10**6, transcendentals=0),
            name="volume_terms" if finished is None else "volume_and_output",
        )(*operands)

    def finish(volume_part, exchanged, last):
        scratch = [pltpu.VMEM((18 * EDGE_K * 8, LANES), F32)]
        if last:
            out_shape = (field_shape, jax.ShapeDtypeStruct(displacement.shape, F32))
            out_specs = (vmem, away)
            scratch = scratch + [
                pltpu.VMEM(displacement.shape, F32),
                pltpu.SemaphoreType.DMA((OUT_PARTS,)),
            ]
        else:
            out_shape = (field_shape,) + layer_shapes + (shape(*displacement.shape),)
            out_specs = (vmem,) * 7
        return pl.pallas_call(
            functools.partial(finish_kernel, depth, last),
            out_shape=out_shape,
            in_specs=[smem] * 2 + [vmem] * 9,
            out_specs=out_specs,
            scratch_shapes=scratch,
            input_output_aliases={2: 0},
            compiler_params=params(30),
            name="finish_last" if last else "finish_first",
        )(
            scalar(scalars),
            scalar(factors),
            near(volume_part),
            *[near(part) for part in exchanged],
            transfer,
            near(weights),
            near(order),
        )

    (volume_part,) = volume(field)
    field, *next_layers, finished = finish(volume_part, exchange(layers), False)
    volume_part, first_apply = volume(field, finished)
    _, second_apply = finish(volume_part, exchange(next_layers), True)
    return first_apply, second_apply


def solution(mesh):
    return jax.shard_map(
        shards,
        mesh=mesh,
        in_specs=(
            P("patch", None, "sect", None),
            P(),
            P("patch", None),
            P("patch", None),
            P("patch", None, None, None),
        ),
        out_specs=(P("patch", None, "sect", None), P("patch", None, "sect", None)),
        check_vma=False,
    )
```

```python
import functools

import jax
import jax.numpy as jnp
import ml_dtypes
import numpy as np
from jax import lax
from jax.experimental import pallas as pl
from jax.experimental.pallas import tpu as pltpu
from jax.sharding import PartitionSpec as P

PAD = 64
LANES = 128
HALO = 3
COMPS = 3
MAXN = 61
FACES = 4
MASS_INT = (2416.0, 1191.0, 120.0, 1.0)
STIFF_INT = (80.0, -15.0, -24.0, -1.0)
SLOPE_INT = (245.0, 56.0, 1.0)
MASS_DEN = 5040.0
STIFF_DEN = 120.0
SLOPE_DEN = 720.0
PENALTY = 3.0
PAIRS = PAD // 2
KEEP = (MAXN + 1) // 2
KBLOCK = 16
KROWS = 8
MIB = 1024 * 1024
F32 = jnp.float32
BF16 = jnp.bfloat16


def split_np(table):
    high = table.astype(ml_dtypes.bfloat16)
    low = (table - high.astype(np.float64)).astype(ml_dtypes.bfloat16)
    return high, low


def band_np(size, kind):
    table = np.zeros((size, size))
    for i in range(size):
        for d in range(0, 4):
            for sign in (1, -1):
                j = i + sign * d
                if 0 <= j < size:
                    if kind == "slope":
                        if d:
                            table[i, j] = sign * SLOPE_INT[d - 1] / SLOPE_DEN
                    elif kind == "mass":
                        table[i, j] = MASS_INT[d] / MASS_DEN
                    else:
                        table[i, j] = STIFF_INT[d] / STIFF_DEN
    return table


def depth_table(depth):
    table = np.concatenate([band_np(depth, k) for k in ("mass", "stiff", "slope")], axis=0)
    high, low = split_np(table)
    return np.concatenate([high, high, low], axis=1)


def in_kernel_bands():
    rows = lax.broadcasted_iota(jnp.int32, (LANES, LANES), 0)
    cols = lax.broadcasted_iota(jnp.int32, (LANES, LANES), 1)
    ahead = jnp.where(rows // PAD == cols // PAD, rows - cols, PAD)
    apart = jnp.abs(ahead)
    mass = jnp.zeros((LANES, LANES), F32)
    stiff, slope = mass, mass
    for d in range(4):
        mass = jnp.where(apart == d, MASS_INT[d] / MASS_DEN, mass)
        stiff = jnp.where(apart == d, STIFF_INT[d] / STIFF_DEN, stiff)
        if d:
            slope = jnp.where(ahead == d, SLOPE_INT[d - 1] / SLOPE_DEN, slope)
            slope = jnp.where(ahead == -d, -SLOPE_INT[d - 1] / SLOPE_DEN, slope)
    return mass, stiff, slope


def layer_order():
    rows = lax.broadcasted_iota(jnp.int32, (512, 512), 0)
    cols = lax.broadcasted_iota(jnp.int32, (512, 512), 1)
    x = 8 * ((rows // 8) % 8) + 2 * (rows // 128) + (rows // 4) % 2
    patch_layer = 4 * ((rows // 64) % 2) + rows % 4
    return jnp.where(cols == patch_layer * 64 + x, 1.0, 0.0).astype(BF16)


def split(values):
    high = values.astype(BF16)
    low = (values - high.astype(F32)).astype(BF16)
    return high, low


def lane_iota(shape=(1, LANES)):
    return lax.broadcasted_iota(jnp.int32, shape, len(shape) - 1)


def swap_halves(values):
    return pltpu.roll(values, PAD, axis=values.ndim - 1)


def merge(low_half, high_half):
    return jnp.where(lane_iota() < PAD, low_half, high_half)


def dot(a, b):
    return jnp.dot(a, b, preferred_element_type=F32)


SIZES, SOURCES, SLOTS, SCALARS = 0, 4, 12, 20


def fill_scalars(sizes_ref, partners_ref, lame_ref, scalars, factors, me, groups):
    for p in range(2):
        for axis in range(2):
            scalars[SIZES + 2 * p + axis] = sizes_ref[p, axis]
    before = lax.rem(me + groups - 1, groups)
    pair_side = 1 - me % 2
    codes = [partners_ref[k // FACES, k % FACES] for k in range(2 * FACES)]
    ring = []
    for code in codes:
        side = jnp.where(code // (2 * FACES) == before, 0, 1)
        ring.append(jnp.where(side == pair_side, 0, 1))
    for k in range(2 * FACES):
        sent, read = jnp.int32(0), jnp.int32(0)
        for other in range(2 * FACES):
            if other != k:
                same = ring[other] == ring[k]
                sent = sent + jnp.where(same & (codes[other] < codes[k]), 1, 0)
                if other < k:
                    read = read + jnp.where(same, 1, 0)
        scalars[SOURCES + ring[k] * FACES + sent] = jnp.int32(k)
        scalars[SLOTS + k] = ring[k] * FACES + read
        p = k // FACES
        factors[k] = (PENALTY - 1.5) * (0.5 * (lame_ref[0, me * 2 + p] + lame_ref[0, codes[k] // FACES]))


def layer_select(scalars):
    rows = lax.broadcasted_iota(jnp.int32, (LANES, LANES), 0)
    cols = lax.broadcasted_iota(jnp.int32, (LANES, LANES), 1)
    layer = cols % 4
    size_y = jnp.where(cols < PAD, scalars[SIZES + 1], scalars[SIZES + 3])
    at = jnp.where(layer < 2, layer, size_y + 1 - layer)
    base = jnp.where(rows == ((cols // 4) % 2) * PAD + at, 1.0, 0.0)
    return [jnp.where(cols // 8 == j, base, 0.0).astype(BF16) for j in range(16)]


def row_of(p, c, k, depth):
    row = ((p * COMPS + c) * PAIRS + k) * depth
    return row if isinstance(row, int) else pl.multiple_of(row, depth)


def pair_at(field, p, k, depth):
    return jnp.concatenate([field[pl.ds(row_of(p, c, k, depth), depth), :] for c in range(COMPS)], axis=0)


def last_pairs(scalars, p):
    size = scalars[SIZES + 2 * p]
    return lax.div(size - 1, 2), lax.div(size - 2, 2), lax.rem(size, 2) == 0


def send_layers(field, scalars, order, own, to_pair, to_ring, z_pair, z_ring, depth):
    even_section = lax.axis_index("sect") % 2 == 0
    for p in range(2):
        for c in range(COMPS):
            for d in range(HALO):
                start = row_of(p, c, 0, depth)
                low = field[pl.ds(start + d, PAIRS, stride=depth), :]
                high = field[pl.ds(start + depth - HALO + d, PAIRS, stride=depth), :]
                z_pair[p, c, d] = jnp.where(even_section, high, low)
                z_ring[p, c, d] = jnp.where(even_section, low, high)
        own[p * FACES] = pair_at(field, p, 0, depth)
        outer_pair, inner_pair, same = last_pairs(scalars, p)
        outer, inner = pair_at(field, p, outer_pair, depth), pair_at(field, p, inner_pair, depth)
        own[p * FACES + 1] = jnp.where(same, swap_halves(outer), merge(outer, inner))
    select = jnp.concatenate(layer_select(scalars), axis=0)
    groups_rows = []
    for g in range(4):
        for c in range(COMPS):
            starts = [row_of(p, c, 4 * j + g, depth) for p in range(2) for j in range(8)]
            groups_rows.append(jnp.concatenate([field[start : start + depth, :] for start in starts], axis=1))
    rows = jnp.concatenate(groups_rows, axis=0)
    count = rows.shape[0]
    row_high, row_low = split(rows)
    picked = dot(jnp.concatenate([row_high, row_low], axis=0), select)
    picked = picked[:count] + picked[count:]
    per = COMPS * depth
    picked = jnp.concatenate([picked[g * per : (g + 1) * per] for g in range(4)], axis=1)
    pick_high, pick_low = split(picked)
    sorted_layers = dot(jnp.concatenate([pick_high, pick_low], axis=0), order[...])
    sorted_layers = sorted_layers[:per] + sorted_layers[per:]
    for p in range(2):
        for f in range(2):
            at = (p * 2 + f) * LANES
            own[p * FACES + 2 + f] = sorted_layers[:, at : at + LANES]
    for slot in range(FACES):
        to_pair[slot] = own[scalars[SOURCES + slot]]
        to_ring[slot] = own[scalars[SOURCES + FACES + slot]]


def active_lanes(scalars, p):
    lane = lane_iota()
    in_y = (lane % PAD) < scalars[SIZES + 2 * p + 1]
    x_left = scalars[SIZES + 2 * p] - lane // PAD
    return lambda k: in_y & (x_left > 2 * k)


MASS, STIFF, SLOPE = 0, 1, 2
TILES = (
    (((0, MASS), (0, STIFF)), ((0, STIFF), (0, MASS))),
    (((1, MASS), (2, SLOPE)), ((0, SLOPE), (1, MASS))),
    (((1, MASS), (1, STIFF)), ((1, STIFF), (1, MASS))),
    (((0, MASS), None), ((1, SLOPE), None)),
    (((2, MASS), (2, STIFF)), ((2, STIFF), (2, MASS))),
    (((0, SLOPE), (1, SLOPE)), ((2, SLOPE), (2, MASS))),
)
TERMS = {
    ((0, MASS), (0, STIFF)): (MASS, "both"),
    ((0, MASS), (0, MASS)): (STIFF, "mu"),
    ((0, STIFF), (0, MASS)): (MASS, "mu"),
    ((1, MASS), (0, SLOPE)): (SLOPE, "grad"),
    ((2, SLOPE), (0, SLOPE)): (MASS, "grad"),
    ((1, MASS), (1, STIFF)): (MASS, "mu"),
    ((1, MASS), (1, MASS)): (STIFF, "both"),
    ((1, STIFF), (1, MASS)): (MASS, "mu"),
    ((2, SLOPE), (1, MASS)): (SLOPE, "grad"),
    ((0, MASS), (1, SLOPE)): (SLOPE, "grad"),
    ((2, MASS), (2, STIFF)): (MASS, "mu"),
    ((2, MASS), (2, MASS)): (STIFF, "mu"),
    ((2, STIFF), (2, MASS)): (MASS, "both"),
    ((1, SLOPE), (2, MASS)): (SLOPE, "grad"),
    ((0, SLOPE), (2, SLOPE)): (MASS, "grad"),
}
OUT_SCALE = {STIFF: 1.0 / STIFF_DEN, MASS: 1.0 / MASS_DEN, SLOPE: 1.0 / SLOPE_DEN}


def fill_weights(lame_ref, me, weights):
    tables = in_kernel_bands()
    for p in range(2):
        mu = lame_ref[0, me * 2 + p]
        grad = mu + lame_ref[1, me * 2 + p]
        factors = {"mu": mu, "both": mu + grad, "grad": -grad}
        placed = set()
        for t, (sources, targets) in enumerate(TILES):
            for i, source in enumerate(sources):
                for o, target in enumerate(targets):
                    term = TERMS.get((source, target))
                    if term is None or (source, target) in placed:
                        block = jnp.zeros((LANES, LANES), F32)
                    else:
                        placed.add((source, target))
                        block = tables[term[0]] * (factors[term[1]] * OUT_SCALE[target[1]])
                    block_high, block_low = split(block)
                    cols = slice(o * LANES, (o + 1) * LANES)
                    for part, piece in enumerate((block_high, block_high, block_low)):
                        at = part * 2 * LANES + i * LANES
                        weights[p * len(TILES) + t, at : at + LANES, cols] = piece


def start_kernel(
    groups, depth, sizes_any, partners_any, lame_any, disp_any,
    field, own, to_pair, to_ring, z_pair, z_ring, weights, order, scalars, factors,
    sizes_ref, partners_ref, lame_ref, disp, sems,
):
    copies = []
    for c in range(COMPS):
        copies.append(pltpu.make_async_copy(disp_any.at[:, c], disp.at[:, c], sems.at[c]))
    small = [
        pltpu.make_async_copy(sizes_any, sizes_ref, sems.at[COMPS]),
        pltpu.make_async_copy(partners_any, partners_ref, sems.at[COMPS + 1]),
        pltpu.make_async_copy(lame_any, lame_ref, sems.at[COMPS + 2]),
    ]
    for copy in small + copies:
        copy.start()
    order[...] = layer_order()
    for copy in small:
        copy.wait()
    me = lax.axis_index("patch")
    fill_scalars(sizes_ref, partners_ref, lame_ref, scalars, factors, me, groups)
    fill_weights(lame_ref, me, weights)
    keeps = [active_lanes(scalars, p) for p in range(2)]
    for c in range(COMPS):
        copies[c].wait()
        for p in range(2):
            for k in range(PAIRS):
                start = row_of(p, c, k, depth)
                value = disp[p, c, :, k * LANES : (k + 1) * LANES]
                field[start : start + depth, :] = jnp.where(keeps[p](k), value, 0.0)
    send_layers(field, scalars, order, own, to_pair, to_ring, z_pair, z_ring, depth)


def plane_sums(fields, weights, p, complete=None):
    sums = {}
    for t, (sources, targets) in enumerate(TILES):
        if sources[1] is None:
            high, low = fields[sources[0]]
            weight = jnp.concatenate(
                [weights[p * len(TILES) + t, part * 2 * LANES : part * 2 * LANES + LANES, :LANES] for part in range(3)],
                axis=0,
            )
        else:
            high, low = [jnp.concatenate([fields[s][part] for s in sources], axis=1) for part in range(2)]
            weight = weights[p * len(TILES) + t]
        out = dot(jnp.concatenate([high, low, high], axis=1), weight)
        for o, target in enumerate(targets):
            if target is not None:
                piece = out[:, o * LANES : (o + 1) * LANES]
                sums[target] = piece if target not in sums else sums[target] + piece
        if complete is not None and t % 2 == 1:
            complete(t // 2, [sums[(t // 2, kind)] for kind in range(3)])
    return sums


def band_x(stiff, mass, slope, count):
    def at(values, d, extra=0):
        return values[2 + d : 2 + d + count + extra]

    total = STIFF_INT[0] * at(stiff, 0) + MASS_INT[0] * at(mass, 0)
    total = total + STIFF_INT[2] * (at(stiff, 1) + at(stiff, -1))
    total = total + MASS_INT[2] * (at(mass, 1) + at(mass, -1))
    total = total + SLOPE_INT[1] * (at(slope, 1) - at(slope, -1))
    odd = STIFF_INT[1] * (at(stiff, 0, 1) + at(stiff, -1, 1))
    odd = odd + MASS_INT[1] * (at(mass, 0, 1) + at(mass, -1, 1))
    odd = odd + SLOPE_INT[0] * (at(slope, 0, 1) - at(slope, -1, 1))
    odd = odd + ((at(mass, 1, 1) + at(mass, -2, 1)) - (at(stiff, 1, 1) + at(stiff, -2, 1)))
    odd = odd + (at(slope, 1, 1) - at(slope, -2, 1))
    return total + swap_halves(merge(odd[1:], odd[:-1]))


def send_output(result, result_any, sems, part, parts):
    lanes = pl.ds(part * (PAD * PAD // parts), PAD * PAD // parts)
    copy = pltpu.make_async_copy(result.at[:, :, :, lanes], result_any.at[:, :, :, lanes], sems.at[part])
    copy.start()
    return copy


OUT_PARTS = 4
SUMS = (18, KEEP + 4)


def volume_kernel(depth, field, z_table, weights, *rest):
    copy = None
    if len(rest) == 2:
        out, sums_ref = rest
    else:
        finished, out, finished_any, sums_ref, sem = rest
        copy = pltpu.make_async_copy(finished, finished_any, sem)
        copy.start()
    for i in range(18):
        for k in (0, 1, KEEP + 2, KEEP + 3):
            sums_ref[i, k] = jnp.zeros((depth, LANES), F32)

    def along_z(p, k0, count):
        fields = {}
        for c in range(COMPS):
            starts = [row_of(p, c, k0 + j, depth) for j in range(count)]
            rows = [field[start : start + depth, :] for start in starts]
            high, low = split(jnp.concatenate(rows, axis=1))
            banded = dot(z_table[...], jnp.concatenate([high, low, high], axis=0))
            parts = split(banded)
            for kind in range(3):
                fields[(c, kind)] = tuple(
                    jnp.concatenate(
                        [
                            part[kind * depth : (kind + 1) * depth, j * LANES : (j + 1) * LANES]
                            for j in range(count)
                        ],
                        axis=0,
                    )
                    for part in parts
                )
        return fields

    def along_x(p, k0, count, c, z0):
        held = [sums_ref[p * 9 + c * 3 + kind, k0 : k0 + count + 4, z0 : z0 + 8, :] for kind in range(3)]
        total = band_x(held[STIFF], held[MASS], held[SLOPE], count)
        for j in range(count):
            start = row_of(p, c, k0 + j, depth) + z0
            out[start : start + 8, :] = total[j]

    blocks = [(p, k0, min(KBLOCK, KEEP - k0)) for p in range(2) for k0 in range(0, KEEP, KBLOCK)]
    done = [0, 0]
    ahead = along_z(*blocks[0])
    for i, (p, k0, count) in enumerate(blocks):
        fields = ahead
        if i + 1 < len(blocks):
            ahead = along_z(*blocks[i + 1])
        ready = KEEP if k0 + count == KEEP else k0 + count - 2
        first = done[p]
        while done[p] < KEEP and min(done[p] + KROWS, KEEP) <= ready:
            done[p] = min(done[p] + KROWS, KEEP)

        def complete(c, values):
            for kind in range(3):
                sums_ref[p * 9 + c * 3 + kind, k0 + 2 : k0 + 2 + count] = values[kind].reshape(count, depth, LANES)
            for k in range(first, done[p], KROWS):
                for z0 in range(0, depth, 8):
                    along_x(p, k, min(KROWS, KEEP - k), c, z0)

        plane_sums(fields, weights, p, complete)
    if copy is not None:
        copy.wait()


def depth_edges(before, after):
    mass, stiff, slope = [], [], []
    for table, den, out, sign in (
        (MASS_INT[1:], MASS_DEN, mass, 1.0),
        (STIFF_INT[1:], STIFF_DEN, stiff, 1.0),
        (SLOPE_INT, SLOPE_DEN, slope, -1.0),
    ):
        coef = [value / den for value in table]
        for z in range(3):
            total = None
            for d in range(z + 1, 4):
                piece = (sign * coef[d - 1]) * before[3 + z - d]
                total = piece if total is None else total + piece
            out.append(total)
        for z in range(3):
            total = None
            for d in range(3 - z, 4):
                piece = coef[d - 1] * after[z + d - 3]
                total = piece if total is None else total + piece
            out.append(total)
    return [jnp.concatenate(parts, axis=0) for parts in (mass, stiff, slope)]


EDGE_K = PAIRS + 4


def finish_kernel(
    depth, last, scalars, factors, volume, own, from_pair, from_ring, z_pair, z_ring, transfer, weights, order,
    field, *rest,
):
    if last:
        result_any, edge, result, sems = rest
    else:
        *sends, result, edge = rest
    section, sections = lax.axis_index("sect"), lax.axis_size("sect")
    even_section = section % 2 == 0
    terms = []
    for k in range(2 * FACES):
        slot = scalars[SLOTS + k]
        far = jnp.where(slot < FACES, from_pair[lax.rem(slot, FACES)], from_ring[lax.rem(slot, FACES)])
        mat = transfer[k // FACES, k % FACES]
        zero = jnp.zeros((PAD, PAD), F32)
        both = jnp.concatenate(
            [jnp.concatenate([mat, zero], axis=1), jnp.concatenate([zero, mat], axis=1)], axis=0
        )
        far_high, far_low = split(far)
        mat_high, mat_low = split(both)
        moved = lax.dot_general(
            jnp.concatenate([far_high, far_low, far_high], axis=1),
            jnp.concatenate([mat_high, mat_high, mat_low], axis=1),
            (((1,), (1,)), ((), ())),
            preferred_element_type=F32,
        )
        terms.append(factors[k] * (own[k] - moved))
    for p in range(2):
        fields = {}
        for c in range(COMPS):
            before, after = [], []
            for d in range(HALO):
                paired, ringed = z_pair[p, c, d], z_ring[p, c, d]
                before.append(jnp.where(section == 0, 0.0, jnp.where(even_section, ringed, paired)))
                after.append(jnp.where(section == sections - 1, 0.0, jnp.where(even_section, paired, ringed)))
            banded = depth_edges(before, after)
            for kind in range(3):
                fields[(c, kind)] = split(banded[kind])
        sums = plane_sums(fields, weights, p)
        for (c, kind), value in sums.items():
            base = (p * 9 + c * 3 + kind) * EDGE_K * 8
            edge[base : base + 16, :] = jnp.zeros((16, LANES), F32)
            edge[base + (2 + PAIRS) * 8 : base + EDGE_K * 8, :] = jnp.zeros((16, LANES), F32)
            for z in range(2 * HALO):
                slot = z if z < HALO else z + 2
                edge[pl.ds(base + 16 + slot, PAIRS, stride=8), :] = value[z * PAIRS : (z + 1) * PAIRS]
    per = COMPS * depth
    stacked = jnp.concatenate([swap_halves(terms[p * FACES + 2 + f]) for p in range(2) for f in range(2)], axis=1)
    term_high, term_low = split(stacked)
    placed = lax.dot_general(
        jnp.concatenate([term_high, term_low], axis=0),
        order[...],
        (((1,), (1,)), ((), ())),
        preferred_element_type=F32,
    )
    placed = placed[:per] + placed[per:]
    placed = jnp.concatenate([placed[:, g * LANES : (g + 1) * LANES] for g in range(4)], axis=0)
    placed_parts = jnp.concatenate(split(placed), axis=1)
    select = layer_select(scalars)

    def add_pair(p, k, addend):
        for c in range(COMPS):
            field[pl.ds(row_of(p, c, k, depth), depth), :] += addend[c * depth : (c + 1) * depth]

    zero = jnp.zeros((per, LANES), F32)
    for p in range(2):
        add_pair(p, 0, swap_halves(terms[p * FACES]))
        outer_pair, inner_pair, same = last_pairs(scalars, p)
        term = terms[p * FACES + 1]
        add_pair(p, outer_pair, jnp.where(same, term, merge(swap_halves(term), zero)))
        add_pair(p, inner_pair, jnp.where(same, zero, merge(zero, swap_halves(term))))
    keeps = [active_lanes(scalars, p) for p in range(2)]
    slot_rows = lax.broadcasted_iota(jnp.int32, (8, LANES), 0)
    copies = []
    for j in range(8):
        both = jnp.concatenate([select[j], select[8 + j]], axis=0)
        spread = lax.dot_general(
            placed_parts,
            jnp.concatenate([both, both], axis=1),
            (((1,), (1,)), ((), ())),
            preferred_element_type=F32,
        )
        for p in range(2):
            for c in range(COMPS):
                held = []
                for kind in range(3):
                    base = ((p * 9 + c * 3 + kind) * EDGE_K + 4 * j) * 8
                    held.append(edge[base : base + 64, :].reshape(8, 8, LANES))
                edges = band_x(held[STIFF], held[MASS], held[SLOPE], 4)
                for g in range(4):
                    k = 4 * j + g
                    start = row_of(p, c, k, depth)
                    row = (g * COMPS + c) * depth
                    value = field[start : start + depth, :] + spread[row : row + depth, p * LANES : (p + 1) * LANES]
                    value = jnp.concatenate(
                        [
                            value[:8] + jnp.where(slot_rows < HALO, edges[g], 0.0),
                            value[8 : depth - 8],
                            value[depth - 8 :] + jnp.where(slot_rows >= 8 - HALO, edges[g], 0.0),
                        ],
                        axis=0,
                    )
                    value = jnp.where(keeps[p](k), value, 0.0)
                    result[p, c, :, k * LANES : (k + 1) * LANES] = value
                    if not last:
                        field[start : start + depth, :] = value
        if last and (j + 1) % (8 // OUT_PARTS) == 0:
            copies.append(send_output(result, result_any, sems, j // (8 // OUT_PARTS), OUT_PARTS))
    if not last:
        send_layers(field, scalars, order, *sends, depth)
    for copy in copies:
        copy.wait()


def shards(displacement, lame_params, patch_sizes, partners, transfer):
    depth = displacement.shape[2]
    groups = lax.axis_size("patch")
    sections = lax.axis_size("sect")
    rows = 2 * COMPS * PAIRS * depth
    per = COMPS * depth
    smem = pl.BlockSpec(memory_space=pltpu.SMEM)
    vmem = pl.BlockSpec(memory_space=pltpu.VMEM)
    away = pl.BlockSpec(memory_space=pl.ANY)
    z_table = jnp.asarray(depth_table(depth))
    lame = lame_params.T

    def shape(*dims, dtype=F32):
        return pltpu.VMEM(dims, dtype)

    def near(values):
        return pltpu.with_memory_space_constraint(values, pltpu.VMEM)

    def scalar(values):
        return pltpu.with_memory_space_constraint(values, pltpu.SMEM)

    def far(values):
        return pltpu.with_memory_space_constraint(values, pltpu.HBM)

    def params(mib):
        return pltpu.CompilerParams(vmem_limit_bytes=mib * MIB)

    field_shape = shape(rows, LANES)
    layer_shapes = (
        shape(2 * FACES, per, LANES),
        shape(FACES, per, LANES),
        shape(FACES, per, LANES),
        shape(2, COMPS, HALO, PAIRS, LANES),
        shape(2, COMPS, HALO, PAIRS, LANES),
    )

    def both_ways(pairs):
        return pairs + [(j, i) for i, j in pairs]

    def exchange(layers):
        own, to_pair, to_ring, z_pair, z_ring = layers
        z_pair = lax.ppermute(z_pair, "sect", both_ways([(i, i + 1) for i in range(0, sections, 2)]))
        z_ring = lax.ppermute(z_ring, "sect", both_ways([(i, (i + 1) % sections) for i in range(1, sections, 2)]))
        from_pair = lax.ppermute(to_pair, "patch", both_ways([(i, i + 1) for i in range(0, groups, 2)]))
        from_ring = lax.ppermute(to_ring, "patch", both_ways([(i, (i + 1) % groups) for i in range(1, groups, 2)]))
        return own, from_pair, from_ring, z_pair, z_ring

    field, *layers, weights, order, scalars, factors = pl.pallas_call(
        functools.partial(start_kernel, groups, depth),
        out_shape=(field_shape,)
        + layer_shapes
        + (shape(2 * len(TILES), 6 * LANES, 2 * LANES, dtype=BF16), shape(512, 512, dtype=BF16))
        + (pltpu.SMEM((SCALARS,), jnp.int32), pltpu.SMEM((2 * FACES,), F32)),
        in_specs=[away] * 4,
        out_specs=(vmem,) * 8 + (smem,) * 2,
        scratch_shapes=[
            pltpu.SMEM(patch_sizes.shape, jnp.int32),
            pltpu.SMEM(partners.shape, jnp.int32),
            pltpu.SMEM(lame.shape, F32),
            pltpu.VMEM(displacement.shape, F32),
            pltpu.SemaphoreType.DMA((COMPS + 3,)),
        ],
        compiler_params=params(24),
        name="start_layers",
    )(far(patch_sizes), far(partners), far(lame), far(displacement))

    def volume(values, finished=None):
        out_shape = (field_shape,)
        operands = (near(values), z_table, near(weights))
        scratch = [pltpu.VMEM(SUMS + (depth, LANES), F32)]
        if finished is not None:
            out_shape = out_shape + (jax.ShapeDtypeStruct(displacement.shape, F32),)
            operands = operands + (near(finished),)
            scratch = scratch + [pltpu.SemaphoreType.DMA(())]
        return pl.pallas_call(
            functools.partial(volume_kernel, depth),
            out_shape=out_shape,
            in_specs=[vmem] * len(operands),
            out_specs=(vmem, away)[: len(out_shape)],
            scratch_shapes=scratch,
            compiler_params=params(30),
            cost_estimate=pl.CostEstimate(flops=10**10, bytes_accessed=8 * 10**6, transcendentals=0),
            name="volume_terms" if finished is None else "volume_and_output",
        )(*operands)

    def finish(volume_part, exchanged, last):
        scratch = [pltpu.VMEM((18 * EDGE_K * 8, LANES), F32)]
        if last:
            out_shape = (field_shape, jax.ShapeDtypeStruct(displacement.shape, F32))
            out_specs = (vmem, away)
            scratch = scratch + [
                pltpu.VMEM(displacement.shape, F32),
                pltpu.SemaphoreType.DMA((OUT_PARTS,)),
            ]
        else:
            out_shape = (field_shape,) + layer_shapes + (shape(*displacement.shape),)
            out_specs = (vmem,) * 7
        return pl.pallas_call(
            functools.partial(finish_kernel, depth, last),
            out_shape=out_shape,
            in_specs=[smem] * 2 + [vmem] * 9,
            out_specs=out_specs,
            scratch_shapes=scratch,
            input_output_aliases={2: 0},
            compiler_params=params(30),
            name="finish_last" if last else "finish_first",
        )(
            scalar(scalars),
            scalar(factors),
            near(volume_part),
            *[near(part) for part in exchanged],
            transfer,
            near(weights),
            near(order),
        )

    (volume_part,) = volume(field)
    field, *next_layers, finished = finish(volume_part, exchange(layers), False)
    volume_part, first_apply = volume(field, finished)
    _, second_apply = finish(volume_part, exchange(next_layers), True)
    return first_apply, second_apply


def solution(mesh):
    return jax.shard_map(
        shards,
        mesh=mesh,
        in_specs=(
            P("patch", None, "sect", None),
            P(),
            P("patch", None),
            P("patch", None),
            P("patch", None, None, None),
        ),
        out_specs=(P("patch", None, "sect", None), P("patch", None, "sect", None)),
        check_vma=False,
    )
```

```python
import functools

import jax
import jax.numpy as jnp
import ml_dtypes
import numpy as np
from jax import lax
from jax.experimental import pallas as pl
from jax.experimental.pallas import tpu as pltpu
from jax.sharding import PartitionSpec as P

PAD = 64
LANES = 128
HALO = 3
COMPS = 3
MAXN = 61
FACES = 4
MASS_INT = (2416.0, 1191.0, 120.0, 1.0)
STIFF_INT = (80.0, -15.0, -24.0, -1.0)
SLOPE_INT = (245.0, 56.0, 1.0)
MASS_DEN = 5040.0
STIFF_DEN = 120.0
SLOPE_DEN = 720.0
PENALTY = 3.0
PAIRS = PAD // 2
KEEP = (MAXN + 1) // 2
KBLOCK = 16
KROWS = 8
MIB = 1024 * 1024
F32 = jnp.float32
BF16 = jnp.bfloat16


def split_np(table):
    high = table.astype(ml_dtypes.bfloat16)
    low = (table - high.astype(np.float64)).astype(ml_dtypes.bfloat16)
    return high, low


def band_np(size, kind):
    table = np.zeros((size, size))
    for i in range(size):
        for d in range(0, 4):
            for sign in (1, -1):
                j = i + sign * d
                if 0 <= j < size:
                    if kind == "slope":
                        if d:
                            table[i, j] = sign * SLOPE_INT[d - 1] / SLOPE_DEN
                    elif kind == "mass":
                        table[i, j] = MASS_INT[d] / MASS_DEN
                    else:
                        table[i, j] = STIFF_INT[d] / STIFF_DEN
    return table


def depth_table(depth):
    table = np.concatenate([band_np(depth, k) for k in ("mass", "stiff", "slope")], axis=0)
    high, low = split_np(table)
    return np.concatenate([high, high, low], axis=1)


def in_kernel_bands():
    rows = lax.broadcasted_iota(jnp.int32, (LANES, LANES), 0)
    cols = lax.broadcasted_iota(jnp.int32, (LANES, LANES), 1)
    ahead = jnp.where(rows // PAD == cols // PAD, rows - cols, PAD)
    apart = jnp.abs(ahead)
    mass = jnp.zeros((LANES, LANES), F32)
    stiff, slope = mass, mass
    for d in range(4):
        mass = jnp.where(apart == d, MASS_INT[d] / MASS_DEN, mass)
        stiff = jnp.where(apart == d, STIFF_INT[d] / STIFF_DEN, stiff)
        if d:
            slope = jnp.where(ahead == d, SLOPE_INT[d - 1] / SLOPE_DEN, slope)
            slope = jnp.where(ahead == -d, -SLOPE_INT[d - 1] / SLOPE_DEN, slope)
    return mass, stiff, slope


def layer_order():
    rows = lax.broadcasted_iota(jnp.int32, (512, 512), 0)
    cols = lax.broadcasted_iota(jnp.int32, (512, 512), 1)
    x = 8 * ((rows // 8) % 8) + 2 * (rows // 128) + (rows // 4) % 2
    patch_layer = 4 * ((rows // 64) % 2) + rows % 4
    return jnp.where(cols == patch_layer * 64 + x, 1.0, 0.0).astype(BF16)


def split(values):
    high = values.astype(BF16)
    low = (values - high.astype(F32)).astype(BF16)
    return high, low


def lane_iota(shape=(1, LANES)):
    return lax.broadcasted_iota(jnp.int32, shape, len(shape) - 1)


def swap_halves(values):
    return pltpu.roll(values, PAD, axis=values.ndim - 1)


def merge(low_half, high_half):
    return jnp.where(lane_iota() < PAD, low_half, high_half)


def dot(a, b):
    return jnp.dot(a, b, preferred_element_type=F32)


SIZES, SOURCES, SLOTS, SCALARS = 0, 4, 12, 20


def fill_scalars(sizes_ref, partners_ref, lame_ref, scalars, factors, me, groups):
    for p in range(2):
        for axis in range(2):
            scalars[SIZES + 2 * p + axis] = sizes_ref[p, axis]
    before = lax.rem(me + groups - 1, groups)
    pair_side = 1 - me % 2
    codes = [partners_ref[k // FACES, k % FACES] for k in range(2 * FACES)]
    ring = []
    for code in codes:
        side = jnp.where(code // (2 * FACES) == before, 0, 1)
        ring.append(jnp.where(side == pair_side, 0, 1))
    for k in range(2 * FACES):
        sent, read = jnp.int32(0), jnp.int32(0)
        for other in range(2 * FACES):
            if other != k:
                same = ring[other] == ring[k]
                sent = sent + jnp.where(same & (codes[other] < codes[k]), 1, 0)
                if other < k:
                    read = read + jnp.where(same, 1, 0)
        scalars[SOURCES + ring[k] * FACES + sent] = jnp.int32(k)
        scalars[SLOTS + k] = ring[k] * FACES + read
        p = k // FACES
        factors[k] = (PENALTY - 1.5) * (0.5 * (lame_ref[0, me * 2 + p] + lame_ref[0, codes[k] // FACES]))


def layer_select(scalars):
    rows = lax.broadcasted_iota(jnp.int32, (LANES, LANES), 0)
    cols = lax.broadcasted_iota(jnp.int32, (LANES, LANES), 1)
    layer = cols % 4
    size_y = jnp.where(cols < PAD, scalars[SIZES + 1], scalars[SIZES + 3])
    at = jnp.where(layer < 2, layer, size_y + 1 - layer)
    base = jnp.where(rows == ((cols // 4) % 2) * PAD + at, 1.0, 0.0)
    return [jnp.where(cols // 8 == j, base, 0.0).astype(BF16) for j in range(16)]


def row_of(p, c, k, depth):
    row = ((p * COMPS + c) * PAIRS + k) * depth
    return row if isinstance(row, int) else pl.multiple_of(row, depth)


def pair_at(field, p, k, depth):
    return jnp.concatenate([field[pl.ds(row_of(p, c, k, depth), depth), :] for c in range(COMPS)], axis=0)


def last_pairs(scalars, p):
    size = scalars[SIZES + 2 * p]
    return lax.div(size - 1, 2), lax.div(size - 2, 2), lax.rem(size, 2) == 0


def send_layers(field, scalars, order, own, to_pair, to_ring, z_pair, z_ring, depth):
    even_section = lax.axis_index("sect") % 2 == 0
    for p in range(2):
        for c in range(COMPS):
            for d in range(HALO):
                start = row_of(p, c, 0, depth)
                low = field[pl.ds(start + d, PAIRS, stride=depth), :]
                high = field[pl.ds(start + depth - HALO + d, PAIRS, stride=depth), :]
                z_pair[p, c, d] = jnp.where(even_section, high, low)
                z_ring[p, c, d] = jnp.where(even_section, low, high)
        own[p * FACES] = pair_at(field, p, 0, depth)
        outer_pair, inner_pair, same = last_pairs(scalars, p)
        outer, inner = pair_at(field, p, outer_pair, depth), pair_at(field, p, inner_pair, depth)
        own[p * FACES + 1] = jnp.where(same, swap_halves(outer), merge(outer, inner))
    select = jnp.concatenate(layer_select(scalars), axis=0)
    groups_rows = []
    for g in range(4):
        for c in range(COMPS):
            starts = [row_of(p, c, 4 * j + g, depth) for p in range(2) for j in range(8)]
            groups_rows.append(jnp.concatenate([field[start : start + depth, :] for start in starts], axis=1))
    rows = jnp.concatenate(groups_rows, axis=0)
    count = rows.shape[0]
    row_high, row_low = split(rows)
    picked = dot(jnp.concatenate([row_high, row_low], axis=0), select)
    picked = picked[:count] + picked[count:]
    per = COMPS * depth
    picked = jnp.concatenate([picked[g * per : (g + 1) * per] for g in range(4)], axis=1)
    pick_high, pick_low = split(picked)
    sorted_layers = dot(jnp.concatenate([pick_high, pick_low], axis=0), order[...])
    sorted_layers = sorted_layers[:per] + sorted_layers[per:]
    for p in range(2):
        for f in range(2):
            at = (p * 2 + f) * LANES
            own[p * FACES + 2 + f] = sorted_layers[:, at : at + LANES]
    for slot in range(FACES):
        to_pair[slot] = own[scalars[SOURCES + slot]]
        to_ring[slot] = own[scalars[SOURCES + FACES + slot]]


def active_lanes(scalars, p):
    lane = lane_iota()
    in_y = (lane % PAD) < scalars[SIZES + 2 * p + 1]
    x_left = scalars[SIZES + 2 * p] - lane // PAD
    return lambda k: in_y & (x_left > 2 * k)


MASS, STIFF, SLOPE = 0, 1, 2
TILES = (
    (((0, MASS), (0, STIFF)), ((0, STIFF), (0, MASS))),
    (((1, MASS), (2, SLOPE)), ((0, SLOPE), (1, MASS))),
    (((1, MASS), (1, STIFF)), ((1, STIFF), (1, MASS))),
    (((0, MASS), None), ((1, SLOPE), None)),
    (((2, MASS), (2, STIFF)), ((2, STIFF), (2, MASS))),
    (((0, SLOPE), (1, SLOPE)), ((2, SLOPE), (2, MASS))),
)
TERMS = {
    ((0, MASS), (0, STIFF)): (MASS, "both"),
    ((0, MASS), (0, MASS)): (STIFF, "mu"),
    ((0, STIFF), (0, MASS)): (MASS, "mu"),
    ((1, MASS), (0, SLOPE)): (SLOPE, "grad"),
    ((2, SLOPE), (0, SLOPE)): (MASS, "grad"),
    ((1, MASS), (1, STIFF)): (MASS, "mu"),
    ((1, MASS), (1, MASS)): (STIFF, "both"),
    ((1, STIFF), (1, MASS)): (MASS, "mu"),
    ((2, SLOPE), (1, MASS)): (SLOPE, "grad"),
    ((0, MASS), (1, SLOPE)): (SLOPE, "grad"),
    ((2, MASS), (2, STIFF)): (MASS, "mu"),
    ((2, MASS), (2, MASS)): (STIFF, "mu"),
    ((2, STIFF), (2, MASS)): (MASS, "both"),
    ((1, SLOPE), (2, MASS)): (SLOPE, "grad"),
    ((0, SLOPE), (2, SLOPE)): (MASS, "grad"),
}
OUT_SCALE = {STIFF: 1.0 / STIFF_DEN, MASS: 1.0 / MASS_DEN, SLOPE: 1.0 / SLOPE_DEN}


def fill_weights(lame_ref, me, weights):
    tables = in_kernel_bands()
    for p in range(2):
        mu = lame_ref[0, me * 2 + p]
        grad = mu + lame_ref[1, me * 2 + p]
        factors = {"mu": mu, "both": mu + grad, "grad": -grad}
        placed = set()
        for t, (sources, targets) in enumerate(TILES):
            for i, source in enumerate(sources):
                for o, target in enumerate(targets):
                    term = TERMS.get((source, target))
                    if term is None or (source, target) in placed:
                        block = jnp.zeros((LANES, LANES), F32)
                    else:
                        placed.add((source, target))
                        block = tables[term[0]] * (factors[term[1]] * OUT_SCALE[target[1]])
                    block_high, block_low = split(block)
                    cols = slice(o * LANES, (o + 1) * LANES)
                    for part, piece in enumerate((block_high, block_high, block_low)):
                        at = part * 2 * LANES + i * LANES
                        weights[p * len(TILES) + t, at : at + LANES, cols] = piece


def start_kernel(
    groups, depth, sizes_any, partners_any, lame_any, disp_any,
    field, own, to_pair, to_ring, z_pair, z_ring, weights, order, scalars, factors,
    sizes_ref, partners_ref, lame_ref, disp, sems,
):
    copies = []
    for c in range(COMPS):
        copies.append(pltpu.make_async_copy(disp_any.at[:, c], disp.at[:, c], sems.at[c]))
    small = [
        pltpu.make_async_copy(sizes_any, sizes_ref, sems.at[COMPS]),
        pltpu.make_async_copy(partners_any, partners_ref, sems.at[COMPS + 1]),
        pltpu.make_async_copy(lame_any, lame_ref, sems.at[COMPS + 2]),
    ]
    for copy in small + copies:
        copy.start()
    order[...] = layer_order()
    for copy in small:
        copy.wait()
    me = lax.axis_index("patch")
    fill_scalars(sizes_ref, partners_ref, lame_ref, scalars, factors, me, groups)
    fill_weights(lame_ref, me, weights)
    keeps = [active_lanes(scalars, p) for p in range(2)]
    for c in range(COMPS):
        copies[c].wait()
        for p in range(2):
            for k in range(PAIRS):
                start = row_of(p, c, k, depth)
                value = disp[p, c, :, k * LANES : (k + 1) * LANES]
                field[start : start + depth, :] = jnp.where(keeps[p](k), value, 0.0)
    send_layers(field, scalars, order, own, to_pair, to_ring, z_pair, z_ring, depth)


def plane_sums(fields, weights, p, complete=None):
    sums = {}
    for t, (sources, targets) in enumerate(TILES):
        if sources[1] is None:
            high, low = fields[sources[0]]
            weight = jnp.concatenate(
                [weights[p * len(TILES) + t, part * 2 * LANES : part * 2 * LANES + LANES, :LANES] for part in range(3)],
                axis=0,
            )
        else:
            high, low = [jnp.concatenate([fields[s][part] for s in sources], axis=1) for part in range(2)]
            weight = weights[p * len(TILES) + t]
        out = dot(jnp.concatenate([high, low, high], axis=1), weight)
        for o, target in enumerate(targets):
            if target is not None:
                piece = out[:, o * LANES : (o + 1) * LANES]
                sums[target] = piece if target not in sums else sums[target] + piece
        if complete is not None and t % 2 == 1:
            complete(t // 2, [sums[(t // 2, kind)] for kind in range(3)])
    return sums


def band_x(stiff, mass, slope, count):
    def at(values, d, extra=0):
        return values[2 + d : 2 + d + count + extra]

    total = STIFF_INT[0] * at(stiff, 0) + MASS_INT[0] * at(mass, 0)
    total = total + STIFF_INT[2] * (at(stiff, 1) + at(stiff, -1))
    total = total + MASS_INT[2] * (at(mass, 1) + at(mass, -1))
    total = total + SLOPE_INT[1] * (at(slope, 1) - at(slope, -1))
    odd = STIFF_INT[1] * (at(stiff, 0, 1) + at(stiff, -1, 1))
    odd = odd + MASS_INT[1] * (at(mass, 0, 1) + at(mass, -1, 1))
    odd = odd + SLOPE_INT[0] * (at(slope, 0, 1) - at(slope, -1, 1))
    odd = odd + ((at(mass, 1, 1) + at(mass, -2, 1)) - (at(stiff, 1, 1) + at(stiff, -2, 1)))
    odd = odd + (at(slope, 1, 1) - at(slope, -2, 1))
    return total + swap_halves(merge(odd[1:], odd[:-1]))


def send_output(result, result_any, sems, part, parts):
    lanes = pl.ds(part * (PAD * PAD // parts), PAD * PAD // parts)
    copy = pltpu.make_async_copy(result.at[:, :, :, lanes], result_any.at[:, :, :, lanes], sems.at[part])
    copy.start()
    return copy


OUT_PARTS = 4
SUMS = (18, KEEP + 4)


def volume_kernel(depth, field, z_table, weights, *rest):
    copy = None
    if len(rest) == 2:
        out, sums_ref = rest
    else:
        finished, out, finished_any, sums_ref, sem = rest
        copy = pltpu.make_async_copy(finished, finished_any, sem)
        copy.start()
    for i in range(18):
        for k in (0, 1, KEEP + 2, KEEP + 3):
            sums_ref[i, k] = jnp.zeros((depth, LANES), F32)

    def along_z(p, k0, count):
        fields = {}
        for c in range(COMPS):
            starts = [row_of(p, c, k0 + j, depth) for j in range(count)]
            rows = [field[start : start + depth, :] for start in starts]
            high, low = split(jnp.concatenate(rows, axis=1))
            banded = dot(z_table[...], jnp.concatenate([high, low, high], axis=0))
            parts = split(banded)
            for kind in range(3):
                fields[(c, kind)] = tuple(
                    jnp.concatenate(
                        [
                            part[kind * depth : (kind + 1) * depth, j * LANES : (j + 1) * LANES]
                            for j in range(count)
                        ],
                        axis=0,
                    )
                    for part in parts
                )
        return fields

    def along_x(p, k0, count, c, z0):
        held = [sums_ref[p * 9 + c * 3 + kind, k0 : k0 + count + 4, z0 : z0 + 8, :] for kind in range(3)]
        total = band_x(held[STIFF], held[MASS], held[SLOPE], count)
        for j in range(count):
            start = row_of(p, c, k0 + j, depth) + z0
            out[start : start + 8, :] = total[j]

    blocks = [(p, k0, min(KBLOCK, KEEP - k0)) for p in range(2) for k0 in range(0, KEEP, KBLOCK)]
    done = [0, 0]
    ahead = along_z(*blocks[0])
    for i, (p, k0, count) in enumerate(blocks):
        fields = ahead
        if i + 1 < len(blocks):
            ahead = along_z(*blocks[i + 1])
        ready = KEEP if k0 + count == KEEP else k0 + count - 2
        first = done[p]
        while done[p] < KEEP and min(done[p] + KROWS, KEEP) <= ready:
            done[p] = min(done[p] + KROWS, KEEP)

        def complete(c, values):
            for kind in range(3):
                sums_ref[p * 9 + c * 3 + kind, k0 + 2 : k0 + 2 + count] = values[kind].reshape(count, depth, LANES)
            for k in range(first, done[p], KROWS):
                for z0 in range(0, depth, 8):
                    along_x(p, k, min(KROWS, KEEP - k), c, z0)

        plane_sums(fields, weights, p, complete)
    if copy is not None:
        copy.wait()


def depth_edges(before, after):
    mass, stiff, slope = [], [], []
    for table, den, out, sign in (
        (MASS_INT[1:], MASS_DEN, mass, 1.0),
        (STIFF_INT[1:], STIFF_DEN, stiff, 1.0),
        (SLOPE_INT, SLOPE_DEN, slope, -1.0),
    ):
        coef = [value / den for value in table]
        for z in range(3):
            total = None
            for d in range(z + 1, 4):
                piece = (sign * coef[d - 1]) * before[3 + z - d]
                total = piece if total is None else total + piece
            out.append(total)
        for z in range(3):
            total = None
            for d in range(3 - z, 4):
                piece = coef[d - 1] * after[z + d - 3]
                total = piece if total is None else total + piece
            out.append(total)
    return [jnp.concatenate(parts, axis=0) for parts in (mass, stiff, slope)]


EDGE_K = PAIRS + 4


def finish_kernel(
    depth, last, scalars, factors, volume, own, from_pair, from_ring, z_pair, z_ring, transfer, weights, order,
    field, *rest,
):
    if last:
        result_any, edge, result, sems = rest
    else:
        *sends, result, edge = rest
    section, sections = lax.axis_index("sect"), lax.axis_size("sect")
    even_section = section % 2 == 0
    terms = []
    for k in range(2 * FACES):
        slot = scalars[SLOTS + k]
        far = jnp.where(slot < FACES, from_pair[lax.rem(slot, FACES)], from_ring[lax.rem(slot, FACES)])
        mat = transfer[k // FACES, k % FACES]
        zero = jnp.zeros((PAD, PAD), F32)
        both = jnp.concatenate(
            [jnp.concatenate([mat, zero], axis=1), jnp.concatenate([zero, mat], axis=1)], axis=0
        )
        far_high, far_low = split(far)
        mat_high, mat_low = split(both)
        moved = lax.dot_general(
            jnp.concatenate([far_high, far_low, far_high], axis=1),
            jnp.concatenate([mat_high, mat_high, mat_low], axis=1),
            (((1,), (1,)), ((), ())),
            preferred_element_type=F32,
        )
        terms.append(factors[k] * (own[k] - moved))
    for p in range(2):
        fields = {}
        for c in range(COMPS):
            before, after = [], []
            for d in range(HALO):
                paired, ringed = z_pair[p, c, d], z_ring[p, c, d]
                before.append(jnp.where(section == 0, 0.0, jnp.where(even_section, ringed, paired)))
                after.append(jnp.where(section == sections - 1, 0.0, jnp.where(even_section, paired, ringed)))
            banded = depth_edges(before, after)
            for kind in range(3):
                fields[(c, kind)] = split(banded[kind])
        sums = plane_sums(fields, weights, p)
        for (c, kind), value in sums.items():
            base = (p * 9 + c * 3 + kind) * EDGE_K * 8
            edge[base : base + 16, :] = jnp.zeros((16, LANES), F32)
            edge[base + (2 + PAIRS) * 8 : base + EDGE_K * 8, :] = jnp.zeros((16, LANES), F32)
            for z in range(2 * HALO):
                slot = z if z < HALO else z + 2
                edge[pl.ds(base + 16 + slot, PAIRS, stride=8), :] = value[z * PAIRS : (z + 1) * PAIRS]
    per = COMPS * depth
    stacked = jnp.concatenate([swap_halves(terms[p * FACES + 2 + f]) for p in range(2) for f in range(2)], axis=1)
    term_high, term_low = split(stacked)
    placed = lax.dot_general(
        jnp.concatenate([term_high, term_low], axis=0),
        order[...],
        (((1,), (1,)), ((), ())),
        preferred_element_type=F32,
    )
    placed = placed[:per] + placed[per:]
    placed = jnp.concatenate([placed[:, g * LANES : (g + 1) * LANES] for g in range(4)], axis=0)
    placed_parts = jnp.concatenate(split(placed), axis=1)
    select = layer_select(scalars)

    def add_pair(p, k, addend):
        for c in range(COMPS):
            field[pl.ds(row_of(p, c, k, depth), depth), :] += addend[c * depth : (c + 1) * depth]

    zero = jnp.zeros((per, LANES), F32)
    for p in range(2):
        add_pair(p, 0, swap_halves(terms[p * FACES]))
        outer_pair, inner_pair, same = last_pairs(scalars, p)
        term = terms[p * FACES + 1]
        add_pair(p, outer_pair, jnp.where(same, term, merge(swap_halves(term), zero)))
        add_pair(p, inner_pair, jnp.where(same, zero, merge(zero, swap_halves(term))))
    keeps = [active_lanes(scalars, p) for p in range(2)]
    slot_rows = lax.broadcasted_iota(jnp.int32, (8, LANES), 0)
    copies = []
    for j in range(8):
        both = jnp.concatenate([select[j], select[8 + j]], axis=0)
        spread = lax.dot_general(
            placed_parts,
            jnp.concatenate([both, both], axis=1),
            (((1,), (1,)), ((), ())),
            preferred_element_type=F32,
        )
        for p in range(2):
            for c in range(COMPS):
                held = []
                for kind in range(3):
                    base = ((p * 9 + c * 3 + kind) * EDGE_K + 4 * j) * 8
                    held.append(edge[base : base + 64, :].reshape(8, 8, LANES))
                edges = band_x(held[STIFF], held[MASS], held[SLOPE], 4)
                for g in range(4):
                    k = 4 * j + g
                    start = row_of(p, c, k, depth)
                    row = (g * COMPS + c) * depth
                    value = field[start : start + depth, :] + spread[row : row + depth, p * LANES : (p + 1) * LANES]
                    value = jnp.concatenate(
                        [
                            value[:8] + jnp.where(slot_rows < HALO, edges[g], 0.0),
                            value[8 : depth - 8],
                            value[depth - 8 :] + jnp.where(slot_rows >= 8 - HALO, edges[g], 0.0),
                        ],
                        axis=0,
                    )
                    value = jnp.where(keeps[p](k), value, 0.0)
                    result[p, c, :, k * LANES : (k + 1) * LANES] = value
                    if not last:
                        field[start : start + depth, :] = value
        if last and (j + 1) % (8 // OUT_PARTS) == 0:
            copies.append(send_output(result, result_any, sems, j // (8 // OUT_PARTS), OUT_PARTS))
    if not last:
        send_layers(field, scalars, order, *sends, depth)
    for copy in copies:
        copy.wait()


def shards(displacement, lame_params, patch_sizes, partners, transfer):
    depth = displacement.shape[2]
    groups = lax.axis_size("patch")
    sections = lax.axis_size("sect")
    rows = 2 * COMPS * PAIRS * depth
    per = COMPS * depth
    smem = pl.BlockSpec(memory_space=pltpu.SMEM)
    vmem = pl.BlockSpec(memory_space=pltpu.VMEM)
    away = pl.BlockSpec(memory_space=pl.ANY)
    z_table = jnp.asarray(depth_table(depth))
    lame = lame_params.T

    def shape(*dims, dtype=F32):
        return pltpu.VMEM(dims, dtype)

    def near(values):
        return pltpu.with_memory_space_constraint(values, pltpu.VMEM)

    def scalar(values):
        return pltpu.with_memory_space_constraint(values, pltpu.SMEM)

    def far(values):
        return pltpu.with_memory_space_constraint(values, pltpu.HBM)

    def params(mib):
        return pltpu.CompilerParams(vmem_limit_bytes=mib * MIB)

    field_shape = shape(rows + depth, LANES)
    layer_shapes = (
        shape(2 * FACES, per, LANES),
        shape(FACES, per, LANES),
        shape(FACES, per, LANES),
        shape(2, COMPS, HALO, PAIRS, LANES),
        shape(2, COMPS, HALO, PAIRS, LANES),
    )

    def both_ways(pairs):
        return pairs + [(j, i) for i, j in pairs]

    def exchange(layers):
        own, to_pair, to_ring, z_pair, z_ring = layers
        z_pair = lax.ppermute(z_pair, "sect", both_ways([(i, i + 1) for i in range(0, sections, 2)]))
        z_ring = lax.ppermute(z_ring, "sect", both_ways([(i, (i + 1) % sections) for i in range(1, sections, 2)]))
        from_pair = lax.ppermute(to_pair, "patch", both_ways([(i, i + 1) for i in range(0, groups, 2)]))
        from_ring = lax.ppermute(to_ring, "patch", both_ways([(i, (i + 1) % groups) for i in range(1, groups, 2)]))
        return own, from_pair, from_ring, z_pair, z_ring

    field, *layers, weights, order, scalars, factors = pl.pallas_call(
        functools.partial(start_kernel, groups, depth),
        out_shape=(field_shape,)
        + layer_shapes
        + (shape(2 * len(TILES), 6 * LANES, 2 * LANES, dtype=BF16), shape(512, 512, dtype=BF16))
        + (pltpu.SMEM((SCALARS,), jnp.int32), pltpu.SMEM((2 * FACES,), F32)),
        in_specs=[away] * 4,
        out_specs=(vmem,) * 8 + (smem,) * 2,
        scratch_shapes=[
            pltpu.SMEM(patch_sizes.shape, jnp.int32),
            pltpu.SMEM(partners.shape, jnp.int32),
            pltpu.SMEM(lame.shape, F32),
            pltpu.VMEM(displacement.shape, F32),
            pltpu.SemaphoreType.DMA((COMPS + 3,)),
        ],
        compiler_params=params(24),
        name="start_layers",
    )(far(patch_sizes), far(partners), far(lame), far(displacement))

    def volume(values, finished=None):
        out_shape = (field_shape,)
        operands = (near(values), z_table, near(weights))
        scratch = [pltpu.VMEM(SUMS + (depth, LANES), F32)]
        if finished is not None:
            out_shape = out_shape + (jax.ShapeDtypeStruct(displacement.shape, F32),)
            operands = operands + (near(finished),)
            scratch = scratch + [pltpu.SemaphoreType.DMA(())]
        return pl.pallas_call(
            functools.partial(volume_kernel, depth),
            out_shape=out_shape,
            in_specs=[vmem] * len(operands),
            out_specs=(vmem, away)[: len(out_shape)],
            scratch_shapes=scratch,
            compiler_params=params(30),
            cost_estimate=pl.CostEstimate(flops=10**10, bytes_accessed=8 * 10**6, transcendentals=0),
            name="volume_terms" if finished is None else "volume_and_output",
        )(*operands)

    def finish(volume_part, exchanged, last):
        scratch = [pltpu.VMEM((18 * EDGE_K * 8, LANES), F32)]
        if last:
            out_shape = (field_shape, jax.ShapeDtypeStruct(displacement.shape, F32))
            out_specs = (vmem, away)
            scratch = scratch + [
                pltpu.VMEM(displacement.shape, F32),
                pltpu.SemaphoreType.DMA((OUT_PARTS,)),
            ]
        else:
            out_shape = (field_shape,) + layer_shapes + (shape(*displacement.shape),)
            out_specs = (vmem,) * 7
        return pl.pallas_call(
            functools.partial(finish_kernel, depth, last),
            out_shape=out_shape,
            in_specs=[smem] * 2 + [vmem] * 9,
            out_specs=out_specs,
            scratch_shapes=scratch,
            input_output_aliases={2: 0},
            compiler_params=params(30),
            name="finish_last" if last else "finish_first",
        )(
            scalar(scalars),
            scalar(factors),
            near(volume_part),
            *[near(part) for part in exchanged],
            transfer,
            near(weights),
            near(order),
        )

    (volume_part,) = volume(field)
    field, *next_layers, finished = finish(volume_part, exchange(layers), False)
    volume_part, first_apply = volume(field, finished)
    _, second_apply = finish(volume_part, exchange(next_layers), True)
    return first_apply, second_apply


def solution(mesh):
    return jax.shard_map(
        shards,
        mesh=mesh,
        in_specs=(
            P("patch", None, "sect", None),
            P(),
            P("patch", None),
            P("patch", None),
            P("patch", None, None, None),
        ),
        out_specs=(P("patch", None, "sect", None), P("patch", None, "sect", None)),
        check_vma=False,
    )
```
